32 devices in a mesh: groups: 2 (over y), cols: 4 (over z), rows: 2 (over x), layers: 2 (over core).
Axes of the slice: x: 2, y: 2, z: 4, core: 2. Of those that a mesh axis runs over, the one named last changes fastest.
Arguments:
- state_field: float32 [32, 128, 256], P(('groups', 'layers'), 'cols', 'rows'), parts along dimension 0, may hold values from -6 to 6
- conductivity: float32 [32, 128, 256], P(('groups', 'layers'), 'cols', 'rows'), parts along dimension 0, may hold values from 0.3 to 3
- storage: float32 [32, 128, 256], P(('groups', 'layers'), 'cols', 'rows'), parts along dimension 0, may hold values from 0.05 to 0.5
- gauge_owner: int32 [131072], P(('groups', 'cols', 'rows', 'layers')), parts along dimension 0, may hold values from 0 to 7, as said below
- gauge_cell: int32 [131072], P(('groups', 'cols', 'rows', 'layers')), parts along dimension 0, may hold values from 0 to 32767
- gauge_value: float32 [131072], P(('groups', 'cols', 'rows', 'layers')), parts along dimension 0, may hold values from -6 to 6
- gauge_weight: float32 [131072], P(('groups', 'cols', 'rows', 'layers')), parts along dimension 0, may hold values from 0.5 to 2
- pilot_index: int32 [128, 256], P('cols', 'rows'), may hold values from 0 to 4095, as said below
Outputs:
- adjoint: float32 [32, 128, 256], P(('groups', 'layers'), 'cols', 'rows'), parts along dimension 0
- pilot_gradient: float32 [8192], P(('groups', 'cols', 'rows')), parts along dimension 0
The draws below stay inside these ranges and needn't reach their ends.
There are 2 independent parts, one for each index of `groups`. The reference program is written for one: setup_inputs(seed, part) draws one part's arguments, and reference() takes and returns one part's arrays. A program takes and returns all parts, laid end to end along the dimension named above; an argument that names none is the same for every part. Nothing has to cross between parts.
Inputs may be any that keep to these rules, and one draw needn't show every extreme that they name: `gauge_owner`: within the 4096 rows of one device no owner is named by more than 2048 rows; in every draw, for each layer half, one owner is named by exactly 2048 rows of every device of that half. `pilot_index`: aligned blocks of 4 x 2 cell columns share one pilot point and every pilot point covers exactly one such block; pilot p belongs to owner p // 512; the block of 32 x 128 columns of one device holds exactly 512 // (4 * 2) pilot points of each owner.
All inputs are finite; a program needn't handle non-finite values.
Results may differ from the reference program's by a relative error of at most 0.0001.
Values sent between devices are 32-bit elements; how exact they have to be, the bound alone decides.
No kernel may reach another device: no remote copies, remote signals or barrier semaphores. Data moves between devices by JAX's collectives and lax.ppermute only.
A program may use at most 64 MiB of HBM per device.

```python
import math
import jax
import jax.numpy as jnp
from jax import lax

CX = 32
CY = 128
CZ = 8
OBS_DEV = 4096
ITERS = 8
NX = 128
NY = 256
NZ = 16
OBS = 65536
PILOTS = 4096
N_COLS = 4
N_ROWS = 2
N_LAYERS = 2


def draw_gauge_owner(key, part):
    key = jax.random.fold_in(key, 11)
    peer_count = N_COLS * N_ROWS
    block_count = peer_count * N_LAYERS
    capacity = 4 * OBS_DEV // peer_count
    hot_key, block_key = jax.random.split(key)
    hottest = jax.random.randint(hot_key, (N_LAYERS,), 0, peer_count)

    def one_block(block_seed, favourite):
        limit_key, score_key, order_key = jax.random.split(block_seed, 3)
        eligible = jax.random.randint(limit_key, (peer_count,), capacity // 2, capacity + 1)
        column = jnp.arange(capacity, dtype=jnp.int32)[None, :]
        owner_grid = jnp.arange(peer_count, dtype=jnp.int32)[:, None]
        allowed = (column < eligible[:, None]) & (owner_grid != favourite)
        scores = jax.random.randint(score_key, (peer_count, capacity), 0, 16384) * (peer_count * capacity) + owner_grid * capacity + column
        scores = jnp.where(allowed, scores, -1).reshape(-1)
        picked = lax.top_k(scores, OBS_DEV - capacity)[1]
        owners = jnp.concatenate([jnp.full((capacity,), favourite, jnp.int32), (picked // capacity).astype(jnp.int32)])
        return owners[jax.random.permutation(order_key, OBS_DEV)]
    seeds = jax.random.split(block_key, block_count)
    favourites = hottest[jnp.arange(block_count) % N_LAYERS]
    return jax.vmap(one_block)(seeds, favourites).reshape(-1).astype(jnp.int32)


def shuffled(seed_key):
    return jax.random.permutation(seed_key, CX * CY // 8)


def draw_pilot_index(key, part):
    key = jax.random.fold_in(key, 23)
    peer_count = N_COLS * N_ROWS
    blocks = CX * CY // 8
    per_owner = blocks // peer_count
    order_key, slot_key = jax.random.split(key)
    orders = jax.vmap(shuffled)(jax.random.split(order_key, peer_count))
    owners = orders // per_owner
    base_slot = jnp.arange(peer_count, dtype=jnp.int32)[:, None] * per_owner + orders % per_owner
    mixing = jax.vmap(shuffled)(jax.random.split(slot_key, peer_count))
    labels = owners * blocks + mixing[owners, base_slot]
    grid = labels.reshape(N_COLS, N_ROWS, CX // 4, CY // 2).transpose(0, 2, 1, 3).reshape(N_COLS * CX // 4, N_ROWS * CY // 2)
    return jnp.repeat(jnp.repeat(grid, 4, axis=0), 2, axis=1).astype(jnp.int32)


def with_ends(drawn, key, least, high):
    longest = drawn.shape.index(max(drawn.shape))
    spots = []
    for shift in (0, 1):
        where = [jax.random.randint(jax.random.fold_in(key, axis), (), 0, length) for axis, length in enumerate(drawn.shape)]
        where[longest] = (where[longest] + shift) % drawn.shape[longest]
        spots.append(tuple(where))
    return drawn.at[spots[0]].set(least).at[spots[1]].set(high)


def shard_levels(own_key, shape, pieces, low, high):
    loudness = 1.0
    for position, shards_of in pieces:
        heights = jax.random.uniform(jax.random.fold_in(jax.random.fold_in(own_key, 6), position), (shards_of,), jnp.float32, low / len(pieces), high / len(pieces))
        loudness = loudness * jnp.repeat(jnp.exp(heights), shape[position] // shards_of).reshape((-1,) + (1,) * (len(shape) - 1 - position))
    return loudness


def noise(key, dims, deviation, most, pieces=(), kind=jnp.bfloat16):
    drawn = deviation * jax.random.normal(key, dims, jnp.float32)
    if pieces:
        drawn = drawn * shard_levels(key, dims, pieces, -0.22, 0.18)
    return jnp.clip(drawn, -most, most).astype(kind)


def setup_inputs(seed: int = 0, part: int = 0) -> dict:
    key_list = jax.random.split(jax.random.key(seed), 9)
    part_keys = jax.random.split(jax.random.fold_in(key_list[8], part), 9)
    return {
        "state_field": noise(part_keys[0], (NZ, NX, NY), 1.0, 6.0, ((0, 2), (1, 4), (2, 2)), jnp.float32),
        "conductivity": jnp.clip(jnp.exp(math.log(3.0) - 2.3025851 * jax.random.uniform(part_keys[1], (NZ, NX, NY), jnp.float32) ** shard_levels(part_keys[1], (NZ, NX, NY), ((0, 2), (1, 4), (2, 2)), -0.2, 0.2)), 0.3, 3.0),
        "storage": jnp.clip(jnp.exp(math.log(0.5) - 2.3025851 * jax.random.uniform(part_keys[2], (NZ, NX, NY), jnp.float32) ** shard_levels(part_keys[2], (NZ, NX, NY), ((0, 2), (1, 4), (2, 2)), -0.2, 0.2)), 0.05, 0.5),
        "gauge_owner": draw_gauge_owner(jax.random.fold_in(jax.random.fold_in(key_list[8], part), 71), part),
        "gauge_cell": with_ends(jax.random.randint(part_keys[4], (OBS,), 0, CX * CY * CZ), jax.random.fold_in(part_keys[4], 1), 0, (CX * CY * CZ) - 1).astype(jnp.int32),
        "gauge_value": noise(part_keys[5], (OBS,), 1.0, 6.0, ((0, 16),), jnp.float32),
        "gauge_weight": jnp.clip(jnp.exp(math.log(2.0) - 1.3862944 * jax.random.uniform(part_keys[6], (OBS,), jnp.float32) ** shard_levels(part_keys[6], (OBS,), ((0, 16),), -0.2, 0.2)), 0.5, 2.0),
        "pilot_index": draw_pilot_index(jax.random.fold_in(key_list[8], 71), part),
    }


def neighbours(padded):
    return [padded[2:, 1:-1, 1:-1], padded[:-2, 1:-1, 1:-1], padded[1:-1, 2:, 1:-1],
            padded[1:-1, :-2, 1:-1], padded[1:-1, 1:-1, 2:], padded[1:-1, 1:-1, :-2]]


def reference(state_field, conductivity, storage, gauge_owner, gauge_cell, gauge_value, gauge_weight, pilot_index):
    face_weights = [0.5 * (conductivity + other) for other in neighbours(jnp.pad(conductivity, 1))]
    diagonal = storage
    for weight_one in face_weights:
        diagonal = diagonal + weight_one

    def operate(field):
        result = diagonal * field
        for weight_one, other in zip(face_weights, neighbours(jnp.pad(field, 1))):
            result = result - weight_one * other
        return result

    row_number = jnp.arange(gauge_owner.shape[0], dtype=jnp.int32)
    layer_half = (row_number // OBS_DEV) % N_LAYERS
    layer_pos = layer_half * CZ + gauge_cell // (CX * CY)
    within = gauge_cell % (CX * CY)
    across = (gauge_owner // N_ROWS) * CX + within // CY
    lateral = (gauge_owner % N_ROWS) * CY + within % CY
    predicted = state_field[layer_pos, across, lateral]
    source_term = jnp.zeros_like(state_field).at[layer_pos, across, lateral].add(gauge_weight * (predicted - gauge_value))

    adjoint = jnp.zeros_like(source_term)
    residual = source_term
    direction = source_term
    norm_now = jnp.sum(residual * residual)
    for iteration in range(ITERS):
        image_field = operate(direction)
        step_length = norm_now / jnp.sum(direction * image_field)
        adjoint = adjoint + step_length * direction
        residual = residual - step_length * image_field
        norm_next = jnp.sum(residual * residual)
        direction = residual + (norm_next / norm_now) * direction
        norm_now = norm_next

    total = jnp.zeros_like(adjoint)
    for adjoint_side, state_side in zip(neighbours(jnp.pad(adjoint, 1)), neighbours(jnp.pad(state_field, 1))):
        total = total + (adjoint - adjoint_side) * (state_field - state_side)
    cell_gradient = -0.5 * conductivity * total
    column_sums = jnp.sum(cell_gradient, axis=0)
    pilot_gradient = jnp.zeros((PILOTS,), jnp.float32).at[pilot_index.reshape(-1)].add(column_sums.reshape(-1))
    return adjoint, pilot_gradient
```

```python
import functools

import jax
import jax.numpy as jnp
from jax import lax
from jax.experimental import pallas as pl
from jax.experimental.pallas import tpu as pltpu
from jax.sharding import PartitionSpec as P

ITERS = 8
HALO = 8
LANES = 128
LANE_BITS = 7
GRID_AXES = ("cols", "rows", "layers")
PEER_AXES = ("cols", "rows")
NT = (((1,), (1,)), ((), ()))
EXACT = lax.Precision.HIGHEST
VMEM_BYTES = 50 * 1024 * 1024


def kernel_call(body, out_shape, scratch=()):
    return functools.partial(
        pl.pallas_call,
        body,
        out_shape=out_shape,
        scratch_shapes=list(scratch),
        compiler_params=pltpu.CompilerParams(vmem_limit_bytes=VMEM_BYTES),
    )


VMEM = pl.BlockSpec(memory_space=pltpu.VMEM)
SMEM = pl.BlockSpec(memory_space=pltpu.SMEM)


def pieces_of(x):
    first = x.astype(jnp.bfloat16).astype(jnp.float32)
    rest = x - first
    second = rest.astype(jnp.bfloat16).astype(jnp.float32)
    return first, second, rest - second


def row_iota(rows, lanes=LANES):
    return lax.broadcasted_iota(jnp.int32, (rows, lanes), 0)


def lane_iota(rows, lanes=LANES):
    return lax.broadcasted_iota(jnp.int32, (rows, lanes), 1)


def picked(mask, row):
    return jnp.where(mask, row, jnp.zeros_like(row)).astype(jnp.bfloat16)


def mm(a, b, dims=(((1,), (0,)), ((), ())), precision=None):
    return lax.dot_general(a, b, dims, precision=precision, preferred_element_type=jnp.float32)


def route_body(peers, capacity, owner_ref, cell_ref, value_ref, weight_ref, out_ref):
    rows = owner_ref.shape[0]
    owner = owner_ref[...]
    ra, ca = row_iota(LANES, 2 * LANES), lane_iota(LANES, 2 * LANES)
    earlier_lane = jnp.where((ra < ca) | (ca >= LANES), 1.0, 0.0).astype(jnp.bfloat16)
    earlier_row = jnp.where(row_iota(rows, rows) > lane_iota(rows, rows), 1.0, 0.0).astype(
        jnp.bfloat16
    )

    def rank_of(peer, rank):
        hit = owner == peer
        counts = mm(jnp.where(hit, 1.0, 0.0).astype(jnp.bfloat16), earlier_lane)
        before = mm(earlier_row, counts[:, LANES:].astype(jnp.bfloat16))
        return rank + jnp.where(hit, counts[:, :LANES] + before, 0.0)

    rank = jnp.zeros((rows, LANES), jnp.float32)
    if peers <= 16:
        for peer in range(peers):
            rank = rank_of(peer, rank)
    else:
        rank = lax.fori_loop(0, peers, rank_of, rank)
    position = owner * capacity + rank.astype(jnp.int32)
    slot_row = lax.shift_right_logical(position, LANE_BITS)
    slot_lane = position & (LANES - 1)
    cell = cell_ref[...]
    columns = [
        lax.shift_right_logical(cell, LANE_BITS).astype(jnp.float32),
        (cell & (LANES - 1)).astype(jnp.float32),
        *pieces_of(value_ref[...]),
        *pieces_of(weight_ref[...]),
    ]
    slot_rows = peers * capacity // LANES
    rows_at, lanes_at = row_iota(slot_rows), row_iota(LANES)
    total = jnp.zeros((slot_rows, len(columns) * LANES), jnp.float32)
    step = 8
    for start in range(0, rows, step):
        left, right = [], [[] for _ in columns]
        for r in range(start, start + step):
            left.append(
                jnp.where(rows_at == slot_row[r : r + 1], 1.0, 0.0).astype(jnp.bfloat16)
            )
            lane_hit = lanes_at == slot_lane[r : r + 1]
            for q, column in enumerate(columns):
                right[q].append(picked(lane_hit, column[r : r + 1]))
        right = jnp.concatenate([jnp.concatenate(q, axis=1) for q in right], axis=0)
        total = total + mm(jnp.concatenate(left, axis=1), right, NT)
    part = [total[:, q * LANES : (q + 1) * LANES] for q in range(len(columns))]
    fields = [
        part[0] * LANES + part[1],
        part[2] + part[3] + part[4],
        part[5] + part[6] + part[7],
    ]
    each = capacity // LANES
    for peer in range(peers):
        for q, field in enumerate(fields):
            out_ref[peer, q * each : (q + 1) * each, :] = field[peer * each : (peer + 1) * each]


def source_body(got_ref, state_ref, out_ref, acc_ref):
    peers, each = got_ref.shape[0], got_ref.shape[1] // 3
    cells = state_ref.shape[0]
    state_t = jnp.concatenate(
        [p.astype(jnp.bfloat16) for p in pieces_of(jnp.transpose(state_ref[...]))], axis=0
    )
    acc_ref[...] = jnp.zeros_like(acc_ref)
    rows_at, lanes_at = row_iota(cells), row_iota(LANES)

    def one_peer(peer, carry):
        cell = got_ref[peer, 0:each, :].astype(jnp.int32)
        value = got_ref[peer, each : 2 * each, :]
        weight = got_ref[peer, 2 * each : 3 * each, :]
        high = lax.shift_right_logical(cell, LANE_BITS)
        low = cell & (LANES - 1)
        row_hits = jnp.concatenate(
            [
                jnp.where(rows_at == high[r : r + 1], 1.0, 0.0).astype(jnp.bfloat16)
                for r in range(each)
            ],
            axis=1,
        )
        heads = mm(state_t, row_hits)
        right = [[], [], []]
        for r in range(each):
            lane_hit = lanes_at == low[r : r + 1]
            here = heads[:, r * LANES : (r + 1) * LANES]
            head = here[:LANES] + here[LANES : 2 * LANES] + here[2 * LANES :]
            head = jnp.sum(jnp.where(lane_hit, head, 0.0), axis=0, keepdims=True)
            misfit = weight[r : r + 1] * (head - value[r : r + 1])
            for q, piece in enumerate(pieces_of(misfit)):
                right[q].append(picked(lane_hit, piece))
        right = jnp.concatenate([jnp.concatenate(q, axis=1) for q in right], axis=0)
        acc_ref[...] += mm(row_hits, right, NT)
        return carry

    lax.fori_loop(0, peers, one_peer, 0)
    out_ref[...] = (
        acc_ref[:, :LANES] + acc_ref[:, LANES : 2 * LANES] + acc_ref[:, 2 * LANES :]
    )


def all_sum(x):
    while x.ndim > 2:
        x = jnp.sum(x, axis=0)
    return jnp.sum(jnp.sum(x, axis=0, keepdims=True), axis=1, keepdims=True)


def safe_ratio(a, b):
    return jnp.where(b > 0.0, a / jnp.where(b > 0.0, b, 1.0), 0.0)


def local_body(source_ref, conductivity_ref, storage_ref, out_ref):
    c = conductivity_ref[...]

    def up(x, axis):
        if axis == 0:
            return jnp.concatenate([x[1:], x[:1]], axis=0)
        return pltpu.roll(x, x.shape[axis] - 1, axis)

    def down(x, axis):
        if axis == 0:
            return jnp.concatenate([x[-1:], x[:-1]], axis=0)
        return pltpu.roll(x, 1, axis)

    faces = [0.5 * (c + up(c, axis)) for axis in range(3)]
    diagonal = storage_ref[...]
    for axis, face in enumerate(faces):
        diagonal = diagonal + face + down(face, axis)

    now, last = source_ref[...], None
    norm_last = None
    lanes = lane_iota(1)
    out = jnp.zeros((1, LANES), jnp.float32)
    for k in range(ITERS):
        image = diagonal * now
        for axis, face in enumerate(faces):
            image = image - face * up(now, axis) - down(face * now, axis)
        norm = all_sum(now * now)
        alpha = safe_ratio(all_sum(now * image), norm)
        beta = norm if k == 0 else safe_ratio(norm, norm_last)
        out = jnp.where(lanes == k, alpha, out)
        out = jnp.where(lanes == ITERS + k, beta, out)
        if k < ITERS - 1:
            following = image - alpha * now
            if k:
                following = following - beta * last
            now, last, norm_last = following, now, norm
    out_ref[...] = jnp.broadcast_to(out, out_ref.shape)


def common_coefficients(got):
    lanes = lane_iota(got.shape[0])
    used = lanes < ITERS
    alpha = jnp.where(used, got, 0.0)
    beta = jnp.where(used, pltpu.roll(got, LANES - ITERS, 1), 0.0)
    weight = jnp.where(used, beta, 1.0)
    for shift in (1, 2, 4):
        weight = weight * jnp.where(lanes >= shift, pltpu.roll(weight, shift, 1), 1.0)
    weight = jnp.where(used, weight, 0.0)
    beta_next = jnp.where(lanes < ITERS - 1, pltpu.roll(beta, LANES - 1, 1), 0.0)
    now = jnp.where(lanes == 0, 1.0, 0.0)
    last = jnp.zeros_like(now)
    alphas, gammas = [], []
    norm_last = None
    for k in range(ITERS):
        image = (
            jnp.where((lanes >= 1) & used, pltpu.roll(now, 1, 1), 0.0)
            + alpha * now
            + beta_next * pltpu.roll(now, LANES - 1, 1)
        )
        norm = all_sum(weight * now * now)
        a = safe_ratio(all_sum(weight * now * image), norm)
        alphas.append(a)
        g = None
        if k:
            g = safe_ratio(norm, norm_last)
            gammas.append(g)
        following = image - a * now
        if k:
            following = following - g * last
        now, last, norm_last = following, now, norm
    return alphas, gammas


def unpack(layer, field, own, other, low, high, sides, padded, strip):
    nz, nx = own.shape[-3], own.shape[-2]
    place = jnp.where(
        lane_iota(2 * HALO)
        == jnp.where(
            row_iota(2 * HALO) < HALO, row_iota(2 * HALO), row_iota(2 * HALO) + LANES - 2 * HALO
        ),
        1.0,
        0.0,
    )
    spread = mm(jnp.transpose(sides[field]), place, precision=EXACT)
    strip[...] = spread.reshape(strip.shape)
    for i in range(nz):
        j = jnp.where(layer == 0, i, nz - 1 - i)
        for half, block in ((0, own), (1, other)):
            to = half * nz + i
            padded[to, HALO : HALO + nx, :LANES] = block[field, j]
            padded[to, :HALO, :LANES] = low[field, half * nz + j]
            padded[to, HALO + nx :, :LANES] = high[field, half * nz + j]
            padded[to, :, LANES:] = strip[half * nz + j]


def basis_body(
    peers,
    layer_ref,
    f_own, f_other, f_low, f_high, f_sides,
    b_own, b_other, b_low, b_high, b_sides,
    got_ref, pilot_ref,
    own_ref, send_ref,
    c_pad, s_pad, h_pad, diag, wx, wy, wz, basis, strip, grads,
):
    layer = layer_ref[0]
    nz, nx = f_own.shape[1], f_own.shape[2]
    planes, width = c_pad.shape[0], c_pad.shape[1]
    for field, target in ((0, c_pad), (1, s_pad), (2, h_pad)):
        unpack(layer, field, f_own, f_other, f_low, f_high, f_sides, target, strip)
    unpack(layer, 0, b_own, b_other, b_low, b_high, b_sides, basis.at[0], strip)

    def right(x):
        return pltpu.roll(x, x.shape[1] - 1, 1)

    def left(x):
        return pltpu.roll(x, 1, 1)

    def fore(x):
        return pltpu.roll(x, x.shape[0] - 1, 0)

    def back(x):
        return pltpu.roll(x, 1, 0)

    def joined(a, b):
        return jnp.where((a > 0.0) & (b > 0.0), 0.5 * (a + b), 0.0)

    for z in range(planes):
        c = c_pad[z]
        cf, cr = fore(c), right(c)
        total = cf + back(c) + cr + left(c)
        wx[z] = joined(c, cf)
        wy[z] = joined(c, cr)
        if z + 1 < planes:
            wz[z] = joined(c, c_pad[z + 1])
            total = total + c_pad[z + 1]
        if z:
            total = total + c_pad[z - 1]
        diag[z] = s_pad[z] + 3.0 * c + 0.5 * total

    alphas, gammas = common_coefficients(got_ref[...])
    betas = [None] + [jnp.sqrt(g) for g in gammas] + [jnp.sqrt(gammas[-1])]
    scales = [None] + [safe_ratio(jnp.ones_like(b), b) for b in betas[1:]]
    for k in range(ITERS):
        for z in range(nz + ITERS - 1 - k):
            v = basis[k, z]
            wxz, wyz = wx[z], wy[z]
            image = (diag[z] - alphas[k]) * v - wz[z] * basis[k, z + 1]
            if z:
                image = image - wz[z - 1] * basis[k, z - 1]
            image = image - wxz * fore(v) - back(wxz * v) - wyz * right(v) - left(wyz * v)
            if k:
                image = image - betas[k] * basis[k - 1, z]
            basis[k + 1, z] = image * scales[k + 1]

    inner = slice(HALO, HALO + nx)
    for z in range(nz):
        c = -0.5 * c_pad[z, inner, :LANES]
        h = h_pad[z, inner, :LANES]
        wide = h_pad[z, inner, :]
        grads[0, z] = c * (h - h_pad[z, HALO + 1 : HALO + nx + 1, :LANES])
        grads[1, z] = c * (h - h_pad[z, HALO - 1 : HALO + nx - 1, :LANES])
        grads[2, z] = c * (h - right(wide)[:, :LANES])
        grads[3, z] = c * (h - left(wide)[:, :LANES])
        grads[4, z] = c * (h - h_pad[z + 1, inner, :LANES])
        grads[5, z] = c * (h - h_pad[z - 1, inner, :LANES]) if z else c * h

    dots = {}
    for i in range(ITERS + 1):
        for j in range(i + 1):
            acc = basis[i, 0, inner, :LANES] * basis[j, 0, inner, :LANES]
            for z in range(1, nz):
                acc = acc + basis[i, z, inner, :LANES] * basis[j, z, inner, :LANES]
            dots[i, j] = dots[j, i] = all_sum(acc)
    lanes = lane_iota(1)
    entries = jnp.zeros((1, LANES), jnp.float32)
    place = 0
    for i in range(ITERS):
        for j in range(i + 1):
            entry = betas[j + 1] * dots[i, j + 1] + alphas[j] * dots[i, j]
            if j:
                entry = entry + betas[j] * dots[i, j - 1]
            entries = jnp.where(lanes == place, entry, entries)
            place += 1
    for i in range(ITERS):
        entries = jnp.where(lanes == place, dots[i, 0], entries)
        place += 1

    sums = []
    for k in range(ITERS):
        acc = jnp.zeros((nx, LANES), jnp.float32)
        for z in range(nz):
            u = basis[k, z, inner, :LANES]
            wide = basis[k, z, inner, :]
            acc = acc + (u - basis[k, z, HALO + 1 : HALO + nx + 1, :LANES]) * grads[0, z]
            acc = acc + (u - basis[k, z, HALO - 1 : HALO + nx - 1, :LANES]) * grads[1, z]
            acc = acc + (u - right(wide)[:, :LANES]) * grads[2, z]
            acc = acc + (u - left(wide)[:, :LANES]) * grads[3, z]
            acc = acc + (u - basis[k, z + 1, inner, :LANES]) * grads[4, z]
            if z:
                acc = acc + (u - basis[k, z - 1, inner, :LANES]) * grads[5, z]
            else:
                acc = acc + u * grads[5, z]
            own_ref[k, jnp.where(layer == 0, z, nz - 1 - z)] = u
        sums.append(acc)
    blocks_x = nx // 4
    four = jnp.where(lax.shift_right_logical(lane_iota(blocks_x, nx), 2) == row_iota(blocks_x, nx), 1.0, 0.0)
    sums = mm(four, jnp.concatenate(sums, axis=1), precision=EXACT)
    pilots = nx * LANES // 8
    each = pilots // LANES
    pilot_rows = peers * each
    pilot = [pilot_ref[4 * r : 4 * r + 1, :] for r in range(blocks_x)]
    lane_hits = jnp.concatenate(
        [jnp.where(row_iota(LANES) == (p & (LANES - 1)), 1.0, 0.0).astype(jnp.bfloat16) for p in pilot],
        axis=1,
    )
    rows_at = row_iota(pilot_rows)
    row_hit = [rows_at == lax.shift_right_logical(p, LANE_BITS) for p in pilot]
    copies = send_ref.shape[0] // peers
    for k in range(ITERS):
        part = pieces_of(sums[:, k * LANES : (k + 1) * LANES])
        values = jnp.concatenate(
            [
                jnp.concatenate(
                    [picked(row_hit[r], p[r : r + 1]) for r in range(blocks_x)], axis=1
                )
                for p in part
            ],
            axis=0,
        )
        dense = mm(values, lane_hits, NT)
        dense = dense[:pilot_rows] + dense[pilot_rows : 2 * pilot_rows] + dense[2 * pilot_rows :]
        for peer in range(peers):
            for copy in range(copies):
                send_ref[peer * copies + copy, k * each : (k + 1) * each, :] = dense[
                    peer * each : (peer + 1) * each
                ]
    tail = send_ref.shape[1] - ITERS * each
    send_ref[:, ITERS * each :, :] = jnp.broadcast_to(
        entries[None], (send_ref.shape[0], tail, LANES)
    )


def solve_body(got_ref, own_ref, adjoint_ref, pilot_ref):
    total = got_ref[0]
    for i in range(1, got_ref.shape[0]):
        total = total + got_ref[i]
    each = pilot_ref.shape[0]
    entries = total[ITERS * each : ITERS * each + 1, :]
    scalar = [entries[0, i] for i in range(ITERS * (ITERS + 1) // 2 + ITERS)]
    matrix, place = {}, 0
    for i in range(ITERS):
        for j in range(i + 1):
            matrix[i, j] = scalar[place]
            place += 1
    rhs = scalar[place:]
    lower, scaled, inverse = {}, {}, []
    for i in range(ITERS):
        for j in range(i + 1):
            s = matrix[i, j]
            for k in range(j):
                s = s - scaled[i, k] * lower[j, k]
            scaled[i, j] = s
            if j < i:
                lower[i, j] = s * inverse[j]
        inverse.append(jnp.where(scaled[i, i] > 0.0, 1.0 / scaled[i, i], 0.0))
    y = []
    for i in range(ITERS):
        s = rhs[i]
        for k in range(i):
            s = s - lower[i, k] * y[k]
        y.append(s)
    x = [None] * ITERS
    for i in reversed(range(ITERS)):
        s = y[i] * inverse[i]
        for k in range(i + 1, ITERS):
            s = s - lower[k, i] * x[k]
        x[i] = s
    pilot = x[0] * total[:each]
    for k in range(1, ITERS):
        pilot = pilot + x[k] * total[k * each : (k + 1) * each]
    pilot_ref[...] = pilot
    for z in range(own_ref.shape[1]):
        acc = x[0] * own_ref[0, z]
        for k in range(1, ITERS):
            acc = acc + x[k] * own_ref[k, z]
        adjoint_ref[z] = acc


def surroundings(block):
    layer_count, row_count, col_count = (lax.axis_size(a) for a in ("layers", "rows", "cols"))
    other = lax.ppermute(block, "layers", [(0, 1), (1, 0)])
    forward = [(i, i + 1) for i in range(col_count - 1)]
    backward = [(b, a) for a, b in forward]
    low_edge = jnp.concatenate([block[:, :, :HALO], other[:, :, :HALO]], axis=1)
    high_edge = jnp.concatenate([block[:, :, -HALO:], other[:, :, -HALO:]], axis=1)
    low = lax.ppermute(high_edge, "cols", forward)
    high = lax.ppermute(low_edge, "cols", backward)
    both = jnp.concatenate([low, jnp.concatenate([block, other], axis=1), high], axis=2)

    def packed(edge):
        return jnp.transpose(edge, (0, 3, 1, 2)).reshape(edge.shape[0], HALO, -1)

    if row_count == 2:
        row = lax.axis_index("rows")
        edge = packed(jnp.where(row == 0, both[..., -HALO:], both[..., :HALO]))
        got = lax.ppermute(edge, "rows", [(0, 1), (1, 0)])
        sides = jnp.concatenate(
            [jnp.where(row == 0, got, 0.0), jnp.where(row == 0, 0.0, got)], axis=1
        )
    else:
        forward = [(i, i + 1) for i in range(row_count - 1)]
        backward = [(b, a) for a, b in forward]
        from_left = lax.ppermute(packed(both[..., -HALO:]), "rows", forward)
        from_right = lax.ppermute(packed(both[..., :HALO]), "rows", backward)
        sides = jnp.concatenate([from_right, from_left], axis=1)
    return block, other, low, high, sides


def on_device(
    state_field,
    conductivity,
    storage,
    gauge_owner,
    gauge_cell,
    gauge_value,
    gauge_weight,
    pilot_index,
):
    nz, nx, ny = state_field.shape
    peers = lax.axis_size("cols") * lax.axis_size("rows")
    devices = peers * lax.axis_size("layers")
    gauges = gauge_owner.shape[0]
    capacity = 4 * gauges // peers
    f32 = jnp.float32

    def shape(*dims):
        return jax.ShapeDtypeStruct(dims, f32)

    fixed = surroundings(jnp.stack([conductivity, storage, state_field]))

    def flat(x):
        return x.reshape(gauges // LANES, LANES)

    payload = kernel_call(
        functools.partial(route_body, peers, capacity),
        shape(peers, 3 * capacity // LANES, LANES),
    )(in_specs=[VMEM] * 4, out_specs=VMEM)(
        flat(gauge_owner), flat(gauge_cell), flat(gauge_value), flat(gauge_weight)
    )
    got = lax.all_to_all(payload, PEER_AXES, 0, 0, tiled=True)
    source = kernel_call(
        source_body, shape(nz * nx, LANES), [pltpu.VMEM((nz * nx, 3 * LANES), f32)]
    )(in_specs=[VMEM] * 2, out_specs=VMEM)(got, state_field.reshape(nz * nx, ny))
    source = source.reshape(nz, nx, ny)
    around = surroundings(source[None])

    local = kernel_call(local_body, shape(devices, LANES))(in_specs=[VMEM] * 3, out_specs=VMEM)(
        source, conductivity, storage
    )
    measures = lax.all_to_all(local, GRID_AXES, 0, 0, tiled=True)

    each = nx * ny // 8 // LANES
    send_rows = (ITERS * each + 8) // 8 * 8
    planes, width = 2 * nz, nx + 2 * HALO
    padded = pltpu.VMEM((planes, width, 2 * LANES), f32)
    layer = lax.axis_index("layers").astype(jnp.int32).reshape(1)
    own, send = kernel_call(
        functools.partial(basis_body, peers),
        (shape(ITERS, nz, nx, LANES), shape(devices, send_rows, LANES)),
        [padded] * 7
        + [
            pltpu.VMEM((ITERS + 1, planes, width, 2 * LANES), f32),
            pltpu.VMEM((planes, width, LANES), f32),
            pltpu.VMEM((6, nz, nx, LANES), f32),
        ],
    )(in_specs=[SMEM] + [VMEM] * 12, out_specs=(VMEM, VMEM))(
        layer, *fixed, *around, measures, pilot_index
    )
    parts = lax.all_to_all(send, GRID_AXES, 0, 0, tiled=True)
    adjoint, pilot = kernel_call(solve_body, (shape(nz, nx, ny), shape(each, LANES)))(
        in_specs=[VMEM] * 2, out_specs=(VMEM, VMEM)
    )(parts, own)
    return adjoint, pilot.reshape(-1)


def solution(mesh):
    return jax.shard_map(
        on_device,
        mesh=mesh,
        in_specs=(
            P(("groups", "layers"), "cols", "rows"),
            P(("groups", "layers"), "cols", "rows"),
            P(("groups", "layers"), "cols", "rows"),
            P(("groups", "cols", "rows", "layers")),
            P(("groups", "cols", "rows", "layers")),
            P(("groups", "cols", "rows", "layers")),
            P(("groups", "cols", "rows", "layers")),
            P("cols", "rows"),
        ),
        out_specs=(P(("groups", "layers"), "cols", "rows"), P(("groups", "cols", "rows"))),
        check_vma=False,
    )
```

```python
import functools

import jax
import jax.numpy as jnp
from jax import lax
from jax.experimental import pallas as pl
from jax.experimental.pallas import tpu as pltpu
from jax.sharding import PartitionSpec as P

ITERS = 8
HALO = 8
FACTS = 64
SLOTS = 96
LANES = 128
LANE_BITS = 7
GRID_AXES = ("cols", "rows", "layers")
PEER_AXES = ("cols", "rows")
NT = (((1,), (1,)), ((), ()))
EXACT = lax.Precision.HIGHEST
VMEM_BYTES = 50 * 1024 * 1024


def kernel_call(body, out_shape, scratch=(), weight=1):
    return functools.partial(
        pl.pallas_call,
        body,
        out_shape=out_shape,
        scratch_shapes=list(scratch),
        compiler_params=pltpu.CompilerParams(vmem_limit_bytes=VMEM_BYTES),
        cost_estimate=pl.CostEstimate(
            flops=0, bytes_accessed=weight * 3_000_000, transcendentals=0
        ),
    )


VMEM = pl.BlockSpec(memory_space=pltpu.VMEM)
SMEM = pl.BlockSpec(memory_space=pltpu.SMEM)
ANY = pl.BlockSpec(memory_space=pl.ANY)


def pieces_of(x):
    first = x.astype(jnp.bfloat16).astype(jnp.float32)
    rest = x - first
    second = rest.astype(jnp.bfloat16).astype(jnp.float32)
    return first, second, rest - second


def row_iota(rows, lanes=LANES):
    return lax.broadcasted_iota(jnp.int32, (rows, lanes), 0)


def lane_iota(rows, lanes=LANES):
    return lax.broadcasted_iota(jnp.int32, (rows, lanes), 1)


def picked(mask, row):
    return jnp.where(mask, row, jnp.zeros_like(row)).astype(jnp.bfloat16)


def mm(a, b, dims=(((1,), (0,)), ((), ())), precision=None):
    return lax.dot_general(a, b, dims, precision=precision, preferred_element_type=jnp.float32)


def ranks(owner, peers):
    rows = owner.shape[0]
    ra, ca = row_iota(LANES, 2 * LANES), lane_iota(LANES, 2 * LANES)
    earlier_lane = jnp.where((ra < ca) | (ca >= LANES), 1.0, 0.0).astype(jnp.bfloat16)
    earlier_row = jnp.where(row_iota(rows, rows) > lane_iota(rows, rows), 1.0, 0.0).astype(
        jnp.bfloat16
    )

    def one(peer, rank):
        hit = owner == peer
        counts = mm(jnp.where(hit, 1.0, 0.0).astype(jnp.bfloat16), earlier_lane)
        before = mm(earlier_row, counts[:, LANES:].astype(jnp.bfloat16))
        return rank + jnp.where(hit, counts[:, :LANES] + before, 0.0)

    rank = jnp.zeros((rows, LANES), jnp.float32)
    if peers <= 16:
        for peer in range(peers):
            rank = one(peer, rank)
    else:
        rank = lax.fori_loop(0, peers, one, rank)
    return rank.astype(jnp.int32)


def route_body(
    peers, capacity, owner_hbm, cell_hbm, value_hbm, weight_hbm, out_ref,
    owner_ref, cell_ref, value_ref, weight_ref, sems,
):
    copies = [
        pltpu.make_async_copy(source, target, sems.at[i])
        for i, (source, target) in enumerate(
            (
                (owner_hbm, owner_ref),
                (cell_hbm, cell_ref),
                (value_hbm, value_ref),
                (weight_hbm, weight_ref),
            )
        )
    ]
    for copy in copies:
        copy.start()
    for copy in copies:
        copy.wait()
    rows = owner_ref.shape[0]
    owner = owner_ref[...]
    position = owner * capacity + ranks(owner, peers)
    slot_row = lax.shift_right_logical(position, LANE_BITS)
    slot_lane = position & (LANES - 1)
    cell = cell_ref[...]
    columns = [
        lax.shift_right_logical(cell, LANE_BITS).astype(jnp.float32),
        (cell & (LANES - 1)).astype(jnp.float32),
        *pieces_of(value_ref[...]),
        *pieces_of(weight_ref[...]),
    ]
    slot_rows = peers * capacity // LANES
    rows_at, lanes_at = row_iota(slot_rows), row_iota(LANES)
    total = jnp.zeros((slot_rows, len(columns) * LANES), jnp.float32)
    step = 8
    for start in range(0, rows, step):
        left, right = [], [[] for _ in columns]
        for r in range(start, start + step):
            left.append(
                jnp.where(rows_at == slot_row[r : r + 1], 1.0, 0.0).astype(jnp.bfloat16)
            )
            lane_hit = lanes_at == slot_lane[r : r + 1]
            for q, column in enumerate(columns):
                right[q].append(picked(lane_hit, column[r : r + 1]))
        right = jnp.concatenate([jnp.concatenate(q, axis=1) for q in right], axis=0)
        total = total + mm(jnp.concatenate(left, axis=1), right, NT)
    part = [total[:, q * LANES : (q + 1) * LANES] for q in range(len(columns))]
    fields = [
        part[0] * LANES + part[1],
        part[2] + part[3] + part[4],
        part[5] + part[6] + part[7],
    ]
    each = capacity // LANES

    for peer in range(peers):
        for q, field in enumerate(fields):
            out_ref[peer, q * each : (q + 1) * each, :] = field[peer * each : (peer + 1) * each]


def pilot_body(pilot_ref, spot_ref, slots_ref):
    peers = slots_ref.shape[0]
    blocks_x = pilot_ref.shape[0] // 4
    pilots = pilot_ref.shape[0] * pilot_ref.shape[1] // 8
    pilot = jnp.concatenate([pilot_ref[4 * r : 4 * r + 1, :] for r in range(blocks_x)], axis=0)
    owner = lax.div(pilot, jnp.int32(pilots))
    slot = pilot - owner * pilots
    first = (lane_iota(blocks_x) & 1) == 0
    owner = jnp.where(first, owner, -1)
    rank = ranks(owner, peers)
    spot_ref[...] = jnp.where(first, owner * LANES + rank, -1)
    left, high, low = [], [], []
    peer_at, lanes_at = row_iota(peers), row_iota(LANES)
    for r in range(blocks_x):
        left.append(jnp.where(peer_at == owner[r : r + 1], 1.0, 0.0).astype(jnp.bfloat16))
        hit = lanes_at == rank[r : r + 1]
        number = slot[r : r + 1]
        high.append(picked(hit, lax.shift_right_logical(number, LANE_BITS).astype(jnp.float32)))
        low.append(picked(hit, (number & (LANES - 1)).astype(jnp.float32)))
    left = jnp.concatenate(left, axis=1)
    slots_ref[...] = mm(left, jnp.concatenate(high, axis=1), NT) * LANES + mm(
        left, jnp.concatenate(low, axis=1), NT
    )


def source_body(
    each, got_ref, conductivity_ref, storage_ref, state_ref, out_ref, up_ref, down_ref, acc_ref
):
    peers = got_ref.shape[0]
    nz, nx = conductivity_ref.shape[0], conductivity_ref.shape[1]
    cells = nz * nx
    state_t = jnp.concatenate(
        [p.astype(jnp.bfloat16) for p in pieces_of(jnp.transpose(state_ref[...].reshape(cells, LANES)))], axis=0
    )
    acc_ref[...] = jnp.zeros_like(acc_ref)
    rows_at, lanes_at = row_iota(cells), row_iota(LANES)

    def one_peer(peer, carry):
        cell = got_ref[peer, 0:each, :].astype(jnp.int32)
        value = got_ref[peer, each : 2 * each, :]
        weight = got_ref[peer, 2 * each : 3 * each, :]
        high = lax.shift_right_logical(cell, LANE_BITS)
        low = cell & (LANES - 1)
        row_hits = jnp.concatenate(
            [
                jnp.where(rows_at == high[r : r + 1], 1.0, 0.0).astype(jnp.bfloat16)
                for r in range(each)
            ],
            axis=1,
        )
        heads = mm(state_t, row_hits)
        right = [[], [], []]
        for r in range(each):
            lane_hit = lanes_at == low[r : r + 1]
            here = heads[:, r * LANES : (r + 1) * LANES]
            head = here[:LANES] + here[LANES : 2 * LANES] + here[2 * LANES :]
            head = jnp.sum(jnp.where(lane_hit, head, 0.0), axis=0, keepdims=True)
            misfit = weight[r : r + 1] * (head - value[r : r + 1])
            for q, piece in enumerate(pieces_of(misfit)):
                right[q].append(picked(lane_hit, piece))
        right = jnp.concatenate([jnp.concatenate(q, axis=1) for q in right], axis=0)
        acc_ref[...] += mm(row_hits, right, NT)
        return carry

    lax.fori_loop(0, peers, one_peer, 0)
    total = acc_ref[:, :LANES] + acc_ref[:, LANES : 2 * LANES] + acc_ref[:, 2 * LANES :]
    out_ref[...] = total.reshape(nz, nx, LANES)
    for f, field in enumerate((conductivity_ref, storage_ref, state_ref, out_ref)):
        up_ref[f] = field[:, nx - HALO :, :]
        down_ref[f] = field[:, :HALO, :]


def all_sum(x):
    while x.ndim > 2:
        x = jnp.sum(x, axis=0)
    return jnp.sum(jnp.sum(x, axis=0, keepdims=True), axis=1, keepdims=True)


def safe_ratio(a, b):
    return jnp.where(b > 0.0, a / jnp.where(b > 0.0, b, 1.0), 0.0)


def pack_body(low_side, where_ref, *refs):
    *fields, low_ref, high_ref, out_ref = refs
    nz, nx = fields[0].shape[0], fields[0].shape[1]
    lanes = lane_iota(2 * (nx + 2 * HALO))
    tall = jnp.zeros(lanes.shape, jnp.float32)
    for pair in range(2):
        for z in range(nz):
            at = (pair * nz + z) * HALO
            x = jnp.concatenate(
                [
                    part
                    for f in (2 * pair, 2 * pair + 1)
                    for part in (low_ref[f, z], fields[f][z], high_ref[f, z])
                ],
                axis=0,
            )
            if low_side is None:
                shift = (at + jnp.where(where_ref[1] == 0, HALO, 0)) & (LANES - 1)
            else:
                shift = at if low_side else (at + HALO) & (LANES - 1)
            x = pltpu.roll(x, shift, 1)
            tall = jnp.where((lanes >= at) & (lanes < at + HALO), x, tall)
    rest = LANES - tall.shape[0]
    tall = jnp.concatenate([tall, jnp.zeros((rest, LANES), jnp.float32)], axis=0)
    out_ref[...] = jnp.transpose(tall).reshape(out_ref.shape)


def unpack(layer, f, own, other, edges, beside, padded):
    nz, nx = own.shape[0], own.shape[1]
    tall = nx + 2 * HALO
    at = lane_iota(tall)
    rows = slice((f % 2) * tall, (f % 2 + 1) * tall)
    for half, block in ((0, own), (1, other)):
        low, high = edges[2 * half], edges[2 * half + 1]
        for i in range(nz):
            j = jnp.where(layer == 0, i, nz - 1 - i)
            to = half * nz + i
            padded[to, HALO : HALO + nx, :LANES] = block[j]
            padded[to, :HALO, :LANES] = low[f, j]
            padded[to, HALO + nx :, :LANES] = high[f, j]
            strip = jnp.zeros((tall, LANES), jnp.float32)
            for tiles, first in beside[half]:
                shift = (2 * LANES + first - (f // 2 * nz + j) * HALO) & (LANES - 1)
                strip = jnp.where(
                    (at >= first) & (at < first + HALO), pltpu.roll(tiles[rows], shift, 1), strip
                )
            padded[to, :, LANES:] = strip


def basis_body(peers, side_count, where_ref, *refs):
    own, other = refs[:4], refs[4:8]
    edges = refs[8:12]
    sides = (refs[12 : 12 + side_count], refs[12 + side_count : 12 + 2 * side_count])
    refs = refs[12 + 2 * side_count :]
    spot_ref, slots_ref, own_ref, send_ref = refs[:4]
    c_pad, s_pad, h_pad, diag, wx, wy, wz, image, basis, grads = refs[4:]
    layer, row = where_ref[0], where_ref[1]
    nz, nx = own[0].shape[0], own[0].shape[1]
    planes, width = c_pad.shape[0], c_pad.shape[1]
    high_side, low_side = 0, LANES - HALO
    if side_count == 1:
        firsts = [jnp.where(row == 0, high_side, low_side)]
    else:
        firsts = [low_side, high_side]
    beside = [
        [
            (jnp.transpose(side[...].reshape(LANES, LANES)), first)
            for side, first in zip(half, firsts)
        ]
        for half in sides
    ]
    for f, target in enumerate((c_pad, s_pad, h_pad, basis.at[0])):
        unpack(layer, f, own[f], other[f], edges, beside, target)
    def right(x):
        return pltpu.roll(x, x.shape[1] - 1, 1)

    def left(x):
        return pltpu.roll(x, 1, 1)

    def fore(x):
        return pltpu.roll(x, x.shape[0] - 1, 0)

    def back(x):
        return pltpu.roll(x, 1, 0)

    def joined(a, b):
        return jnp.where((a > 0.0) & (b > 0.0), 0.5 * (a + b), 0.0)

    for z in range(planes):
        c = c_pad[z]
        cf, cr = fore(c), right(c)
        total = cf + back(c) + cr + left(c)
        wx[z] = joined(c, cf)
        wy[z] = joined(c, cr)
        if z + 1 < planes:
            wz[z] = joined(c, c_pad[z + 1])
            total = total + c_pad[z + 1]
        if z:
            total = total + c_pad[z - 1]
        diag[z] = s_pad[z] + 3.0 * c + 0.5 * total

    alphas, gammas, norms = [], [], []

    def member(k, z, rows=slice(None), lanes=slice(None)):
        u = image[z, rows, lanes] - alphas[k - 1] * basis[k - 1, z, rows, lanes]
        if k > 1:
            u = u - gammas[k - 1] * basis[k - 2, z, rows, lanes]
        basis[k, z, rows, lanes] = u

    def folded(x):
        x = x[:, :LANES] + x[:, LANES:]
        return sum(x[r : r + 8] for r in range(8, width, 8)) + x[:8]

    for k in range(ITERS):
        if k:
            member(k, 0)
        norm = jnp.zeros((8, LANES), jnp.float32)
        energy = jnp.zeros((8, LANES), jnp.float32)
        for z in range(nz + ITERS - 1 - k):
            if k:
                member(k, z + 1)
            v = basis[k, z]
            wxz, wyz = wx[z], wy[z]
            av = diag[z] * v - wz[z] * basis[k, z + 1]
            if z:
                av = av - wz[z - 1] * basis[k, z - 1]
            av = av - wxz * fore(v) - back(wxz * v) - wyz * right(v) - left(wyz * v)
            image[z] = av
            norm = norm + folded(v * v)
            energy = energy + folded(v * av)
        norm = all_sum(norm)
        alphas.append(safe_ratio(all_sum(energy), norm))
        gammas.append(safe_ratio(norm, norms[-1]) if k else jnp.zeros_like(norm))
        norms.append(norm)
    inner = slice(HALO, HALO + nx)
    for z in range(nz):
        member(ITERS, z, inner, slice(LANES))

    for z in range(nz):
        c = -0.5 * c_pad[z, inner, :LANES]
        h = h_pad[z, inner, :LANES]
        wide = h_pad[z, inner, :]
        grads[0, z] = c * (h - h_pad[z, HALO + 1 : HALO + nx + 1, :LANES])
        grads[1, z] = c * (h - h_pad[z, HALO - 1 : HALO + nx - 1, :LANES])
        grads[2, z] = c * (h - right(wide)[:, :LANES])
        grads[3, z] = c * (h - left(wide)[:, :LANES])
        grads[4, z] = c * (h - h_pad[z + 1, inner, :LANES])
        grads[5, z] = c * (h - h_pad[z - 1, inner, :LANES]) if z else c * h

    dots = {}
    for i in range(ITERS + 1):
        for j in range(i + 1):
            acc = basis[i, 0, inner, :LANES] * basis[j, 0, inner, :LANES]
            for z in range(1, nz):
                acc = acc + basis[i, z, inner, :LANES] * basis[j, z, inner, :LANES]
            dots[i, j] = dots[j, i] = all_sum(acc)

    def operator(i, j):
        entry = dots[i, j + 1] + alphas[j] * dots[i, j]
        return entry + gammas[j] * dots[i, j - 1] if j else entry

    lanes = lane_iota(1)
    facts = []
    for j in range(ITERS):
        row_facts = [0.5 * (operator(j, m) + operator(m, j)) for m in range(ITERS)]
        row_facts += [alphas[j], gammas[j], norms[j], dots[j, 0]]
        entries = jnp.zeros((1, LANES), jnp.float32)
        for place, entry in enumerate(row_facts):
            entries = jnp.where(lanes == FACTS + place, entry, entries)
        facts.append(entries)

    sums = []
    for k in range(ITERS):
        acc = jnp.zeros((nx, LANES), jnp.float32)
        for z in range(nz):
            u = basis[k, z, inner, :LANES]
            wide = basis[k, z, inner, :]
            acc = acc + (u - basis[k, z, HALO + 1 : HALO + nx + 1, :LANES]) * grads[0, z]
            acc = acc + (u - basis[k, z, HALO - 1 : HALO + nx - 1, :LANES]) * grads[1, z]
            acc = acc + (u - right(wide)[:, :LANES]) * grads[2, z]
            acc = acc + (u - left(wide)[:, :LANES]) * grads[3, z]
            acc = acc + (u - basis[k, z + 1, inner, :LANES]) * grads[4, z]
            if z:
                acc = acc + (u - basis[k, z - 1, inner, :LANES]) * grads[5, z]
            else:
                acc = acc + u * grads[5, z]
            own_ref[k, jnp.where(layer == 0, z, nz - 1 - z)] = u
        sums.append(acc)
    blocks_x = nx // 4
    four = jnp.where(
        lax.shift_right_logical(lane_iota(blocks_x, nx), 2) == row_iota(blocks_x, nx), 1.0, 0.0
    )
    sums = mm(four, jnp.concatenate(sums, axis=1), precision=EXACT)
    spot = [spot_ref[r : r + 1, :] for r in range(blocks_x)]
    lane_hits = jnp.concatenate(
        [
            jnp.where(row_iota(LANES) == (p & (LANES - 1)), 1.0, 0.0).astype(jnp.bfloat16)
            for p in spot
        ],
        axis=1,
    )
    peer_at = row_iota(peers)
    row_hit = [(p >= 0) & (peer_at == lax.shift_right_arithmetic(p, LANE_BITS)) for p in spot]
    values = []
    for k in range(ITERS):
        pair = sums[:, k * LANES : (k + 1) * LANES]
        pair = pair + pltpu.roll(pair, LANES - 1, 1)
        for p in pieces_of(pair):
            values.append(
                jnp.concatenate(
                    [picked(row_hit[r], p[r : r + 1]) for r in range(blocks_x)], axis=1
                )
            )
    dense = mm(jnp.concatenate(values, axis=0), lane_hits, NT)
    copies = send_ref.shape[0] // peers
    for k in range(ITERS):
        at = 3 * k * peers
        rows = dense[at : at + peers] + dense[at + peers : at + 2 * peers]
        rows = rows + dense[at + 2 * peers : at + 3 * peers]
        rows = jnp.where(lane_iota(peers) < FACTS, rows, facts[k])
        if k < 2:
            slots = pltpu.roll(slots_ref[...], (1 - k) * (LANES - SLOTS) + FACTS, 1)
            rows = jnp.where(lane_iota(peers) < SLOTS, rows, slots)
        for peer in range(peers):
            for copy in range(copies):
                send_ref[peer * copies + copy, k : k + 1, :] = rows[peer : peer + 1]


def solve_body(copies, where_ref, got_ref, own_ref, adjoint_ref, pilot_ref):
    senders = got_ref.shape[0]
    peers = senders // copies
    groups = senders * ITERS // LANES
    got = got_ref[...].reshape(groups, LANES, LANES)
    turned = [jnp.transpose(got[g])[FACTS:SLOTS] for g in range(groups)]

    def fact(place):
        return jnp.concatenate([t[place : place + 1] for t in turned], axis=0)

    alpha, gamma, weight, rhs = (fact(ITERS + place) for place in range(4))
    at = lane_iota(groups) & (ITERS - 1)
    gamma_next = jnp.where(at < ITERS - 1, pltpu.roll(gamma, LANES - 1, 1), 0.0)

    now = jnp.where(at == 0, 1.0, 0.0)
    last, norm_last = None, None
    common = []
    for k in range(ITERS):
        common.append(now)
        if k == ITERS - 1:
            break
        image = jnp.where(at > 0, pltpu.roll(now, 1, 1), 0.0) + alpha * now
        image = image + gamma_next * pltpu.roll(now, LANES - 1, 1)
        norm = all_sum(weight * now * now)
        following = image - safe_ratio(all_sum(weight * now * image), norm) * now
        if k:
            following = following - safe_ratio(norm, norm_last) * last
        now, last, norm_last = following, now, norm

    lanes = lane_iota(ITERS)
    ra, ca = row_iota(LANES), lane_iota(LANES)
    same = lax.shift_right_logical(ra, 3) == lax.shift_right_logical(ca, 3)
    spread = jnp.concatenate(
        [jnp.where(same & ((ra & (ITERS - 1)) == m), 1.0, 0.0) for m in range(ITERS)], axis=1
    )
    system = jnp.zeros((ITERS, LANES), jnp.float32)
    stacked = []
    for g in range(groups):
        t = jnp.concatenate([c[g : g + 1] for c in common], axis=0)
        stacked.append(t)
        wide = mm(t, spread, precision=EXACT)
        image = jnp.zeros((ITERS, LANES), jnp.float32)
        for m in range(ITERS):
            image = image + turned[g][m : m + 1] * wide[:, m * LANES : (m + 1) * LANES]
        right = jnp.concatenate(
            [image, rhs[g : g + 1], jnp.zeros((LANES - ITERS - 1, LANES), jnp.float32)], axis=0
        )
        system = system + mm(t, right, NT, precision=EXACT)
    rows = row_iota(ITERS)
    for p in range(ITERS):
        pivot_row = system[p : p + 1]
        pivot = jnp.sum(jnp.where(lanes == p, system, 0.0), axis=1, keepdims=True)
        inverse = jnp.sum(jnp.where(rows[:, :1] == p, pivot, 0.0), axis=0, keepdims=True)
        inverse = jnp.where(inverse > 0.0, 1.0 / jnp.where(inverse > 0.0, inverse, 1.0), 0.0)
        pivot_row = pivot_row * inverse
        system = jnp.where(rows == p, pivot_row, system - pivot * pivot_row)
    answer = jnp.sum(jnp.where(lanes == ITERS, system, 0.0), axis=1, keepdims=True)

    weights = [jnp.sum(answer * t, axis=0, keepdims=True) for t in stacked]
    me = where_ref[3]
    mine = []
    for k in range(ITERS):
        w = jnp.zeros((1, 1), jnp.float32)
        for g in range(groups):
            hit = lane_iota(1) == me * ITERS + k - g * LANES
            w = w + jnp.sum(jnp.where(hit, weights[g], 0.0), axis=1, keepdims=True)
        mine.append(w)
    for z in range(own_ref.shape[1]):
        acc = mine[0] * own_ref[0, z]
        for k in range(1, ITERS):
            acc = acc + mine[k] * own_ref[k, z]
        adjoint_ref[z] = acc

    per_group = LANES // ITERS // copies
    sender = lax.div(lane_iota(per_group), jnp.int32(ITERS * copies))
    values = jnp.concatenate(
        [
            mm(jnp.where(sender == row_iota(per_group), weights[g], 0.0), got[g], precision=EXACT)
            for g in range(groups)
        ],
        axis=0,
    )
    rows_at, lanes_at = row_iota(pilot_ref.shape[0]), row_iota(LANES)
    held = lane_iota(peers) < pilot_ref.shape[0] * LANES // peers
    pieces = pieces_of(jnp.where(held, values, 0.0))
    left, right = [[], [], []], []
    room = LANES - SLOTS
    for s in range(peers):
        slot = jnp.where(
            lane_iota(1) < room,
            pltpu.roll(got_ref[s * copies, 0:1, :], room, 1),
            pltpu.roll(got_ref[s * copies, 1:2, :], 2 * room, 1),
        ).astype(jnp.int32)
        hit = rows_at == lax.shift_right_logical(slot, LANE_BITS)
        for q, piece in enumerate(pieces):
            left[q].append(picked(hit, piece[s : s + 1]))
        right.append(
            jnp.where(lanes_at == (slot & (LANES - 1)), 1.0, 0.0).astype(jnp.bfloat16)
        )
    right = jnp.concatenate(right, axis=1)
    pilot_ref[...] = sum(mm(jnp.concatenate(q, axis=1), right, NT) for q in left)


def tied(*values):
    return lax.optimization_barrier(values)


def neighbour_pairs(axis):
    forward = [(i, i + 1) for i in range(lax.axis_size(axis) - 1)]
    return forward, [(b, a) for a, b in forward]


def swapped(x):
    return lax.ppermute(x, "layers", [(0, 1), (1, 0)])


def on_device(
    state_field,
    conductivity,
    storage,
    gauge_owner,
    gauge_cell,
    gauge_value,
    gauge_weight,
    pilot_index,
):
    nz, nx, ny = state_field.shape
    peers = lax.axis_size("cols") * lax.axis_size("rows")
    devices = peers * lax.axis_size("layers")
    gauges = gauge_owner.shape[0]
    capacity = 4 * gauges // peers
    f32 = jnp.float32
    row_count = lax.axis_size("rows")

    def shape(*dims, dtype=f32):
        return jax.ShapeDtypeStruct(dims, dtype)

    def flat(x):
        return x.reshape(gauges // LANES, LANES)

    where = jnp.stack(
        [lax.axis_index(a) for a in ("layers", "rows", "cols", GRID_AXES)]
    ).astype(jnp.int32)

    obs = pltpu.VMEM((gauges // LANES, LANES), f32)
    obs_int = pltpu.VMEM((gauges // LANES, LANES), jnp.int32)
    payload = kernel_call(
        functools.partial(route_body, peers, capacity),
        shape(peers, 3 * capacity // LANES, LANES),
        [obs_int, obs_int, obs, obs, pltpu.SemaphoreType.DMA((4,))],
        weight=5,
    )(in_specs=[ANY] * 4, out_specs=VMEM)(
        flat(gauge_owner), flat(gauge_cell), flat(gauge_value), flat(gauge_weight)
    )
    payload, pilot_index = tied(payload, pilot_index)
    got = lax.all_to_all(payload, PEER_AXES, 0, 0, tiled=True)
    spot, slots = kernel_call(
        pilot_body, (shape(nx // 4, LANES, dtype=jnp.int32), shape(peers, LANES))
    )(in_specs=[VMEM], out_specs=(VMEM, VMEM))(pilot_index)

    fixed = (conductivity, storage, state_field)
    got, spot, *fixed = tied(got, spot, *fixed)
    fixed_other = [swapped(x) for x in fixed]
    edge = shape(4, nz, HALO, LANES)
    source, up, down = kernel_call(
        functools.partial(source_body, capacity // LANES),
        (shape(nz, nx, LANES), edge, edge),
        [pltpu.VMEM((nz * nx, 3 * LANES), f32)],
        weight=10,
    )(in_specs=[VMEM] * 4, out_specs=(VMEM,) * 3)(got, *fixed)
    forward, backward = neighbour_pairs("cols")
    low = lax.ppermute(up, "cols", forward)
    high = lax.ppermute(down, "cols", backward)
    other = swapped(source)

    mine = (*fixed, source)

    def packed(low_side):
        return kernel_call(
            functools.partial(pack_body, low_side), shape(2 * nz, HALO, LANES)
        )(in_specs=[SMEM] + [VMEM] * 6, out_specs=VMEM)(where, *mine, low, high)

    if row_count == 2:
        sides = [lax.ppermute(packed(None), "rows", [(0, 1), (1, 0)])]
    else:
        forward, backward = neighbour_pairs("rows")
        sides = [
            lax.ppermute(packed(False), "rows", forward),
            lax.ppermute(packed(True), "rows", backward),
        ]
    edges = [low, high, swapped(low), swapped(high)]
    sides = sides + [swapped(x) for x in sides]

    each = nx * ny // 8 // LANES
    planes, width = 2 * nz, nx + 2 * HALO
    padded = pltpu.VMEM((planes, width, 2 * LANES), f32)
    own, send = kernel_call(
        functools.partial(basis_body, peers, len(sides) // 2),
        (shape(ITERS, nz, nx, LANES), shape(devices, ITERS, LANES)),
        [padded] * 8
        + [
            pltpu.VMEM((ITERS + 1, planes, width, 2 * LANES), f32),
            pltpu.VMEM((6, nz, nx, LANES), f32),
        ],
        weight=10,
    )(in_specs=[SMEM] + [VMEM] * (14 + len(sides)), out_specs=(VMEM, VMEM))(
        where, *mine, *fixed_other, other, *edges, *sides, spot, slots
    )
    parts = lax.all_to_all(send, GRID_AXES, 0, 0, tiled=True)
    adjoint, pilot = kernel_call(
        functools.partial(solve_body, devices // peers), (shape(nz, nx, ny), shape(each, LANES))
    )(in_specs=[SMEM] + [VMEM] * 2, out_specs=(VMEM, VMEM))(where, parts, own)
    return adjoint, pilot.reshape(-1)


def solution(mesh):
    return jax.shard_map(
        on_device,
        mesh=mesh,
        in_specs=(
            P(("groups", "layers"), "cols", "rows"),
            P(("groups", "layers"), "cols", "rows"),
            P(("groups", "layers"), "cols", "rows"),
            P(("groups", "cols", "rows", "layers")),
            P(("groups", "cols", "rows", "layers")),
            P(("groups", "cols", "rows", "layers")),
            P(("groups", "cols", "rows", "layers")),
            P("cols", "rows"),
        ),
        out_specs=(P(("groups", "layers"), "cols", "rows"), P(("groups", "cols", "rows"))),
        check_vma=False,
    )
```

```python
import functools

import jax
import jax.numpy as jnp
from jax import lax
from jax.experimental import pallas as pl
from jax.experimental.pallas import tpu as pltpu
from jax.sharding import PartitionSpec as P

ITERS = 8
HALO = 8
FACTS = 64
SLOTS = 96
LANES = 128
LANE_BITS = 7
GRID_AXES = ("cols", "rows", "layers")
PEER_AXES = ("cols", "rows")
NT = (((1,), (1,)), ((), ()))
EXACT = lax.Precision.HIGHEST
VMEM_BYTES = 50 * 1024 * 1024


def kernel_call(body, out_shape, scratch=(), weight=1, vmem=VMEM_BYTES):
    return functools.partial(
        pl.pallas_call,
        body,
        out_shape=out_shape,
        scratch_shapes=list(scratch),
        compiler_params=pltpu.CompilerParams(vmem_limit_bytes=vmem),
        cost_estimate=pl.CostEstimate(
            flops=0, bytes_accessed=weight * 3_000_000, transcendentals=0
        ),
    )


VMEM = pl.BlockSpec(memory_space=pltpu.VMEM)
SMEM = pl.BlockSpec(memory_space=pltpu.SMEM)
HBM = pl.BlockSpec(memory_space=pltpu.HBM)


def pieces_of(x):
    first = x.astype(jnp.bfloat16).astype(jnp.float32)
    rest = x - first
    second = rest.astype(jnp.bfloat16).astype(jnp.float32)
    return first, second, rest - second


def row_iota(rows, lanes=LANES):
    return lax.broadcasted_iota(jnp.int32, (rows, lanes), 0)


def lane_iota(rows, lanes=LANES):
    return lax.broadcasted_iota(jnp.int32, (rows, lanes), 1)


def picked(mask, row):
    return jnp.where(mask, row, jnp.zeros_like(row)).astype(jnp.bfloat16)


TILE = 16


def spread16(x, r):
    return jnp.broadcast_to(x[r : r + 1], (TILE, LANES)).astype(jnp.bfloat16)


def hits16(count, row):
    at = row_iota(TILE).astype(jnp.float32).astype(jnp.bfloat16)
    return [at + jnp.bfloat16(TILE * i) == row for i in range(count // TILE)]


def filled16(masks, value):
    zero = jnp.zeros((TILE, LANES), jnp.bfloat16)
    return jnp.concatenate([jnp.where(m, value, zero) for m in masks], axis=0)


def mm(a, b, dims=(((1,), (0,)), ((), ())), precision=None):
    return lax.dot_general(a, b, dims, precision=precision, preferred_element_type=jnp.float32)


def ranks(owner, peers):
    rows = owner.shape[0]
    ra, ca = row_iota(LANES, 2 * LANES), lane_iota(LANES, 2 * LANES)
    earlier_lane = jnp.where((ra < ca) | (ca >= LANES), 1.0, 0.0).astype(jnp.bfloat16)
    earlier_row = jnp.where(row_iota(rows, rows) > lane_iota(rows, rows), 1.0, 0.0).astype(
        jnp.bfloat16
    )
    hits = [owner == peer for peer in range(peers)]
    ones = jnp.concatenate([jnp.where(h, 1.0, 0.0).astype(jnp.bfloat16) for h in hits], axis=0)
    counts = mm(ones, earlier_lane)
    part = [counts[p * rows : (p + 1) * rows] for p in range(peers)]
    before = mm(
        earlier_row, jnp.concatenate([c[:, LANES:] for c in part], axis=1).astype(jnp.bfloat16)
    )
    rank = jnp.zeros((rows, LANES), jnp.float32)
    for p in range(peers):
        rank = jnp.where(
            hits[p], part[p][:, :LANES] + before[:, p * LANES : (p + 1) * LANES], rank
        )
    return rank.astype(jnp.int32)


def route_body(
    peers, capacity, owner_hbm, cell_hbm, value_hbm, weight_hbm, out_ref,
    owner_ref, cell_ref, value_ref, weight_ref, sems,
):
    copies = [
        pltpu.make_async_copy(source, target, sems.at[i])
        for i, (source, target) in enumerate(
            (
                (owner_hbm, owner_ref),
                (cell_hbm, cell_ref),
                (value_hbm, value_ref),
                (weight_hbm, weight_ref),
            )
        )
    ]
    for copy in copies:
        copy.start()
    for copy in copies:
        copy.wait()
    rows = owner_ref.shape[0]
    owner = owner_ref[...]
    position = owner * capacity + ranks(owner, peers)
    slot_row = lax.shift_right_logical(position, LANE_BITS).astype(jnp.float32)
    slot_lane = (position & (LANES - 1)).astype(jnp.float32)
    cell = cell_ref[...]
    columns = [
        lax.shift_right_logical(cell, LANE_BITS).astype(jnp.float32),
        (cell & (LANES - 1)).astype(jnp.float32),
        *pieces_of(value_ref[...]),
        *pieces_of(weight_ref[...]),
    ]
    slot_rows = peers * capacity // LANES
    one = jnp.ones((TILE, LANES), jnp.bfloat16)
    total = None
    for start in range(0, rows, TILE):
        at_row, at_lane = [], [[] for _ in columns]
        for r in range(start, start + TILE):
            at_row.append(filled16(hits16(slot_rows, spread16(slot_row, r)), one))
            masks = hits16(LANES, spread16(slot_lane, r))
            for q, column in enumerate(columns):
                at_lane[q].append(filled16(masks, spread16(column, r)))
        at_lane = jnp.concatenate([jnp.concatenate(q, axis=1) for q in at_lane], axis=0)
        part = mm(at_lane, jnp.concatenate(at_row, axis=1), NT)
        total = part if total is None else total + part
    part = [total[q * LANES : (q + 1) * LANES] for q in range(len(columns))]
    fields = [
        part[0] * LANES + part[1],
        part[2] + part[3] + part[4],
        part[5] + part[6] + part[7],
    ]
    fields = [jnp.transpose(f) for f in fields]
    each = capacity // LANES
    for peer in range(peers):
        for q, field in enumerate(fields):
            out_ref[peer, q * each : (q + 1) * each, :] = field[peer * each : (peer + 1) * each]


def pilot_body(pilot_ref, spot_ref, slots_ref):
    peers = slots_ref.shape[0]
    blocks_x = pilot_ref.shape[0] // 4
    pilots = pilot_ref.shape[0] * pilot_ref.shape[1] // 8
    pilot = jnp.concatenate([pilot_ref[4 * r : 4 * r + 1, :] for r in range(blocks_x)], axis=0)
    owner = lax.div(pilot, jnp.int32(pilots))
    slot = pilot - owner * pilots
    first = (lane_iota(blocks_x) & 1) == 0
    owner = jnp.where(first, owner, -1)
    rank = ranks(owner, peers)
    spot_ref[...] = jnp.where(first, owner * LANES + rank, -1)
    left, high, low = [], [], []
    peer_at, lanes_at = row_iota(peers), row_iota(LANES)
    for r in range(blocks_x):
        left.append(jnp.where(peer_at == owner[r : r + 1], 1.0, 0.0).astype(jnp.bfloat16))
        hit = lanes_at == rank[r : r + 1]
        number = slot[r : r + 1]
        high.append(picked(hit, lax.shift_right_logical(number, LANE_BITS).astype(jnp.float32)))
        low.append(picked(hit, (number & (LANES - 1)).astype(jnp.float32)))
    left = jnp.concatenate(left, axis=1)
    slots_ref[...] = mm(left, jnp.concatenate(high, axis=1), NT) * LANES + mm(
        left, jnp.concatenate(low, axis=1), NT
    )


def source_body(
    each, got_ref, conductivity_ref, storage_ref, state_ref, out_ref, up_ref, down_ref
):
    peers = got_ref.shape[0]
    nz, nx = state_ref.shape[0], state_ref.shape[1]
    cells = nz * nx
    one = jnp.ones((TILE, LANES), jnp.bfloat16)

    def sixteen(group, q):
        peer, row = divmod(group * TILE, each)
        if each >= TILE:
            return got_ref[peer, q * each + row : q * each + row + TILE, :]
        return jnp.concatenate(
            [got_ref[peer + i, q * each : (q + 1) * each, :] for i in range(TILE // each)], axis=0
        )

    total = None
    for group in range(peers * each // TILE):
        cell = sixteen(group, 0).astype(jnp.int32)
        high = lax.shift_right_logical(cell, LANE_BITS)
        low = cell & (LANES - 1)
        heads = []
        for r in range(0, TILE, 8):
            head = jnp.zeros((8, LANES), jnp.float32)
            for z in range(nz):
                for x in range(nx):
                    line = jnp.broadcast_to(state_ref[z, x : x + 1, :], (8, LANES))
                    line = jnp.take_along_axis(line, low[r : r + 8], axis=1)
                    head = jnp.where(high[r : r + 8] == z * nx + x, line, head)
            heads.append(head)
        misfit = sixteen(group, 2) * (jnp.concatenate(heads, axis=0) - sixteen(group, 1))
        coarse = misfit.astype(jnp.bfloat16).astype(jnp.float32)
        pieces = (coarse, misfit - coarse)
        high, low = high.astype(jnp.float32), low.astype(jnp.float32)
        at_row, at_lane = [], [[] for _ in pieces]
        for r in range(TILE):
            at_row.append(filled16(hits16(cells, spread16(high, r)), one))
            masks = hits16(LANES, spread16(low, r))
            for q, piece in enumerate(pieces):
                at_lane[q].append(filled16(masks, spread16(piece, r)))
        at_lane = jnp.concatenate([jnp.concatenate(q, axis=1) for q in at_lane], axis=0)
        part = mm(at_lane, jnp.concatenate(at_row, axis=1), NT)
        total = part if total is None else total + part
    total = jnp.transpose(total[:LANES] + total[LANES:])
    out_ref[...] = total.reshape(nz, nx, LANES)
    for f, field in enumerate((conductivity_ref, storage_ref, state_ref, out_ref)):
        up_ref[f] = field[:, nx - HALO :, :]
        down_ref[f] = field[:, :HALO, :]


def all_sum(x):
    while x.ndim > 2:
        x = jnp.sum(x, axis=0)
    return jnp.sum(jnp.sum(x, axis=0, keepdims=True), axis=1, keepdims=True)


def safe_ratio(a, b):
    return jnp.where(b > 0.0, a / jnp.where(b > 0.0, b, 1.0), 0.0)


def pack_body(low_side, where_ref, *refs):
    *fields, low_ref, high_ref, out_ref = refs
    nz, nx = fields[0].shape[0], fields[0].shape[1]
    lanes = lane_iota(2 * (nx + 2 * HALO))
    tall = jnp.zeros(lanes.shape, jnp.float32)
    for pair in range(2):
        for z in range(nz):
            at = (pair * nz + z) * HALO
            x = jnp.concatenate(
                [
                    part
                    for f in (2 * pair, 2 * pair + 1)
                    for part in (low_ref[f, z], fields[f][z], high_ref[f, z])
                ],
                axis=0,
            )
            if low_side is None:
                shift = (at + jnp.where(where_ref[1] == 0, HALO, 0)) & (LANES - 1)
            else:
                shift = at if low_side else (at + HALO) & (LANES - 1)
            x = pltpu.roll(x, shift, 1)
            tall = jnp.where((lanes >= at) & (lanes < at + HALO), x, tall)
    rest = LANES - tall.shape[0]
    tall = jnp.concatenate([tall, jnp.zeros((rest, LANES), jnp.float32)], axis=0)
    out_ref[...] = jnp.transpose(tall).reshape(out_ref.shape)


def unpack(layer, f, own, other, edges, beside, padded):
    nz, nx = own.shape[0], own.shape[1]
    tall = nx + 2 * HALO
    at = lane_iota(tall)
    rows = slice((f % 2) * tall, (f % 2 + 1) * tall)
    for half, block in ((0, own), (1, other)):
        low, high = edges[2 * half], edges[2 * half + 1]
        for i in range(nz):
            j = jnp.where(layer == 0, i, nz - 1 - i)
            to = half * nz + i
            padded[to, HALO : HALO + nx, :LANES] = block[j]
            padded[to, :HALO, :LANES] = low[f, j]
            padded[to, HALO + nx :, :LANES] = high[f, j]
            strip = jnp.zeros((tall, LANES), jnp.float32)
            for tiles, first in beside[half]:
                shift = (2 * LANES + first - (f // 2 * nz + j) * HALO) & (LANES - 1)
                strip = jnp.where(
                    (at >= first) & (at < first + HALO), pltpu.roll(tiles[rows], shift, 1), strip
                )
            padded[to, :, LANES:] = strip


def basis_body(peers, side_count, where_ref, *refs):
    own, other = refs[:4], refs[4:8]
    edges = refs[8:12]
    sides = (refs[12 : 12 + side_count], refs[12 + side_count : 12 + 2 * side_count])
    refs = refs[12 + 2 * side_count :]
    spot_ref, slots_ref, own_ref, send_ref = refs[:4]
    c_pad, s_pad, h_pad, diag, wx, wy, wz, image, basis, grads = refs[4:]
    layer, row = where_ref[0], where_ref[1]
    nz, nx = own[0].shape[0], own[0].shape[1]
    planes, width = c_pad.shape[0], c_pad.shape[1]
    high_side, low_side = 0, LANES - HALO
    if side_count == 1:
        firsts = [jnp.where(row == 0, high_side, low_side)]
    else:
        firsts = [low_side, high_side]
    beside = [
        [
            (jnp.transpose(side[...].reshape(LANES, LANES)), first)
            for side, first in zip(half, firsts)
        ]
        for half in sides
    ]
    for f, target in enumerate((c_pad, s_pad, h_pad, basis.at[0])):
        unpack(layer, f, own[f], other[f], edges, beside, target)
    def right(x):
        return pltpu.roll(x, x.shape[1] - 1, 1)

    def left(x):
        return pltpu.roll(x, 1, 1)

    def fore(x):
        return pltpu.roll(x, x.shape[0] - 1, 0)

    def back(x):
        return pltpu.roll(x, 1, 0)

    def joined(a, b):
        return jnp.where((a > 0.0) & (b > 0.0), 0.5 * (a + b), 0.0)

    for z in range(planes):
        c = c_pad[z]
        cf, cr = fore(c), right(c)
        total = cf + back(c) + cr + left(c)
        wx[z] = joined(c, cf)
        wy[z] = joined(c, cr)
        if z + 1 < planes:
            wz[z] = joined(c, c_pad[z + 1])
            total = total + c_pad[z + 1]
        if z:
            total = total + c_pad[z - 1]
        diag[z] = s_pad[z] + 3.0 * c + 0.5 * total

    alphas, gammas, norms = [], [], []

    def member(k, z, rows=slice(None), lanes=slice(None)):
        u = image[z, rows, lanes] - alphas[k - 1] * basis[k - 1, z, rows, lanes]
        if k > 1:
            u = u - gammas[k - 1] * basis[k - 2, z, rows, lanes]
        basis[k, z, rows, lanes] = u

    def folded(x):
        x = x[:, :LANES] + x[:, LANES:]
        return sum(x[r : r + 8] for r in range(8, width, 8)) + x[:8]

    for k in range(ITERS):
        if k:
            member(k, 0)
        norm = jnp.zeros((8, LANES), jnp.float32)
        energy = jnp.zeros((8, LANES), jnp.float32)
        for z in range(nz + ITERS - 1 - k):
            if k:
                member(k, z + 1)
            v = basis[k, z]
            wxz, wyz = wx[z], wy[z]
            av = diag[z] * v - wz[z] * basis[k, z + 1]
            if z:
                av = av - wz[z - 1] * basis[k, z - 1]
            av = av - wxz * fore(v) - back(wxz * v) - wyz * right(v) - left(wyz * v)
            image[z] = av
            norm = norm + folded(v * v)
            energy = energy + folded(v * av)
        norm = all_sum(norm)
        alphas.append(safe_ratio(all_sum(energy), norm))
        gammas.append(safe_ratio(norm, norms[-1]) if k else jnp.zeros_like(norm))
        norms.append(norm)
    inner = slice(HALO, HALO + nx)
    for z in range(nz):
        member(ITERS, z, inner, slice(LANES))

    for z in range(nz):
        c = -0.5 * c_pad[z, inner, :LANES]
        h = h_pad[z, inner, :LANES]
        wide = h_pad[z, inner, :]
        grads[0, z] = c * (h - h_pad[z, HALO + 1 : HALO + nx + 1, :LANES])
        grads[1, z] = c * (h - h_pad[z, HALO - 1 : HALO + nx - 1, :LANES])
        grads[2, z] = c * (h - right(wide)[:, :LANES])
        grads[3, z] = c * (h - left(wide)[:, :LANES])
        grads[4, z] = c * (h - h_pad[z + 1, inner, :LANES])
        grads[5, z] = c * (h - h_pad[z - 1, inner, :LANES]) if z else c * h

    dots = {}
    for i in range(ITERS + 1):
        for j in range(i + 1):
            acc = basis[i, 0, inner, :LANES] * basis[j, 0, inner, :LANES]
            for z in range(1, nz):
                acc = acc + basis[i, z, inner, :LANES] * basis[j, z, inner, :LANES]
            dots[i, j] = dots[j, i] = all_sum(acc)

    def operator(i, j):
        entry = dots[i, j + 1] + alphas[j] * dots[i, j]
        return entry + gammas[j] * dots[i, j - 1] if j else entry

    lanes = lane_iota(1)
    facts = []
    for j in range(ITERS):
        row_facts = [0.5 * (operator(j, m) + operator(m, j)) for m in range(ITERS)]
        row_facts += [alphas[j], gammas[j], norms[j], dots[j, 0]]
        entries = jnp.zeros((1, LANES), jnp.float32)
        for place, entry in enumerate(row_facts):
            entries = jnp.where(lanes == FACTS + place, entry, entries)
        facts.append(entries)

    sums = []
    for k in range(ITERS):
        acc = jnp.zeros((nx, LANES), jnp.float32)
        for z in range(nz):
            u = basis[k, z, inner, :LANES]
            wide = basis[k, z, inner, :]
            acc = acc + (u - basis[k, z, HALO + 1 : HALO + nx + 1, :LANES]) * grads[0, z]
            acc = acc + (u - basis[k, z, HALO - 1 : HALO + nx - 1, :LANES]) * grads[1, z]
            acc = acc + (u - right(wide)[:, :LANES]) * grads[2, z]
            acc = acc + (u - left(wide)[:, :LANES]) * grads[3, z]
            acc = acc + (u - basis[k, z + 1, inner, :LANES]) * grads[4, z]
            if z:
                acc = acc + (u - basis[k, z - 1, inner, :LANES]) * grads[5, z]
            else:
                acc = acc + u * grads[5, z]
            own_ref[k, jnp.where(layer == 0, z, nz - 1 - z)] = u
        sums.append(acc)
    blocks_x = nx // 4
    four = jnp.where(
        lax.shift_right_logical(lane_iota(blocks_x, nx), 2) == row_iota(blocks_x, nx), 1.0, 0.0
    )
    sums = mm(four, jnp.concatenate(sums, axis=1), precision=EXACT)
    spot = [spot_ref[r : r + 1, :] for r in range(blocks_x)]
    lane_hits = jnp.concatenate(
        [
            jnp.where(row_iota(LANES) == (p & (LANES - 1)), 1.0, 0.0).astype(jnp.bfloat16)
            for p in spot
        ],
        axis=1,
    )
    peer_at = row_iota(peers)
    row_hit = [(p >= 0) & (peer_at == lax.shift_right_arithmetic(p, LANE_BITS)) for p in spot]
    values = []
    for k in range(ITERS):
        pair = sums[:, k * LANES : (k + 1) * LANES]
        pair = pair + pltpu.roll(pair, LANES - 1, 1)
        for p in pieces_of(pair):
            values.append(
                jnp.concatenate(
                    [picked(row_hit[r], p[r : r + 1]) for r in range(blocks_x)], axis=1
                )
            )
    dense = mm(jnp.concatenate(values, axis=0), lane_hits, NT)
    copies = send_ref.shape[0] // peers
    for k in range(ITERS):
        at = 3 * k * peers
        rows = dense[at : at + peers] + dense[at + peers : at + 2 * peers]
        rows = rows + dense[at + 2 * peers : at + 3 * peers]
        rows = jnp.where(lane_iota(peers) < FACTS, rows, facts[k])
        if k < 2:
            slots = pltpu.roll(slots_ref[...], (1 - k) * (LANES - SLOTS) + FACTS, 1)
            rows = jnp.where(lane_iota(peers) < SLOTS, rows, slots)
        for peer in range(peers):
            for copy in range(copies):
                send_ref[peer * copies + copy, k : k + 1, :] = rows[peer : peer + 1]


def solve_body(copies, where_ref, got_ref, own_ref, adjoint_ref, pilot_ref):
    senders = got_ref.shape[0]
    peers = senders // copies
    groups = senders * ITERS // LANES
    got = got_ref[...].reshape(groups, LANES, LANES)
    turned = [jnp.transpose(got[g])[FACTS:SLOTS] for g in range(groups)]

    def fact(place):
        return jnp.concatenate([t[place : place + 1] for t in turned], axis=0)

    alpha, gamma, weight, rhs = (fact(ITERS + place) for place in range(4))
    at = lane_iota(groups) & (ITERS - 1)
    gamma_next = jnp.where(at < ITERS - 1, pltpu.roll(gamma, LANES - 1, 1), 0.0)

    now = jnp.where(at == 0, 1.0, 0.0)
    last, norm_last = None, None
    common = []
    for k in range(ITERS):
        common.append(now)
        if k == ITERS - 1:
            break
        image = jnp.where(at > 0, pltpu.roll(now, 1, 1), 0.0) + alpha * now
        image = image + gamma_next * pltpu.roll(now, LANES - 1, 1)
        norm = all_sum(weight * now * now)
        following = image - safe_ratio(all_sum(weight * now * image), norm) * now
        if k:
            following = following - safe_ratio(norm, norm_last) * last
        now, last, norm_last = following, now, norm

    lanes = lane_iota(ITERS)
    ra, ca = row_iota(LANES), lane_iota(LANES)
    same = lax.shift_right_logical(ra, 3) == lax.shift_right_logical(ca, 3)
    spread = jnp.concatenate(
        [jnp.where(same & ((ra & (ITERS - 1)) == m), 1.0, 0.0) for m in range(ITERS)], axis=1
    )
    system = jnp.zeros((ITERS, LANES), jnp.float32)
    stacked = []
    for g in range(groups):
        t = jnp.concatenate([c[g : g + 1] for c in common], axis=0)
        stacked.append(t)
        wide = mm(t, spread, precision=EXACT)
        image = jnp.zeros((ITERS, LANES), jnp.float32)
        for m in range(ITERS):
            image = image + turned[g][m : m + 1] * wide[:, m * LANES : (m + 1) * LANES]
        right = jnp.concatenate(
            [image, rhs[g : g + 1], jnp.zeros((LANES - ITERS - 1, LANES), jnp.float32)], axis=0
        )
        system = system + mm(t, right, NT, precision=EXACT)
    rows = row_iota(ITERS)
    for p in range(ITERS):
        pivot_row = system[p : p + 1]
        pivot = jnp.sum(jnp.where(lanes == p, system, 0.0), axis=1, keepdims=True)
        inverse = jnp.sum(jnp.where(rows[:, :1] == p, pivot, 0.0), axis=0, keepdims=True)
        inverse = jnp.where(inverse > 0.0, 1.0 / jnp.where(inverse > 0.0, inverse, 1.0), 0.0)
        pivot_row = pivot_row * inverse
        system = jnp.where(rows == p, pivot_row, system - pivot * pivot_row)
    answer = jnp.sum(jnp.where(lanes == ITERS, system, 0.0), axis=1, keepdims=True)

    weights = [jnp.sum(answer * t, axis=0, keepdims=True) for t in stacked]
    me = where_ref[3]
    mine = []
    for k in range(ITERS):
        w = jnp.zeros((1, 1), jnp.float32)
        for g in range(groups):
            hit = lane_iota(1) == me * ITERS + k - g * LANES
            w = w + jnp.sum(jnp.where(hit, weights[g], 0.0), axis=1, keepdims=True)
        mine.append(w)
    for z in range(own_ref.shape[1]):
        acc = mine[0] * own_ref[0, z]
        for k in range(1, ITERS):
            acc = acc + mine[k] * own_ref[k, z]
        adjoint_ref[z] = acc

    per_group = LANES // ITERS // copies
    sender = lax.div(lane_iota(per_group), jnp.int32(ITERS * copies))
    values = jnp.concatenate(
        [
            mm(jnp.where(sender == row_iota(per_group), weights[g], 0.0), got[g], precision=EXACT)
            for g in range(groups)
        ],
        axis=0,
    )
    rows_at, lanes_at = row_iota(pilot_ref.shape[0]), row_iota(LANES)
    held = lane_iota(peers) < pilot_ref.shape[0] * LANES // peers
    pieces = pieces_of(jnp.where(held, values, 0.0))
    left, right = [[], [], []], []
    room = LANES - SLOTS
    for s in range(peers):
        slot = jnp.where(
            lane_iota(1) < room,
            pltpu.roll(got_ref[s * copies, 0:1, :], room, 1),
            pltpu.roll(got_ref[s * copies, 1:2, :], 2 * room, 1),
        ).astype(jnp.int32)
        hit = rows_at == lax.shift_right_logical(slot, LANE_BITS)
        for q, piece in enumerate(pieces):
            left[q].append(picked(hit, piece[s : s + 1]))
        right.append(
            jnp.where(lanes_at == (slot & (LANES - 1)), 1.0, 0.0).astype(jnp.bfloat16)
        )
    right = jnp.concatenate(right, axis=1)
    pilot_ref[...] = sum(mm(jnp.concatenate(q, axis=1), right, NT) for q in left)


def tied(*values):
    return lax.optimization_barrier(values)


def neighbour_pairs(axis):
    forward = [(i, i + 1) for i in range(lax.axis_size(axis) - 1)]
    return forward, [(b, a) for a, b in forward]


def swapped(x):
    return lax.ppermute(x, "layers", [(0, 1), (1, 0)])


def on_device(
    state_field,
    conductivity,
    storage,
    gauge_owner,
    gauge_cell,
    gauge_value,
    gauge_weight,
    pilot_index,
):
    nz, nx, ny = state_field.shape
    peers = lax.axis_size("cols") * lax.axis_size("rows")
    devices = peers * lax.axis_size("layers")
    gauges = gauge_owner.shape[0]
    capacity = 4 * gauges // peers
    f32 = jnp.float32
    row_count = lax.axis_size("rows")

    def shape(*dims, dtype=f32):
        return jax.ShapeDtypeStruct(dims, dtype)

    def flat(x):
        return x.reshape(gauges // LANES, LANES)

    where = jnp.stack(
        [lax.axis_index(a) for a in ("layers", "rows", "cols", GRID_AXES)]
    ).astype(jnp.int32)

    obs = pltpu.VMEM((gauges // LANES, LANES), f32)
    obs_int = pltpu.VMEM((gauges // LANES, LANES), jnp.int32)
    payload = kernel_call(
        functools.partial(route_body, peers, capacity),
        shape(peers, 3 * capacity // LANES, LANES),
        [obs_int, obs_int, obs, obs, pltpu.SemaphoreType.DMA((4,))],
        weight=5,
        vmem=64 * 1024 * 1024,
    )(in_specs=[HBM] * 4, out_specs=VMEM)(
        flat(gauge_owner), flat(gauge_cell), flat(gauge_value), flat(gauge_weight)
    )
    payload, pilot_index = tied(payload, pilot_index)
    got = lax.all_to_all(payload, PEER_AXES, 0, 0, tiled=True)
    spot, slots = kernel_call(
        pilot_body, (shape(nx // 4, LANES, dtype=jnp.int32), shape(peers, LANES))
    )(in_specs=[VMEM], out_specs=(VMEM, VMEM))(pilot_index)

    fixed = (conductivity, storage, state_field)
    got, spot, *fixed = tied(got, spot, *fixed)
    fixed_other = [swapped(x) for x in fixed]
    edge = shape(4, nz, HALO, LANES)
    source, up, down = kernel_call(
        functools.partial(source_body, capacity // LANES),
        (shape(nz, nx, LANES), edge, edge),
        weight=6,
    )(in_specs=[VMEM] * 4, out_specs=(VMEM,) * 3)(got, *fixed)
    forward, backward = neighbour_pairs("cols")
    low = lax.ppermute(up, "cols", forward)
    high = lax.ppermute(down, "cols", backward)
    other = swapped(source)

    mine = (*fixed, source)

    def packed(low_side):
        return kernel_call(
            functools.partial(pack_body, low_side), shape(2 * nz, HALO, LANES)
        )(in_specs=[SMEM] + [VMEM] * 6, out_specs=VMEM)(where, *mine, low, high)

    if row_count == 2:
        sides = [lax.ppermute(packed(None), "rows", [(0, 1), (1, 0)])]
    else:
        forward, backward = neighbour_pairs("rows")
        sides = [
            lax.ppermute(packed(False), "rows", forward),
            lax.ppermute(packed(True), "rows", backward),
        ]
    edges = [low, high, swapped(low), swapped(high)]
    sides = sides + [swapped(x) for x in sides]

    each = nx * ny // 8 // LANES
    planes, width = 2 * nz, nx + 2 * HALO
    padded = pltpu.VMEM((planes, width, 2 * LANES), f32)
    own, send = kernel_call(
        functools.partial(basis_body, peers, len(sides) // 2),
        (shape(ITERS, nz, nx, LANES), shape(devices, ITERS, LANES)),
        [padded] * 8
        + [
            pltpu.VMEM((ITERS + 1, planes, width, 2 * LANES), f32),
            pltpu.VMEM((6, nz, nx, LANES), f32),
        ],
        weight=10,
    )(in_specs=[SMEM] + [VMEM] * (14 + len(sides)), out_specs=(VMEM, VMEM))(
        where, *mine, *fixed_other, other, *edges, *sides, spot, slots
    )
    parts = lax.all_to_all(send, GRID_AXES, 0, 0, tiled=True)
    adjoint, pilot = kernel_call(
        functools.partial(solve_body, devices // peers), (shape(nz, nx, ny), shape(each, LANES))
    )(in_specs=[SMEM] + [VMEM] * 2, out_specs=(VMEM, VMEM))(where, parts, own)
    return adjoint, pilot.reshape(-1)


def solution(mesh):
    return jax.shard_map(
        on_device,
        mesh=mesh,
        in_specs=(
            P(("groups", "layers"), "cols", "rows"),
            P(("groups", "layers"), "cols", "rows"),
            P(("groups", "layers"), "cols", "rows"),
            P(("groups", "cols", "rows", "layers")),
            P(("groups", "cols", "rows", "layers")),
            P(("groups", "cols", "rows", "layers")),
            P(("groups", "cols", "rows", "layers")),
            P("cols", "rows"),
        ),
        out_specs=(P(("groups", "layers"), "cols", "rows"), P(("groups", "cols", "rows"))),
        check_vma=False,
    )
```

```python
import functools

import jax
import jax.numpy as jnp
from jax import lax
from jax.experimental import pallas as pl
from jax.experimental.pallas import tpu as pltpu
from jax.sharding import PartitionSpec as P

ITERS = 8
HALO = 8
FACTS = 64
SLOTS = 96
LANES = 128
LANE_BITS = 7
GRID_AXES = ("cols", "rows", "layers")
PEER_AXES = ("cols", "rows")
NT = (((1,), (1,)), ((), ()))
EXACT = lax.Precision.HIGHEST
VMEM_BYTES = 24 * 1024 * 1024


def kernel_call(body, out_shape, scratch=(), weight=1, vmem=VMEM_BYTES):
    return functools.partial(
        pl.pallas_call,
        body,
        out_shape=out_shape,
        scratch_shapes=list(scratch),
        compiler_params=pltpu.CompilerParams(vmem_limit_bytes=vmem),
        cost_estimate=pl.CostEstimate(
            flops=0, bytes_accessed=weight * 3_000_000, transcendentals=0
        ),
    )


VMEM = pl.BlockSpec(memory_space=pltpu.VMEM)
SMEM = pl.BlockSpec(memory_space=pltpu.SMEM)
HBM = pl.BlockSpec(memory_space=pltpu.HBM)


def pieces_of(x):
    first = x.astype(jnp.bfloat16).astype(jnp.float32)
    rest = x - first
    second = rest.astype(jnp.bfloat16).astype(jnp.float32)
    return first, second, rest - second


def row_iota(rows, lanes=LANES):
    return lax.broadcasted_iota(jnp.int32, (rows, lanes), 0)


def lane_iota(rows, lanes=LANES):
    return lax.broadcasted_iota(jnp.int32, (rows, lanes), 1)


def picked(mask, row):
    return jnp.where(mask, row, jnp.zeros_like(row)).astype(jnp.bfloat16)


TILE = 16


def spread16(x, r):
    return jnp.broadcast_to(x[r : r + 1], (TILE, LANES)).astype(jnp.bfloat16)


def hits16(count, row):
    at = row_iota(TILE).astype(jnp.float32).astype(jnp.bfloat16)
    return [at + jnp.bfloat16(TILE * i) == row for i in range(count // TILE)]


def filled16(masks, value):
    zero = jnp.zeros((TILE, LANES), jnp.bfloat16)
    return jnp.concatenate([jnp.where(m, value, zero) for m in masks], axis=0)


def mm(a, b, dims=(((1,), (0,)), ((), ())), precision=None):
    return lax.dot_general(a, b, dims, precision=precision, preferred_element_type=jnp.float32)


def ranks(owner, peers):
    rows = owner.shape[0]
    ra, ca = row_iota(LANES, 2 * LANES), lane_iota(LANES, 2 * LANES)
    earlier_lane = jnp.where((ra < ca) | (ca >= LANES), 1.0, 0.0).astype(jnp.bfloat16)
    earlier_row = jnp.where(row_iota(rows, rows) > lane_iota(rows, rows), 1.0, 0.0).astype(
        jnp.bfloat16
    )
    hits = [owner == peer for peer in range(peers)]
    ones = jnp.concatenate([jnp.where(h, 1.0, 0.0).astype(jnp.bfloat16) for h in hits], axis=0)
    counts = mm(ones, earlier_lane)
    part = [counts[p * rows : (p + 1) * rows] for p in range(peers)]
    before = mm(
        earlier_row, jnp.concatenate([c[:, LANES:] for c in part], axis=1).astype(jnp.bfloat16)
    )
    rank = jnp.zeros((rows, LANES), jnp.float32)
    for p in range(peers):
        rank = jnp.where(
            hits[p], part[p][:, :LANES] + before[:, p * LANES : (p + 1) * LANES], rank
        )
    return rank.astype(jnp.int32)


def route_body(
    peers, capacity, owner_hbm, cell_hbm, value_hbm, weight_hbm, out_ref,
    owner_ref, cell_ref, value_ref, weight_ref, sems,
):
    copies = [
        pltpu.make_async_copy(source, target, sems.at[i])
        for i, (source, target) in enumerate(
            (
                (owner_hbm, owner_ref),
                (cell_hbm, cell_ref),
                (value_hbm, value_ref),
                (weight_hbm, weight_ref),
            )
        )
    ]
    for copy in copies:
        copy.start()
    for copy in copies:
        copy.wait()
    rows = owner_ref.shape[0]
    owner = owner_ref[...]
    position = owner * capacity + ranks(owner, peers)
    slot_row = lax.shift_right_logical(position, LANE_BITS).astype(jnp.float32)
    slot_lane = (position & (LANES - 1)).astype(jnp.float32)
    cell = cell_ref[...]
    columns = [
        lax.shift_right_logical(cell, LANE_BITS).astype(jnp.float32),
        (cell & (LANES - 1)).astype(jnp.float32),
        *pieces_of(value_ref[...]),
        *pieces_of(weight_ref[...]),
    ]
    slot_rows = peers * capacity // LANES
    one = jnp.ones((TILE, LANES), jnp.bfloat16)
    total = None
    for start in range(0, rows, TILE):
        at_row, at_lane = [], [[] for _ in columns]
        for r in range(start, start + TILE):
            at_row.append(filled16(hits16(slot_rows, spread16(slot_row, r)), one))
            masks = hits16(LANES, spread16(slot_lane, r))
            for q, column in enumerate(columns):
                at_lane[q].append(filled16(masks, spread16(column, r)))
        at_lane = jnp.concatenate([jnp.concatenate(q, axis=1) for q in at_lane], axis=0)
        part = mm(at_lane, jnp.concatenate(at_row, axis=1), NT)
        total = part if total is None else total + part
    part = [total[q * LANES : (q + 1) * LANES] for q in range(len(columns))]
    fields = [
        part[0] * LANES + part[1],
        part[2] + part[3] + part[4],
        part[5] + part[6] + part[7],
    ]
    fields = [jnp.transpose(f) for f in fields]
    each = capacity // LANES
    for peer in range(peers):
        for q, field in enumerate(fields):
            out_ref[peer, q * each : (q + 1) * each, :] = field[peer * each : (peer + 1) * each]


def pilot_body(pilot_ref, spot_ref, slots_ref):
    peers = slots_ref.shape[0]
    blocks_x = pilot_ref.shape[0] // 4
    pilots = pilot_ref.shape[0] * pilot_ref.shape[1] // 8
    pilot = jnp.concatenate([pilot_ref[4 * r : 4 * r + 1, :] for r in range(blocks_x)], axis=0)
    owner = lax.div(pilot, jnp.int32(pilots))
    slot = pilot - owner * pilots
    first = (lane_iota(blocks_x) & 1) == 0
    owner = jnp.where(first, owner, -1)
    rank = ranks(owner, peers)
    spot_ref[...] = jnp.where(first, owner * LANES + rank, -1)
    left, high, low = [], [], []
    peer_at, lanes_at = row_iota(peers), row_iota(LANES)
    for r in range(blocks_x):
        left.append(jnp.where(peer_at == owner[r : r + 1], 1.0, 0.0).astype(jnp.bfloat16))
        hit = lanes_at == rank[r : r + 1]
        number = slot[r : r + 1]
        high.append(picked(hit, lax.shift_right_logical(number, LANE_BITS).astype(jnp.float32)))
        low.append(picked(hit, (number & (LANES - 1)).astype(jnp.float32)))
    left = jnp.concatenate(left, axis=1)
    slots_ref[...] = mm(left, jnp.concatenate(high, axis=1), NT) * LANES + mm(
        left, jnp.concatenate(low, axis=1), NT
    )


def source_body(
    each, got_ref, conductivity_ref, storage_ref, state_ref, out_ref, up_ref, down_ref
):
    peers = got_ref.shape[0]
    nz, nx = state_ref.shape[0], state_ref.shape[1]
    cells = nz * nx
    one = jnp.ones((TILE, LANES), jnp.bfloat16)

    def sixteen(group, q):
        peer, row = divmod(group * TILE, each)
        if each >= TILE:
            return got_ref[peer, q * each + row : q * each + row + TILE, :]
        return jnp.concatenate(
            [got_ref[peer + i, q * each : (q + 1) * each, :] for i in range(TILE // each)], axis=0
        )

    total = None
    for group in range(peers * each // TILE):
        cell = sixteen(group, 0).astype(jnp.int32)
        high = lax.shift_right_logical(cell, LANE_BITS)
        low = cell & (LANES - 1)
        heads = []
        for r in range(0, TILE, 8):
            head = jnp.zeros((8, LANES), jnp.float32)
            for z in range(nz):
                for x in range(nx):
                    line = jnp.broadcast_to(state_ref[z, x : x + 1, :], (8, LANES))
                    line = jnp.take_along_axis(line, low[r : r + 8], axis=1)
                    head = jnp.where(high[r : r + 8] == z * nx + x, line, head)
            heads.append(head)
        misfit = sixteen(group, 2) * (jnp.concatenate(heads, axis=0) - sixteen(group, 1))
        coarse = misfit.astype(jnp.bfloat16).astype(jnp.float32)
        pieces = (coarse, misfit - coarse)
        high, low = high.astype(jnp.float32), low.astype(jnp.float32)
        at_row, at_lane = [], [[] for _ in pieces]
        for r in range(TILE):
            at_row.append(filled16(hits16(cells, spread16(high, r)), one))
            masks = hits16(LANES, spread16(low, r))
            for q, piece in enumerate(pieces):
                at_lane[q].append(filled16(masks, spread16(piece, r)))
        at_lane = jnp.concatenate([jnp.concatenate(q, axis=1) for q in at_lane], axis=0)
        part = mm(at_lane, jnp.concatenate(at_row, axis=1), NT)
        total = part if total is None else total + part
    total = jnp.transpose(total[:LANES] + total[LANES:])
    out_ref[...] = total.reshape(nz, nx, LANES)
    for f, field in enumerate((conductivity_ref, storage_ref, state_ref, out_ref)):
        up_ref[f] = field[:, nx - HALO :, :]
        down_ref[f] = field[:, :HALO, :]


def all_sum(x):
    while x.ndim > 2:
        x = jnp.sum(x, axis=0)
    return jnp.sum(jnp.sum(x, axis=0, keepdims=True), axis=1, keepdims=True)


def safe_ratio(a, b):
    return jnp.where(b > 0.0, a / jnp.where(b > 0.0, b, 1.0), 0.0)


def pack_body(low_side, where_ref, *refs):
    *fields, low_ref, high_ref, out_ref = refs
    nz, nx = fields[0].shape[0], fields[0].shape[1]
    lanes = lane_iota(2 * (nx + 2 * HALO))
    tall = jnp.zeros(lanes.shape, jnp.float32)
    for pair in range(2):
        for z in range(nz):
            at = (pair * nz + z) * HALO
            x = jnp.concatenate(
                [
                    part
                    for f in (2 * pair, 2 * pair + 1)
                    for part in (low_ref[f, z], fields[f][z], high_ref[f, z])
                ],
                axis=0,
            )
            if low_side is None:
                shift = (at + jnp.where(where_ref[1] == 0, HALO, 0)) & (LANES - 1)
            else:
                shift = at if low_side else (at + HALO) & (LANES - 1)
            x = pltpu.roll(x, shift, 1)
            tall = jnp.where((lanes >= at) & (lanes < at + HALO), x, tall)
    rest = LANES - tall.shape[0]
    tall = jnp.concatenate([tall, jnp.zeros((rest, LANES), jnp.float32)], axis=0)
    out_ref[...] = jnp.transpose(tall).reshape(out_ref.shape)


def joined(a, b):
    return jnp.where((a > 0.0) & (b > 0.0), 0.5 * (a + b), 0.0)


def right(x):
    return pltpu.roll(x, x.shape[1] - 1, 1)


def left(x):
    return pltpu.roll(x, 1, 1)


def fore(x):
    return pltpu.roll(x, x.shape[0] - 1, 0)


def back(x):
    return pltpu.roll(x, 1, 0)


def unpack(layer, f, own, other, edges, padded, top=0):
    nz, nx = own.shape[0], own.shape[1]
    for half, block in ((0, own), (1, other)):
        low, high = edges[2 * half], edges[2 * half + 1]
        for i in range(nz):
            j = jnp.where(layer == 0, i, nz - 1 - i)
            to = half * nz + i
            padded[to, top : top + HALO, :] = low[f, j]
            padded[to, top + HALO : top + HALO + nx, :] = block[j]
            padded[to, top + HALO + nx : top + 2 * HALO + nx, :] = high[f, j]


def prepare_body(where_ref, *refs):
    own, other, edges = refs[:3], refs[3:6], refs[6:10]
    c_pad, diag, wx, wx_back, wy, wz, grads, outer, s_pad, h_pad = refs[10:]
    layer = where_ref[0]
    nz, nx = own[0].shape[0], own[0].shape[1]
    planes, width = c_pad.shape[0], c_pad.shape[1]
    for f, target in enumerate((c_pad, s_pad, h_pad)):
        unpack(layer, f, own[f], other[f], edges, target)
    lanes = lane_iota(width)
    last = lanes == LANES - 1
    for z in range(planes):
        c = c_pad[z]
        cf, cr = fore(c), jnp.where(last, 0.0, right(c))
        total = cf + back(c) + cr + jnp.where(lanes == 0, 0.0, left(c))
        wx[z] = joined(c, cf)
        wx_back[z] = joined(c, back(c))
        wy[z] = joined(c, cr)
        if z + 1 < planes:
            wz[z] = joined(c, c_pad[z + 1])
            total = total + c_pad[z + 1]
        if z:
            total = total + c_pad[z - 1]
        diag[z] = s_pad[z] + 3.0 * c + 0.5 * total

    span = HALO + nx
    rows, lanes = row_iota(width), lane_iota(width)
    mine = (rows >= HALO) & (rows < span)
    before = (rows >= HALO - 1) & (rows < span - 1)
    odd = (lanes & 1) == 1
    inside = mine & (lanes < LANES - 1)

    def kept(mask, x):
        return jnp.where(mask, x, 0.0)[:span]

    for z in range(nz):
        c, h = -0.5 * c_pad[z], h_pad[z]
        fall = h - fore(h)
        grads[0, z] = kept(mine, c * fall)
        grads[1, z] = kept(before, fore(c) * fall)
        fall = h - right(h)
        following = right(c) * fall
        grads[2, z] = kept(inside, c * fall + jnp.where(odd, 0.0, following))
        grads[3, z] = kept(inside & odd, following)
        weight = c + -0.5 * c_pad[z + 1] if z + 1 < nz else c
        grads[4, z] = kept(mine, weight * (h - h_pad[z + 1]))
        grads[5, z] = kept(mine & ((lanes == 0) | (lanes == LANES - 1)), c * h)
    outer[...] = kept(mine, -0.5 * c_pad[0] * h_pad[0])


def basis_body(peers, side_count, where_ref, *refs):
    c_pad, diag_in, wx, wx_back, wy, wz, grads, outer = refs[:8]
    b_own, b_other, edges, refs = refs[8], refs[9], refs[10:14], refs[14:]
    sides = list(zip(refs[:side_count], refs[side_count : 2 * side_count]))
    spot_ref, slots_ref, own_ref, send_ref = refs[2 * side_count : 2 * side_count + 4]
    diag, ws, edge_grads, image, basis = refs[2 * side_count + 4 :]
    layer, row = where_ref[0], where_ref[1]
    nz, nx = b_own.shape[0], b_own.shape[1]
    planes, width = c_pad.shape[0], c_pad.shape[1]
    span = HALO + nx
    inner = slice(HALO, span)
    top = HALO
    body = slice(top, top + width)
    for k in range(ITERS):
        for z in range(planes):
            basis[k, z, :top, :] = jnp.zeros((top, LANES), jnp.float32)
            basis[k, z, top + width :, :] = jnp.zeros((top, LANES), jnp.float32)
    unpack(layer, 3, b_own, b_other, edges, basis.at[0], top)

    lanes, rows = lane_iota(width), row_iota(width)
    y_at = lanes & (HALO - 1)
    if side_count == 1:
        meetings = [(jnp.where(row == 0, LANES - 1, 0), jnp.where(row == 0, 0, HALO - 1))]
    else:
        meetings = [(0, HALO - 1), (LANES - 1, 0)]
    strips = []
    for (here, there), (edge, meet) in zip(sides, meetings):
        halves = [jnp.transpose(x[...].reshape(LANES, LANES)) for x in (here, there)]
        first = jnp.where(layer == 0, halves[0], halves[1])
        second = jnp.where(layer == 0, halves[1], halves[0])
        fields = []
        for f in range(4):
            part = slice((f % 2) * width, (f % 2 + 1) * width)
            half = LANES // 2
            fields.append(
                jnp.where(
                    lanes < half,
                    pltpu.roll(first[part], half, 1) if f // 2 else first[part],
                    second[part] if f // 2 else pltpu.roll(second[part], half, 1),
                )
            )
        shifts = []
        for z in range(planes):
            spot = jnp.where(layer == 0, z, planes - 1 - z) * HALO + meet
            shifts.append(
                ((edge - spot) & (LANES - 1), (spot - edge) & (LANES - 1))
            )
        strips.append((fields, lanes == edge, shifts))

    def from_strips(values, z):
        total = jnp.zeros((width, LANES), jnp.float32)
        for (_, at_edge, shifts), value in zip(strips, values):
            total = jnp.where(at_edge, pltpu.roll(value, shifts[z][0], 1), total)
        return total

    def to_strip(strip, value, z):
        _, at_edge, shifts = strip
        if side_count > 1:
            value = jnp.where(at_edge, value, 0.0)
        return pltpu.roll(value, shifts[z][1], 1)

    edge_c = [jnp.zeros((width, LANES), jnp.float32) for _ in strips]
    mine = (rows >= HALO) & (rows < span)
    for z in range(planes):
        c = c_pad[z]
        c_side = from_strips([s[0][0] for s in strips], z)
        ws[z] = joined(c, c_side)
        diag[z] = diag_in[z] + 0.5 * c_side
        for i, strip in enumerate(strips):
            edge_c[i] = edge_c[i] + to_strip(strip, jnp.where(strip[1], c, 0.0), z)
        if z < nz:
            h_side = from_strips([s[0][2] for s in strips], z)
            edge_grads[z] = grads[5, z] + jnp.where(mine, 0.5 * c * h_side, 0.0)[:span]
    strip_terms = []
    for (fields, _, _), beside in zip(strips, edge_c):
        c = fields[0]
        cf = fore(c)
        cr = jnp.where(y_at < HALO - 1, right(c), 0.0)
        cu = jnp.where(lanes < LANES - HALO, pltpu.roll(c, LANES - HALO, 1), 0.0)
        total = cf + back(c) + cr + cu + beside
        total = total + jnp.where(y_at > 0, left(c), 0.0)
        total = total + jnp.where(lanes >= HALO, pltpu.roll(c, HALO, 1), 0.0)
        strip_terms.append(
            (fields[1] + 3.0 * c + 0.5 * total, joined(c, cf), joined(c, cr), joined(c, cu))
        )

    alphas, gammas, norms, sums = [], [], [], []

    def following(k, image_now, now, before):
        u = image_now - alphas[k - 1] * now
        return u - gammas[k - 1] * before if k > 1 else u

    def member(k, z):
        before = basis[k - 2, z, body, :] if k > 1 else None
        u = following(k, image[z], basis[k - 1, z, body, :], before)
        basis[k, z, body, :] = u
        return u

    def folded(x):
        return sum(x[r : r + 8] for r in range(8, width, 8)) + x[:8]

    side_now = [s[0][3] for s in strips]
    side_last, side_image = None, None
    for k in range(ITERS):
        above = member(k, 0) if k else basis[0, 0, body, :]
        v = None
        if k:
            side_next = [
                following(k, side_image[i], side_now[i], side_last[i] if k > 1 else None)
                for i in range(side_count)
            ]
            side_now, side_last = side_next, side_now
        norm = jnp.zeros((8, LANES), jnp.float32)
        energy = jnp.zeros((8, LANES), jnp.float32)
        side_image = []
        for x, (d, sx, sy, sz) in zip(side_now, strip_terms):
            ax = d * x - sx * fore(x) - back(sx * x) - sy * right(x) - left(sy * x)
            ax = ax - sz * pltpu.roll(x, LANES - HALO, 1) - pltpu.roll(sz * x, HALO, 1)
            side_image.append(ax)
        acc = basis[k, 0, top : top + span, :] * outer[...]
        acc_x = jnp.zeros((span, LANES), jnp.float32)
        acc_y = jnp.zeros((span, LANES), jnp.float32)
        for z in range(nz + ITERS - 1 - k):
            below, v = v, above
            above = member(k, z + 1) if k else basis[0, z + 1, body, :]
            side = from_strips(side_now, z)
            vf, vr = basis[k, z, top + 1 : top + 1 + width, :], right(v)
            vb = basis[k, z, top - 1 : top - 1 + width, :]
            wyz, wsz = wy[z], ws[z]
            av = diag[z] * v - wz[z] * above
            if z:
                av = av - wz[z - 1] * below
            av = av - wx[z] * vf - wx_back[z] * vb - wyz * vr - left(wyz * v) - wsz * side
            image[z] = av
            edge = wsz * v
            for i, strip in enumerate(strips):
                side_image[i] = side_image[i] - to_strip(strip, edge, z)
            norm = norm + folded(v * v)
            energy = energy + folded(v * av)
            if z < nz:
                fall = (v - vf)[:span]
                acc = acc + fall * grads[0, z]
                acc_x = acc_x + fall * grads[1, z]
                fall = (v - vr)[:span]
                acc = acc + fall * grads[2, z]
                acc_y = acc_y + fall * grads[3, z]
                acc = acc + (v - above)[:span] * grads[4, z]
                acc = acc + (v - side)[:span] * edge_grads[z]
                own_ref[k, jnp.where(layer == 0, z, nz - 1 - z)] = v[inner]
        for x, ax in zip(side_now, side_image):
            norm = norm + folded(x * x)
            energy = energy + folded(x * ax)
        sums.append((acc + back(acc_x) + left(acc_y))[inner])
        norm = all_sum(norm)
        alphas.append(safe_ratio(all_sum(energy), norm))
        gammas.append(safe_ratio(norm, norms[-1]) if k else jnp.zeros_like(norm))
        norms.append(norm)
    for z in range(nz):
        member(ITERS, z)
    own_rows = slice(top + HALO, top + span)

    dots = {}
    for i in range(ITERS + 1):
        for j in range(i + 1):
            acc = basis[i, 0, own_rows, :] * basis[j, 0, own_rows, :]
            for z in range(1, nz):
                acc = acc + basis[i, z, own_rows, :] * basis[j, z, own_rows, :]
            dots[i, j] = dots[j, i] = all_sum(acc)

    def operator(i, j):
        entry = dots[i, j + 1] + alphas[j] * dots[i, j]
        return entry + gammas[j] * dots[i, j - 1] if j else entry

    lanes = lane_iota(1)
    facts = []
    for j in range(ITERS):
        row_facts = [0.5 * (operator(j, m) + operator(m, j)) for m in range(ITERS)]
        row_facts += [alphas[j], gammas[j], norms[j], dots[j, 0]]
        entries = jnp.zeros((1, LANES), jnp.float32)
        for place, entry in enumerate(row_facts):
            entries = jnp.where(lanes == FACTS + place, entry, entries)
        facts.append(entries)

    blocks_x = nx // 4
    four = jnp.where(
        lax.shift_right_logical(lane_iota(blocks_x, nx), 2) == row_iota(blocks_x, nx), 1.0, 0.0
    )
    sums = mm(four, jnp.concatenate(sums, axis=1), precision=EXACT)
    spot = [spot_ref[r : r + 1, :] for r in range(blocks_x)]
    lane_hits = jnp.concatenate(
        [
            jnp.where(row_iota(LANES) == (p & (LANES - 1)), 1.0, 0.0).astype(jnp.bfloat16)
            for p in spot
        ],
        axis=1,
    )
    peer_at = row_iota(peers)
    row_hit = [(p >= 0) & (peer_at == lax.shift_right_arithmetic(p, LANE_BITS)) for p in spot]
    values = []
    for k in range(ITERS):
        pair = sums[:, k * LANES : (k + 1) * LANES]
        pair = pair + pltpu.roll(pair, LANES - 1, 1)
        for p in pieces_of(pair):
            values.append(
                jnp.concatenate(
                    [picked(row_hit[r], p[r : r + 1]) for r in range(blocks_x)], axis=1
                )
            )
    dense = mm(jnp.concatenate(values, axis=0), lane_hits, NT)
    copies = send_ref.shape[0] // peers
    for k in range(ITERS):
        at = 3 * k * peers
        rows = dense[at : at + peers] + dense[at + peers : at + 2 * peers]
        rows = rows + dense[at + 2 * peers : at + 3 * peers]
        rows = jnp.where(lane_iota(peers) < FACTS, rows, facts[k])
        if k < 2:
            slots = pltpu.roll(slots_ref[...], (1 - k) * (LANES - SLOTS) + FACTS, 1)
            rows = jnp.where(lane_iota(peers) < SLOTS, rows, slots)
        for peer in range(peers):
            for copy in range(copies):
                send_ref[peer * copies + copy, k : k + 1, :] = rows[peer : peer + 1]


def solve_body(copies, where_ref, got_ref, own_ref, adjoint_ref, pilot_ref):
    senders = got_ref.shape[0]
    peers = senders // copies
    groups = senders * ITERS // LANES
    got = got_ref[...].reshape(groups, LANES, LANES)
    turned = [jnp.transpose(got[g])[FACTS:SLOTS] for g in range(groups)]

    def fact(place):
        return jnp.concatenate([t[place : place + 1] for t in turned], axis=0)

    alpha, gamma, weight, rhs = (fact(ITERS + place) for place in range(4))
    at = lane_iota(groups) & (ITERS - 1)
    gamma_next = jnp.where(at < ITERS - 1, pltpu.roll(gamma, LANES - 1, 1), 0.0)

    now = jnp.where(at == 0, 1.0, 0.0)
    last, norm_last = None, None
    common = []
    for k in range(ITERS):
        common.append(now)
        if k == ITERS - 1:
            break
        image = jnp.where(at > 0, pltpu.roll(now, 1, 1), 0.0) + alpha * now
        image = image + gamma_next * pltpu.roll(now, LANES - 1, 1)
        norm = all_sum(weight * now * now)
        following = image - safe_ratio(all_sum(weight * now * image), norm) * now
        if k:
            following = following - safe_ratio(norm, norm_last) * last
        now, last, norm_last = following, now, norm

    lanes = lane_iota(ITERS)
    system = jnp.zeros((ITERS, LANES), jnp.float32)
    stacked = []
    per = LANES // ITERS
    for g in range(groups):
        t = jnp.concatenate([c[g : g + 1] for c in common], axis=0)
        stacked.append(t)
        blocks = []
        for i in range(per):
            block = pltpu.roll(got_ref[g * per + i], (ITERS * i - FACTS) % LANES, 1)
            blocks.append(
                jnp.where((lanes >= ITERS * i) & (lanes < ITERS * (i + 1)), block, 0.0)
            )
        image = mm(t, jnp.concatenate(blocks, axis=0), precision=EXACT)
        beside = jnp.concatenate(
            [image, rhs[g : g + 1], jnp.zeros((LANES - ITERS - 1, LANES), jnp.float32)], axis=0
        )
        system = system + mm(t, beside, NT, precision=EXACT)
    rows = row_iota(ITERS)
    for p in range(ITERS):
        pivot = system[p : p + 1, p : p + 1]
        inverse = jnp.where(pivot > 0.0, 1.0 / jnp.where(pivot > 0.0, pivot, 1.0), 0.0)
        pivot_row = system[p : p + 1] * inverse
        system = jnp.where(rows == p, pivot_row, system - system[:, p : p + 1] * pivot_row)
    answer = system[:, ITERS : ITERS + 1]

    weights = [jnp.sum(answer * t, axis=0, keepdims=True) for t in stacked]
    me = where_ref[3]
    mine = []
    for k in range(ITERS):
        w = jnp.zeros((1, 1), jnp.float32)
        for g in range(groups):
            hit = lane_iota(1) == me * ITERS + k - g * LANES
            w = w + jnp.sum(jnp.where(hit, weights[g], 0.0), axis=1, keepdims=True)
        mine.append(w)
    for z in range(own_ref.shape[1]):
        acc = mine[0] * own_ref[0, z]
        for k in range(1, ITERS):
            acc = acc + mine[k] * own_ref[k, z]
        adjoint_ref[z] = acc

    per_group = LANES // ITERS // copies
    sender = lax.div(lane_iota(per_group), jnp.int32(ITERS * copies))
    values = jnp.concatenate(
        [
            mm(jnp.where(sender == row_iota(per_group), weights[g], 0.0), got[g], precision=EXACT)
            for g in range(groups)
        ],
        axis=0,
    )
    rows_at, lanes_at = row_iota(pilot_ref.shape[0]), row_iota(LANES)
    held = lane_iota(peers) < pilot_ref.shape[0] * LANES // peers
    pieces = pieces_of(jnp.where(held, values, 0.0))
    left, right = [[], [], []], []
    room = LANES - SLOTS
    for s in range(peers):
        slot = jnp.where(
            lane_iota(1) < room,
            pltpu.roll(got_ref[s * copies, 0:1, :], room, 1),
            pltpu.roll(got_ref[s * copies, 1:2, :], 2 * room, 1),
        ).astype(jnp.int32)
        hit = rows_at == lax.shift_right_logical(slot, LANE_BITS)
        for q, piece in enumerate(pieces):
            left[q].append(picked(hit, piece[s : s + 1]))
        right.append(
            jnp.where(lanes_at == (slot & (LANES - 1)), 1.0, 0.0).astype(jnp.bfloat16)
        )
    right = jnp.concatenate(right, axis=1)
    pilot_ref[...] = sum(mm(jnp.concatenate(q, axis=1), right, NT) for q in left)


def tied(*values):
    return lax.optimization_barrier(values)


def neighbour_pairs(axis):
    forward = [(i, i + 1) for i in range(lax.axis_size(axis) - 1)]
    return forward, [(b, a) for a, b in forward]


def swapped(x):
    return lax.ppermute(x, "layers", [(0, 1), (1, 0)])


def on_device(
    state_field,
    conductivity,
    storage,
    gauge_owner,
    gauge_cell,
    gauge_value,
    gauge_weight,
    pilot_index,
):
    nz, nx, ny = state_field.shape
    peers = lax.axis_size("cols") * lax.axis_size("rows")
    devices = peers * lax.axis_size("layers")
    gauges = gauge_owner.shape[0]
    capacity = 4 * gauges // peers
    f32 = jnp.float32
    row_count = lax.axis_size("rows")

    def shape(*dims, dtype=f32):
        return jax.ShapeDtypeStruct(dims, dtype)

    def flat(x):
        return x.reshape(gauges // LANES, LANES)

    where = jnp.stack(
        [lax.axis_index(a) for a in ("layers", "rows", "cols", GRID_AXES)]
    ).astype(jnp.int32)

    obs = pltpu.VMEM((gauges // LANES, LANES), f32)
    obs_int = pltpu.VMEM((gauges // LANES, LANES), jnp.int32)
    payload = kernel_call(
        functools.partial(route_body, peers, capacity),
        shape(peers, 3 * capacity // LANES, LANES),
        [obs_int, obs_int, obs, obs, pltpu.SemaphoreType.DMA((4,))],
        weight=5,
        vmem=64 * 1024 * 1024,
    )(in_specs=[HBM] * 4, out_specs=VMEM)(
        flat(gauge_owner), flat(gauge_cell), flat(gauge_value), flat(gauge_weight)
    )
    payload, pilot_index = tied(payload, pilot_index)
    got = lax.all_to_all(payload, PEER_AXES, 0, 0, tiled=True)
    spot, slots = kernel_call(
        pilot_body, (shape(nx // 4, LANES, dtype=jnp.int32), shape(peers, LANES))
    )(in_specs=[VMEM], out_specs=(VMEM, VMEM))(pilot_index)

    fixed = (conductivity, storage, state_field)
    got, spot, *fixed_other = tied(got, spot, *(swapped(x) for x in fixed))
    edge = shape(4, nz, HALO, LANES)
    source, up, down = kernel_call(
        functools.partial(source_body, capacity // LANES),
        (shape(nz, nx, LANES), edge, edge),
        weight=6,
    )(in_specs=[VMEM] * 4, out_specs=(VMEM,) * 3)(got, *fixed)
    forward, backward = neighbour_pairs("cols")
    low = lax.ppermute(up, "cols", forward)
    high = lax.ppermute(down, "cols", backward)
    other = swapped(source)

    def packed(low_side):
        return kernel_call(
            functools.partial(pack_body, low_side), shape(2 * nz, HALO, LANES)
        )(in_specs=[SMEM] + [VMEM] * 6, out_specs=VMEM)(where, *fixed, source, low, high)

    if row_count == 2:
        send = [(packed(None), [(0, 1), (1, 0)])]
    else:
        forward, backward = neighbour_pairs("rows")
        send = [(packed(False), forward), (packed(True), backward)]
    edges = tied(low, high, swapped(low), swapped(high), *(x for x, _ in send))[:4]
    sides = [lax.ppermute(x, "rows", pairs) for x, pairs in send]
    planes, width, span = 2 * nz, nx + 2 * HALO, nx + HALO
    padded = (planes, width, LANES)
    prepared = kernel_call(
        prepare_body,
        (*(shape(*padded) for _ in range(6)), shape(6, nz, span, LANES), shape(span, LANES)),
        [pltpu.VMEM(padded, f32)] * 2,
        weight=3,
    )(in_specs=[SMEM] + [VMEM] * 10, out_specs=(VMEM,) * 8)(where, *fixed, *fixed_other, *edges)
    *sides, prepared = tied(*sides, prepared)
    sides = sides + [swapped(x) for x in sides]

    each = nx * ny // 8 // LANES
    own, send = kernel_call(
        functools.partial(basis_body, peers, len(sides) // 2),
        (shape(ITERS, nz, nx, LANES), shape(devices, ITERS, LANES)),
        [
            pltpu.VMEM(padded, f32),
            pltpu.VMEM(padded, f32),
            pltpu.VMEM((nz, span, LANES), f32),
            pltpu.VMEM(padded, f32),
            pltpu.VMEM((ITERS + 1, planes, width + 2 * HALO, LANES), f32),
        ],
        weight=10,
    )(in_specs=[SMEM] + [VMEM] * (16 + len(sides)), out_specs=(VMEM, VMEM))(
        where, *prepared, source, other, *edges, *sides, spot, slots
    )
    parts = lax.all_to_all(send, GRID_AXES, 0, 0, tiled=True)
    adjoint, pilot = kernel_call(
        functools.partial(solve_body, devices // peers), (shape(nz, nx, ny), shape(each, LANES))
    )(in_specs=[SMEM] + [VMEM] * 2, out_specs=(VMEM, VMEM))(where, parts, own)
    return adjoint, pilot.reshape(-1)


def solution(mesh):
    return jax.shard_map(
        on_device,
        mesh=mesh,
        in_specs=(
            P(("groups", "layers"), "cols", "rows"),
            P(("groups", "layers"), "cols", "rows"),
            P(("groups", "layers"), "cols", "rows"),
            P(("groups", "cols", "rows", "layers")),
            P(("groups", "cols", "rows", "layers")),
            P(("groups", "cols", "rows", "layers")),
            P(("groups", "cols", "rows", "layers")),
            P("cols", "rows"),
        ),
        out_specs=(P(("groups", "layers"), "cols", "rows"), P(("groups", "cols", "rows"))),
        check_vma=False,
    )
```

```python
import functools

import jax
import jax.numpy as jnp
from jax import lax
from jax.experimental import pallas as pl
from jax.experimental.pallas import tpu as pltpu
from jax.sharding import PartitionSpec as P

ITERS = 8
HALO = 8
FACTS = 64
SLOTS = 96
LANES = 128
LANE_BITS = 7
GRID_AXES = ("cols", "rows", "layers")
PEER_AXES = ("cols", "rows")
NT = (((1,), (1,)), ((), ()))
EXACT = lax.Precision.HIGHEST
VMEM_BYTES = 24 * 1024 * 1024


def kernel_call(body, out_shape, scratch=(), weight=1, vmem=VMEM_BYTES):
    return functools.partial(
        pl.pallas_call,
        body,
        out_shape=out_shape,
        scratch_shapes=list(scratch),
        compiler_params=pltpu.CompilerParams(vmem_limit_bytes=vmem),
        cost_estimate=pl.CostEstimate(
            flops=0, bytes_accessed=weight * 3_000_000, transcendentals=0
        ),
    )


VMEM = pl.BlockSpec(memory_space=pltpu.VMEM)
HBM = pl.BlockSpec(memory_space=pltpu.HBM)


def pieces_of(x):
    first = x.astype(jnp.bfloat16).astype(jnp.float32)
    rest = x - first
    second = rest.astype(jnp.bfloat16).astype(jnp.float32)
    return first, second, rest - second


def row_iota(rows, lanes=LANES):
    return lax.broadcasted_iota(jnp.int32, (rows, lanes), 0)


def lane_iota(rows, lanes=LANES):
    return lax.broadcasted_iota(jnp.int32, (rows, lanes), 1)


def picked(mask, row):
    return jnp.where(mask, row, jnp.zeros_like(row)).astype(jnp.bfloat16)


TILE = 16


def spread16(x, r):
    return jnp.broadcast_to(x[r : r + 1], (TILE, LANES)).astype(jnp.bfloat16)


def hits16(count, row):
    at = row_iota(TILE).astype(jnp.float32).astype(jnp.bfloat16)
    return [at + jnp.bfloat16(TILE * i) == row for i in range(count // TILE)]


def filled16(masks, value):
    zero = jnp.zeros((TILE, LANES), jnp.bfloat16)
    return jnp.concatenate([jnp.where(m, value, zero) for m in masks], axis=0)


def mm(a, b, dims=(((1,), (0,)), ((), ())), precision=None):
    return lax.dot_general(a, b, dims, precision=precision, preferred_element_type=jnp.float32)


def ranks(owner, peers):
    rows = owner.shape[0]
    ra, ca = row_iota(LANES, 2 * LANES), lane_iota(LANES, 2 * LANES)
    earlier_lane = jnp.where((ra < ca) | (ca >= LANES), 1.0, 0.0).astype(jnp.bfloat16)
    earlier_row = jnp.where(row_iota(rows, rows) > lane_iota(rows, rows), 1.0, 0.0).astype(
        jnp.bfloat16
    )
    hits = [owner == peer for peer in range(peers)]
    ones = jnp.concatenate([jnp.where(h, 1.0, 0.0).astype(jnp.bfloat16) for h in hits], axis=0)
    counts = mm(ones, earlier_lane)
    part = [counts[p * rows : (p + 1) * rows] for p in range(peers)]
    before = mm(
        earlier_row, jnp.concatenate([c[:, LANES:] for c in part], axis=1).astype(jnp.bfloat16)
    )
    rank = jnp.zeros((rows, LANES), jnp.float32)
    for p in range(peers):
        rank = jnp.where(
            hits[p], part[p][:, :LANES] + before[:, p * LANES : (p + 1) * LANES], rank
        )
    return rank.astype(jnp.int32)


def route_body(
    peers, capacity, owner_hbm, cell_hbm, value_hbm, weight_hbm, out_ref,
    owner_ref, cell_ref, value_ref, weight_ref, sems,
):
    copies = [
        pltpu.make_async_copy(source, target, sems.at[i])
        for i, (source, target) in enumerate(
            (
                (owner_hbm, owner_ref),
                (cell_hbm, cell_ref),
                (value_hbm, value_ref),
                (weight_hbm, weight_ref),
            )
        )
    ]
    for copy in copies:
        copy.start()
    for copy in copies:
        copy.wait()
    rows = owner_ref.shape[0]
    owner = owner_ref[...]
    position = owner * capacity + ranks(owner, peers)
    slot_row = lax.shift_right_logical(position, LANE_BITS).astype(jnp.float32)
    slot_lane = (position & (LANES - 1)).astype(jnp.float32)
    cell = cell_ref[...]
    columns = [
        lax.shift_right_logical(cell, LANE_BITS).astype(jnp.float32),
        (cell & (LANES - 1)).astype(jnp.float32),
        *pieces_of(value_ref[...]),
        *pieces_of(weight_ref[...]),
    ]
    slot_rows = peers * capacity // LANES
    one = jnp.ones((TILE, LANES), jnp.bfloat16)
    total = None
    for start in range(0, rows, TILE):
        at_row, at_lane = [], [[] for _ in columns]
        for r in range(start, start + TILE):
            at_row.append(filled16(hits16(slot_rows, spread16(slot_row, r)), one))
            masks = hits16(LANES, spread16(slot_lane, r))
            for q, column in enumerate(columns):
                at_lane[q].append(filled16(masks, spread16(column, r)))
        at_lane = jnp.concatenate([jnp.concatenate(q, axis=1) for q in at_lane], axis=0)
        part = mm(at_lane, jnp.concatenate(at_row, axis=1), NT)
        total = part if total is None else total + part
    part = [total[q * LANES : (q + 1) * LANES] for q in range(len(columns))]
    fields = [
        part[0] * LANES + part[1],
        part[2] + part[3] + part[4],
        part[5] + part[6] + part[7],
    ]
    fields = [jnp.transpose(f) for f in fields]
    each = capacity // LANES
    for peer in range(peers):
        for q, field in enumerate(fields):
            out_ref[peer, q * each : (q + 1) * each, :] = field[peer * each : (peer + 1) * each]


def pilot_body(pilot_ref, spot_ref, slots_ref):
    peers = slots_ref.shape[0]
    blocks_x = pilot_ref.shape[0] // 4
    pilots = pilot_ref.shape[0] * pilot_ref.shape[1] // 8
    pilot = jnp.concatenate([pilot_ref[4 * r : 4 * r + 1, :] for r in range(blocks_x)], axis=0)
    owner = lax.div(pilot, jnp.int32(pilots))
    slot = pilot - owner * pilots
    first = (lane_iota(blocks_x) & 1) == 0
    owner = jnp.where(first, owner, -1)
    rank = ranks(owner, peers)
    spot_ref[...] = jnp.where(first, owner * LANES + rank, -1)
    left, high, low = [], [], []
    peer_at, lanes_at = row_iota(peers), row_iota(LANES)
    for r in range(blocks_x):
        left.append(jnp.where(peer_at == owner[r : r + 1], 1.0, 0.0).astype(jnp.bfloat16))
        hit = lanes_at == rank[r : r + 1]
        number = slot[r : r + 1]
        high.append(picked(hit, lax.shift_right_logical(number, LANE_BITS).astype(jnp.float32)))
        low.append(picked(hit, (number & (LANES - 1)).astype(jnp.float32)))
    left = jnp.concatenate(left, axis=1)
    slots_ref[...] = mm(left, jnp.concatenate(high, axis=1), NT) * LANES + mm(
        left, jnp.concatenate(low, axis=1), NT
    )


def source_body(
    each, got_ref, conductivity_ref, storage_ref, state_ref, out_ref, near_ref, far_ref
):
    peers = got_ref.shape[0]
    nz, nx = state_ref.shape[0], state_ref.shape[1]
    cells = nz * nx
    one = jnp.ones((TILE, LANES), jnp.bfloat16)

    def sixteen(group, q):
        peer, row = divmod(group * TILE, each)
        if each >= TILE:
            return got_ref[peer, q * each + row : q * each + row + TILE, :]
        return jnp.concatenate(
            [got_ref[peer + i, q * each : (q + 1) * each, :] for i in range(TILE // each)], axis=0
        )

    total = None
    for group in range(peers * each // TILE):
        cell = sixteen(group, 0).astype(jnp.int32)
        high = lax.shift_right_logical(cell, LANE_BITS)
        low = cell & (LANES - 1)
        heads = []
        for r in range(0, TILE, 8):
            head = jnp.zeros((8, LANES), jnp.float32)
            for z in range(nz):
                for x in range(nx):
                    line = jnp.broadcast_to(state_ref[z, x : x + 1, :], (8, LANES))
                    line = jnp.take_along_axis(line, low[r : r + 8], axis=1)
                    head = jnp.where(high[r : r + 8] == z * nx + x, line, head)
            heads.append(head)
        misfit = sixteen(group, 2) * (jnp.concatenate(heads, axis=0) - sixteen(group, 1))
        coarse = misfit.astype(jnp.bfloat16).astype(jnp.float32)
        pieces = (coarse, misfit - coarse)
        high, low = high.astype(jnp.float32), low.astype(jnp.float32)
        at_row, at_lane = [], [[] for _ in pieces]
        for r in range(TILE):
            at_row.append(filled16(hits16(cells, spread16(high, r)), one))
            masks = hits16(LANES, spread16(low, r))
            for q, piece in enumerate(pieces):
                at_lane[q].append(filled16(masks, spread16(piece, r)))
        at_lane = jnp.concatenate([jnp.concatenate(q, axis=1) for q in at_lane], axis=0)
        part = mm(at_lane, jnp.concatenate(at_row, axis=1), NT)
        total = part if total is None else total + part
    total = jnp.transpose(total[:LANES] + total[LANES:])
    out_ref[...] = total.reshape(nz, nx, LANES)
    even = (lax.axis_index("cols") & 1) == 0
    total = total.reshape(nz, nx, LANES)
    for f, field in enumerate((conductivity_ref, storage_ref, state_ref, total)):
        low, high = field[:, :HALO, :], field[:, nx - HALO :, :]
        near_ref[f] = jnp.where(even, high, low)
        far_ref[f] = jnp.where(even, low, high)


def all_sum(x):
    while x.ndim > 2:
        x = jnp.sum(x, axis=0)
    return jnp.sum(jnp.sum(x, axis=0, keepdims=True), axis=1, keepdims=True)


def safe_ratio(a, b):
    return jnp.where(b > 0.0, a / jnp.where(b > 0.0, b, 1.0), 0.0)


def pack_body(low_side, *refs):
    *fields, near_ref, far_ref, out_ref = refs
    even = (lax.axis_index("cols") & 1) == 0
    nz, nx = fields[0].shape[0], fields[0].shape[1]
    lanes = lane_iota(2 * (nx + 2 * HALO))
    tall = jnp.zeros(lanes.shape, jnp.float32)
    for pair in range(2):
        for z in range(nz):
            at = (pair * nz + z) * HALO
            x = jnp.concatenate(
                [
                    part
                    for f in (2 * pair, 2 * pair + 1)
                    for part in (
                        jnp.where(even, far_ref[f, z], near_ref[f, z]),
                        fields[f][z],
                        jnp.where(even, near_ref[f, z], far_ref[f, z]),
                    )
                ],
                axis=0,
            )
            if low_side is None:
                shift = (at + jnp.where(lax.axis_index("rows") == 0, HALO, 0)) & (LANES - 1)
            else:
                shift = at if low_side else (at + HALO) & (LANES - 1)
            x = pltpu.roll(x, shift, 1)
            tall = jnp.where((lanes >= at) & (lanes < at + HALO), x, tall)
    rest = LANES - tall.shape[0]
    tall = jnp.concatenate([tall, jnp.zeros((rest, LANES), jnp.float32)], axis=0)
    out_ref[...] = jnp.transpose(tall).reshape(out_ref.shape)


def joined(a, b):
    return jnp.where((a > 0.0) & (b > 0.0), 0.5 * (a + b), 0.0)


def right(x):
    return pltpu.roll(x, x.shape[1] - 1, 1)


def left(x):
    return pltpu.roll(x, 1, 1)


def fore(x):
    return pltpu.roll(x, x.shape[0] - 1, 0)


def back(x):
    return pltpu.roll(x, 1, 0)


def unpack(f, own, other, edges, padded, top=0):
    nz, nx = own.shape[0], own.shape[1]
    layer, even = lax.axis_index("layers"), (lax.axis_index("cols") & 1) == 0
    after = pl.multiple_of(jnp.where(even, top + HALO + nx, top), HALO)
    before = pl.multiple_of(jnp.where(even, top, top + HALO + nx), HALO)
    for half, block in ((0, own), (1, other)):
        near, far = edges[2 * half], edges[2 * half + 1]
        for i in range(nz):
            j = jnp.where(layer == 0, i, nz - 1 - i)
            to = half * nz + i
            padded[to, top + HALO : top + HALO + nx, :] = block[j]
            padded[to, pl.ds(after, HALO), :] = near[f, j]
            padded[to, pl.ds(before, HALO), :] = far[f, j]


def prepare_body(*refs):
    own, other, edges = refs[:3], refs[3:6], refs[6:10]
    c_pad, diag, wx, wx_back, wy, wz, grads, outer, s_pad, h_pad = refs[10:]
    nz, nx = own[0].shape[0], own[0].shape[1]
    planes, width = c_pad.shape[0], c_pad.shape[1]
    for f, target in enumerate((c_pad, s_pad, h_pad)):
        unpack(f, own[f], other[f], edges, target)
    lanes = lane_iota(width)
    last = lanes == LANES - 1
    for z in range(planes):
        c = c_pad[z]
        cf, cr = fore(c), jnp.where(last, 0.0, right(c))
        total = cf + back(c) + cr + jnp.where(lanes == 0, 0.0, left(c))
        wx[z] = joined(c, cf)
        wx_back[z] = joined(c, back(c))
        wy[z] = joined(c, cr)
        if z + 1 < planes:
            wz[z] = joined(c, c_pad[z + 1])
            total = total + c_pad[z + 1]
        if z:
            total = total + c_pad[z - 1]
        diag[z] = s_pad[z] + 3.0 * c + 0.5 * total

    span = HALO + nx
    rows, lanes = row_iota(width), lane_iota(width)
    mine = (rows >= HALO) & (rows < span)
    before = (rows >= HALO - 1) & (rows < span - 1)
    odd = (lanes & 1) == 1
    inside = mine & (lanes < LANES - 1)

    def kept(mask, x):
        return jnp.where(mask, x, 0.0)[:span]

    for z in range(nz):
        c, h = -0.5 * c_pad[z], h_pad[z]
        fall = h - fore(h)
        grads[0, z] = kept(mine, c * fall)
        grads[1, z] = kept(before, fore(c) * fall)
        fall = h - right(h)
        following = right(c) * fall
        grads[2, z] = kept(inside, c * fall + jnp.where(odd, 0.0, following))
        grads[3, z] = kept(inside & odd, following)
        weight = c + -0.5 * c_pad[z + 1] if z + 1 < nz else c
        grads[4, z] = kept(mine, weight * (h - h_pad[z + 1]))
        grads[5, z] = kept(mine & ((lanes == 0) | (lanes == LANES - 1)), c * h)
    outer[...] = kept(mine, -0.5 * c_pad[0] * h_pad[0])


def basis_body(peers, side_count, *refs):
    c_pad, diag_in, wx, wx_back, wy, wz, grads, outer = refs[:8]
    b_own, b_other, edges, refs = refs[8], refs[9], refs[10:14], refs[14:]
    sides = list(zip(refs[:side_count], refs[side_count : 2 * side_count]))
    spot_ref, slots_ref, own_ref, send_ref = refs[2 * side_count : 2 * side_count + 4]
    diag, ws, edge_grads, image, basis = refs[2 * side_count + 4 :]
    layer, row = lax.axis_index("layers"), lax.axis_index("rows")
    nz, nx = b_own.shape[0], b_own.shape[1]
    planes, width = c_pad.shape[0], c_pad.shape[1]
    span = HALO + nx
    inner = slice(HALO, span)
    top = HALO
    body = slice(top, top + width)
    for k in range(ITERS):
        for z in range(planes):
            basis[k, z, :top, :] = jnp.zeros((top, LANES), jnp.float32)
            basis[k, z, top + width :, :] = jnp.zeros((top, LANES), jnp.float32)
    unpack(3, b_own, b_other, edges, basis.at[0], top)

    lanes, rows = lane_iota(width), row_iota(width)
    y_at = lanes & (HALO - 1)
    if side_count == 1:
        meetings = [(jnp.where(row == 0, LANES - 1, 0), jnp.where(row == 0, 0, HALO - 1))]
    else:
        meetings = [(0, HALO - 1), (LANES - 1, 0)]
    strips = []
    for (here, there), (edge, meet) in zip(sides, meetings):
        halves = [jnp.transpose(x[...].reshape(LANES, LANES)) for x in (here, there)]
        first = jnp.where(layer == 0, halves[0], halves[1])
        second = jnp.where(layer == 0, halves[1], halves[0])
        fields = []
        for f in range(4):
            part = slice((f % 2) * width, (f % 2 + 1) * width)
            half = LANES // 2
            fields.append(
                jnp.where(
                    lanes < half,
                    pltpu.roll(first[part], half, 1) if f // 2 else first[part],
                    second[part] if f // 2 else pltpu.roll(second[part], half, 1),
                )
            )
        shifts = []
        for z in range(planes):
            spot = jnp.where(layer == 0, z, planes - 1 - z) * HALO + meet
            shifts.append(
                ((edge - spot) & (LANES - 1), (spot - edge) & (LANES - 1))
            )
        strips.append((fields, lanes == edge, shifts))

    def from_strips(values, z):
        total = jnp.zeros((width, LANES), jnp.float32)
        for (_, at_edge, shifts), value in zip(strips, values):
            total = jnp.where(at_edge, pltpu.roll(value, shifts[z][0], 1), total)
        return total

    def to_strip(strip, value, z):
        _, at_edge, shifts = strip
        if side_count > 1:
            value = jnp.where(at_edge, value, 0.0)
        return pltpu.roll(value, shifts[z][1], 1)

    edge_c = [jnp.zeros((width, LANES), jnp.float32) for _ in strips]
    mine = (rows >= HALO) & (rows < span)
    for z in range(planes):
        c = c_pad[z]
        c_side = from_strips([s[0][0] for s in strips], z)
        ws[z] = joined(c, c_side)
        diag[z] = diag_in[z] + 0.5 * c_side
        for i, strip in enumerate(strips):
            edge_c[i] = edge_c[i] + to_strip(strip, jnp.where(strip[1], c, 0.0), z)
        if z < nz:
            h_side = from_strips([s[0][2] for s in strips], z)
            edge_grads[z] = grads[5, z] + jnp.where(mine, 0.5 * c * h_side, 0.0)[:span]
    strip_terms = []
    for (fields, _, _), beside in zip(strips, edge_c):
        c = fields[0]
        cf = fore(c)
        cr = jnp.where(y_at < HALO - 1, right(c), 0.0)
        cu = jnp.where(lanes < LANES - HALO, pltpu.roll(c, LANES - HALO, 1), 0.0)
        total = cf + back(c) + cr + cu + beside
        total = total + jnp.where(y_at > 0, left(c), 0.0)
        total = total + jnp.where(lanes >= HALO, pltpu.roll(c, HALO, 1), 0.0)
        strip_terms.append(
            (fields[1] + 3.0 * c + 0.5 * total, joined(c, cf), joined(c, cr), joined(c, cu))
        )

    alphas, gammas, norms, sums = [], [], [], []

    def following(k, image_now, now, before):
        u = image_now - alphas[k - 1] * now
        return u - gammas[k - 1] * before if k > 1 else u

    def member(k, z):
        before = basis[k - 2, z, body, :] if k > 1 else None
        u = following(k, image[z], basis[k - 1, z, body, :], before)
        basis[k, z, body, :] = u
        return u

    def folded(x):
        return sum(x[r : r + 8] for r in range(8, width, 8)) + x[:8]

    side_now = [s[0][3] for s in strips]
    side_last, side_image = None, None
    for k in range(ITERS):
        above = member(k, 0) if k else basis[0, 0, body, :]
        v = None
        if k:
            side_next = [
                following(k, side_image[i], side_now[i], side_last[i] if k > 1 else None)
                for i in range(side_count)
            ]
            side_now, side_last = side_next, side_now
        norm = jnp.zeros((8, LANES), jnp.float32)
        energy = jnp.zeros((8, LANES), jnp.float32)
        side_image = []
        for x, (d, sx, sy, sz) in zip(side_now, strip_terms):
            ax = d * x - sx * fore(x) - back(sx * x) - sy * right(x) - left(sy * x)
            ax = ax - sz * pltpu.roll(x, LANES - HALO, 1) - pltpu.roll(sz * x, HALO, 1)
            side_image.append(ax)
        acc = basis[k, 0, top : top + span, :] * outer[...]
        acc_x = jnp.zeros((span, LANES), jnp.float32)
        acc_y = jnp.zeros((span, LANES), jnp.float32)
        for z in range(nz + ITERS - 1 - k):
            below, v = v, above
            above = member(k, z + 1) if k else basis[0, z + 1, body, :]
            side = from_strips(side_now, z)
            vf, vr = basis[k, z, top + 1 : top + 1 + width, :], right(v)
            vb = basis[k, z, top - 1 : top - 1 + width, :]
            wyz, wsz = wy[z], ws[z]
            av = diag[z] * v - wz[z] * above
            if z:
                av = av - wz[z - 1] * below
            av = av - wx[z] * vf - wx_back[z] * vb - wyz * vr - left(wyz * v) - wsz * side
            image[z] = av
            edge = wsz * v
            for i, strip in enumerate(strips):
                side_image[i] = side_image[i] - to_strip(strip, edge, z)
            norm = norm + folded(v * v)
            energy = energy + folded(v * av)
            if z < nz:
                fall = (v - vf)[:span]
                acc = acc + fall * grads[0, z]
                acc_x = acc_x + fall * grads[1, z]
                fall = (v - vr)[:span]
                acc = acc + fall * grads[2, z]
                acc_y = acc_y + fall * grads[3, z]
                acc = acc + (v - above)[:span] * grads[4, z]
                acc = acc + (v - side)[:span] * edge_grads[z]
                own_ref[k, jnp.where(layer == 0, z, nz - 1 - z)] = v[inner]
        for x, ax in zip(side_now, side_image):
            norm = norm + folded(x * x)
            energy = energy + folded(x * ax)
        sums.append((acc + back(acc_x) + left(acc_y))[inner])
        norm = all_sum(norm)
        alphas.append(safe_ratio(all_sum(energy), norm))
        gammas.append(safe_ratio(norm, norms[-1]) if k else jnp.zeros_like(norm))
        norms.append(norm)
    for z in range(nz):
        member(ITERS, z)
    own_rows = slice(top + HALO, top + span)

    dots = {}
    for i in range(ITERS + 1):
        for j in range(i + 1):
            acc = basis[i, 0, own_rows, :] * basis[j, 0, own_rows, :]
            for z in range(1, nz):
                acc = acc + basis[i, z, own_rows, :] * basis[j, z, own_rows, :]
            dots[i, j] = dots[j, i] = all_sum(acc)

    def operator(i, j):
        entry = dots[i, j + 1] + alphas[j] * dots[i, j]
        return entry + gammas[j] * dots[i, j - 1] if j else entry

    lanes = lane_iota(1)
    facts = []
    for j in range(ITERS):
        row_facts = [0.5 * (operator(j, m) + operator(m, j)) for m in range(ITERS)]
        row_facts += [alphas[j], gammas[j], norms[j], dots[j, 0]]
        entries = jnp.zeros((1, LANES), jnp.float32)
        for place, entry in enumerate(row_facts):
            entries = jnp.where(lanes == FACTS + place, entry, entries)
        facts.append(entries)

    blocks_x = nx // 4
    four = jnp.where(
        lax.shift_right_logical(lane_iota(blocks_x, nx), 2) == row_iota(blocks_x, nx), 1.0, 0.0
    )
    sums = mm(four, jnp.concatenate(sums, axis=1), precision=EXACT)
    spot = [spot_ref[r : r + 1, :] for r in range(blocks_x)]
    lane_hits = jnp.concatenate(
        [
            jnp.where(row_iota(LANES) == (p & (LANES - 1)), 1.0, 0.0).astype(jnp.bfloat16)
            for p in spot
        ],
        axis=1,
    )
    peer_at = row_iota(peers)
    row_hit = [(p >= 0) & (peer_at == lax.shift_right_arithmetic(p, LANE_BITS)) for p in spot]
    values = []
    for k in range(ITERS):
        pair = sums[:, k * LANES : (k + 1) * LANES]
        pair = pair + pltpu.roll(pair, LANES - 1, 1)
        for p in pieces_of(pair):
            values.append(
                jnp.concatenate(
                    [picked(row_hit[r], p[r : r + 1]) for r in range(blocks_x)], axis=1
                )
            )
    dense = mm(jnp.concatenate(values, axis=0), lane_hits, NT)
    copies = send_ref.shape[0] // peers
    for k in range(ITERS):
        at = 3 * k * peers
        rows = dense[at : at + peers] + dense[at + peers : at + 2 * peers]
        rows = rows + dense[at + 2 * peers : at + 3 * peers]
        rows = jnp.where(lane_iota(peers) < FACTS, rows, facts[k])
        if k < 2:
            slots = pltpu.roll(slots_ref[...], (1 - k) * (LANES - SLOTS) + FACTS, 1)
            rows = jnp.where(lane_iota(peers) < SLOTS, rows, slots)
        for peer in range(peers):
            for copy in range(copies):
                send_ref[peer * copies + copy, k : k + 1, :] = rows[peer : peer + 1]


def solve_body(copies, got_ref, own_ref, adjoint_ref, pilot_ref):
    senders = got_ref.shape[0]
    peers = senders // copies
    groups = senders * ITERS // LANES
    got = got_ref[...].reshape(groups, LANES, LANES)
    turned = [jnp.transpose(got[g])[FACTS:SLOTS] for g in range(groups)]

    def fact(place):
        return jnp.concatenate([t[place : place + 1] for t in turned], axis=0)

    alpha, gamma, weight, rhs = (fact(ITERS + place) for place in range(4))
    at = lane_iota(groups) & (ITERS - 1)
    gamma_next = jnp.where(at < ITERS - 1, pltpu.roll(gamma, LANES - 1, 1), 0.0)

    def over_senders(x):
        for shift in (8, 16, 32, 64):
            x = x + pltpu.roll(x, shift, 1)
        return jnp.sum(x, axis=0, keepdims=True)

    norm = over_senders(weight)
    means = safe_ratio(over_senders(weight * alpha), norm)
    growth = safe_ratio(norm, pltpu.roll(norm, 1, 1))
    now = jnp.where(at == 0, 1.0, 0.0)
    last = None
    common = [now]
    for k in range(ITERS - 1):
        image = jnp.where(at > 0, pltpu.roll(now, 1, 1), 0.0) + alpha * now
        image = image + gamma_next * pltpu.roll(now, LANES - 1, 1)
        following = image - means[:, k : k + 1] * now
        if k:
            following = following - growth[:, k : k + 1] * last
        now, last = following, now
        common.append(now)

    lanes = lane_iota(ITERS)
    system = jnp.zeros((ITERS, LANES), jnp.float32)
    stacked = []
    per = LANES // ITERS
    for g in range(groups):
        t = jnp.concatenate([c[g : g + 1] for c in common], axis=0)
        stacked.append(t)
        blocks = []
        for i in range(per):
            block = pltpu.roll(got_ref[g * per + i], (ITERS * i - FACTS) % LANES, 1)
            blocks.append(
                jnp.where((lanes >= ITERS * i) & (lanes < ITERS * (i + 1)), block, 0.0)
            )
        image = mm(t, jnp.concatenate(blocks, axis=0), precision=EXACT)
        beside = jnp.concatenate(
            [image, rhs[g : g + 1], jnp.zeros((LANES - ITERS - 1, LANES), jnp.float32)], axis=0
        )
        system = system + mm(t, beside, NT, precision=EXACT)
    rows = row_iota(ITERS)
    for p in range(ITERS):
        pivot = system[p : p + 1, p : p + 1]
        inverse = jnp.where(pivot > 0.0, 1.0 / jnp.where(pivot > 0.0, pivot, 1.0), 0.0)
        pivot_row = system[p : p + 1] * inverse
        system = jnp.where(rows == p, pivot_row, system - system[:, p : p + 1] * pivot_row)
    answer = system[:, ITERS : ITERS + 1]

    weights = [jnp.sum(answer * t, axis=0, keepdims=True) for t in stacked]
    me = lax.axis_index(GRID_AXES)
    mine = []
    for k in range(ITERS):
        w = jnp.zeros((1, 1), jnp.float32)
        for g in range(groups):
            hit = lane_iota(1) == me * ITERS + k - g * LANES
            w = w + jnp.sum(jnp.where(hit, weights[g], 0.0), axis=1, keepdims=True)
        mine.append(w)
    for z in range(own_ref.shape[1]):
        acc = mine[0] * own_ref[0, z]
        for k in range(1, ITERS):
            acc = acc + mine[k] * own_ref[k, z]
        adjoint_ref[z] = acc

    per_group = LANES // ITERS // copies
    sender = lax.div(lane_iota(per_group), jnp.int32(ITERS * copies))
    values = jnp.concatenate(
        [
            mm(jnp.where(sender == row_iota(per_group), weights[g], 0.0), got[g], precision=EXACT)
            for g in range(groups)
        ],
        axis=0,
    )
    rows_at, lanes_at = row_iota(pilot_ref.shape[0]), row_iota(LANES)
    held = lane_iota(peers) < pilot_ref.shape[0] * LANES // peers
    pieces = pieces_of(jnp.where(held, values, 0.0))
    left, right = [[], [], []], []
    room = LANES - SLOTS
    for s in range(peers):
        slot = jnp.where(
            lane_iota(1) < room,
            pltpu.roll(got_ref[s * copies, 0:1, :], room, 1),
            pltpu.roll(got_ref[s * copies, 1:2, :], 2 * room, 1),
        ).astype(jnp.int32)
        hit = rows_at == lax.shift_right_logical(slot, LANE_BITS)
        for q, piece in enumerate(pieces):
            left[q].append(picked(hit, piece[s : s + 1]))
        right.append(
            jnp.where(lanes_at == (slot & (LANES - 1)), 1.0, 0.0).astype(jnp.bfloat16)
        )
    right = jnp.concatenate(right, axis=1)
    pilot_ref[...] = sum(mm(jnp.concatenate(q, axis=1), right, NT) for q in left)


def tied(*values):
    return lax.optimization_barrier(values)


def neighbour_pairs(axis):
    forward = [(i, i + 1) for i in range(lax.axis_size(axis) - 1)]
    return forward, [(b, a) for a, b in forward]


def swap_pairs(axis, first):
    pairs = [(i, i + 1) for i in range(first, lax.axis_size(axis) - 1, 2)]
    return pairs + [(b, a) for a, b in pairs]


def swapped(x):
    return lax.ppermute(x, "layers", [(0, 1), (1, 0)])


def on_device(
    state_field,
    conductivity,
    storage,
    gauge_owner,
    gauge_cell,
    gauge_value,
    gauge_weight,
    pilot_index,
):
    nz, nx, ny = state_field.shape
    peers = lax.axis_size("cols") * lax.axis_size("rows")
    devices = peers * lax.axis_size("layers")
    gauges = gauge_owner.shape[0]
    capacity = 4 * gauges // peers
    f32 = jnp.float32
    row_count = lax.axis_size("rows")

    def shape(*dims, dtype=f32):
        return jax.ShapeDtypeStruct(dims, dtype)

    def flat(x):
        return x.reshape(gauges // LANES, LANES)

    obs = pltpu.VMEM((gauges // LANES, LANES), f32)
    obs_int = pltpu.VMEM((gauges // LANES, LANES), jnp.int32)
    payload = kernel_call(
        functools.partial(route_body, peers, capacity),
        shape(peers, 3 * capacity // LANES, LANES),
        [obs_int, obs_int, obs, obs, pltpu.SemaphoreType.DMA((4,))],
        weight=5,
        vmem=64 * 1024 * 1024,
    )(in_specs=[HBM] * 4, out_specs=VMEM)(
        flat(gauge_owner), flat(gauge_cell), flat(gauge_value), flat(gauge_weight)
    )
    payload, pilot_index = tied(payload, pilot_index)
    got = lax.all_to_all(payload, PEER_AXES, 0, 0, tiled=True)
    spot, slots = kernel_call(
        pilot_body, (shape(nx // 4, LANES, dtype=jnp.int32), shape(peers, LANES))
    )(in_specs=[VMEM], out_specs=(VMEM, VMEM))(pilot_index)

    fixed = (conductivity, storage, state_field)
    got, spot, *fixed_other = tied(got, spot, *(swapped(x) for x in fixed))
    edge = shape(4, nz, HALO, LANES)
    source, near, far = kernel_call(
        functools.partial(source_body, capacity // LANES),
        (shape(nz, nx, LANES), edge, edge),
        weight=6,
    )(in_specs=[VMEM] * 4, out_specs=(VMEM,) * 3)(got, *fixed)
    near = lax.ppermute(near, "cols", swap_pairs("cols", 0))
    far = lax.ppermute(far, "cols", swap_pairs("cols", 1))
    other = swapped(source)

    def packed(low_side):
        return kernel_call(
            functools.partial(pack_body, low_side), shape(2 * nz, HALO, LANES)
        )(in_specs=[VMEM] * 6, out_specs=VMEM)(*fixed, source, near, far)

    if row_count == 2:
        send = [(packed(None), [(0, 1), (1, 0)])]
    else:
        forward, backward = neighbour_pairs("rows")
        send = [(packed(False), forward), (packed(True), backward)]
    edges = tied(near, far, swapped(near), swapped(far), *(x for x, _ in send))[:4]
    sides = [lax.ppermute(x, "rows", pairs) for x, pairs in send]
    planes, width, span = 2 * nz, nx + 2 * HALO, nx + HALO
    padded = (planes, width, LANES)
    prepared = kernel_call(
        prepare_body,
        (*(shape(*padded) for _ in range(6)), shape(6, nz, span, LANES), shape(span, LANES)),
        [pltpu.VMEM(padded, f32)] * 2,
        weight=3,
    )(in_specs=[VMEM] * 10, out_specs=(VMEM,) * 8)(*fixed, *fixed_other, *edges)
    *sides, prepared = tied(*sides, prepared)
    sides = sides + [swapped(x) for x in sides]

    each = nx * ny // 8 // LANES
    own, send = kernel_call(
        functools.partial(basis_body, peers, len(sides) // 2),
        (shape(ITERS, nz, nx, LANES), shape(devices, ITERS, LANES)),
        [
            pltpu.VMEM(padded, f32),
            pltpu.VMEM(padded, f32),
            pltpu.VMEM((nz, span, LANES), f32),
            pltpu.VMEM(padded, f32),
            pltpu.VMEM((ITERS + 1, planes, width + 2 * HALO, LANES), f32),
        ],
        weight=10,
    )(in_specs=[VMEM] * (16 + len(sides)), out_specs=(VMEM, VMEM))(
        *prepared, source, other, *edges, *sides, spot, slots
    )
    parts = lax.all_to_all(send, GRID_AXES, 0, 0, tiled=True)
    adjoint, pilot = kernel_call(
        functools.partial(solve_body, devices // peers), (shape(nz, nx, ny), shape(each, LANES))
    )(in_specs=[VMEM] * 2, out_specs=(VMEM, VMEM))(parts, own)
    return adjoint, pilot.reshape(-1)


def solution(mesh):
    return jax.shard_map(
        on_device,
        mesh=mesh,
        in_specs=(
            P(("groups", "layers"), "cols", "rows"),
            P(("groups", "layers"), "cols", "rows"),
            P(("groups", "layers"), "cols", "rows"),
            P(("groups", "cols", "rows", "layers")),
            P(("groups", "cols", "rows", "layers")),
            P(("groups", "cols", "rows", "layers")),
            P(("groups", "cols", "rows", "layers")),
            P("cols", "rows"),
        ),
        out_specs=(P(("groups", "layers"), "cols", "rows"), P(("groups", "cols", "rows"))),
        check_vma=False,
    )
```

```python
import functools

import jax
import jax.numpy as jnp
from jax import lax
from jax.experimental import pallas as pl
from jax.experimental.pallas import tpu as pltpu
from jax.sharding import PartitionSpec as P

ITERS = 8
HALO = 8
EDGE = (0, 1, 1, 2)
FACTS = 64
SLOTS = 96
LANES = 128
LANE_BITS = 7
GRID_AXES = ("cols", "rows", "layers")
PEER_AXES = ("cols", "rows")
NT = (((1,), (1,)), ((), ()))
EXACT = lax.Precision.HIGHEST
VMEM_BYTES = 24 * 1024 * 1024


def kernel_call(body, out_shape, scratch=(), weight=1, vmem=VMEM_BYTES):
    return functools.partial(
        pl.pallas_call,
        body,
        out_shape=out_shape,
        scratch_shapes=list(scratch),
        compiler_params=pltpu.CompilerParams(vmem_limit_bytes=vmem),
        cost_estimate=pl.CostEstimate(
            flops=0, bytes_accessed=weight * 3_000_000, transcendentals=0
        ),
    )


VMEM = pl.BlockSpec(memory_space=pltpu.VMEM)
HBM = pl.BlockSpec(memory_space=pltpu.HBM)


def pieces_of(x):
    first = x.astype(jnp.bfloat16).astype(jnp.float32)
    rest = x - first
    second = rest.astype(jnp.bfloat16).astype(jnp.float32)
    return first, second, rest - second


def halves_of(x):
    first = x.astype(jnp.bfloat16).astype(jnp.float32)
    return first, x - first


def row_iota(rows, lanes=LANES):
    return lax.broadcasted_iota(jnp.int32, (rows, lanes), 0)


def lane_iota(rows, lanes=LANES):
    return lax.broadcasted_iota(jnp.int32, (rows, lanes), 1)


def picked(mask, row):
    return jnp.where(mask, row, jnp.zeros_like(row)).astype(jnp.bfloat16)


TILE = 16


def spread16(x, r):
    return jnp.broadcast_to(x[r : r + 1], (TILE, LANES)).astype(jnp.bfloat16)


def hits16(count, row):
    at = row_iota(TILE).astype(jnp.float32).astype(jnp.bfloat16)
    return [at + jnp.bfloat16(TILE * i) == row for i in range(count // TILE)]


def filled16(masks, value):
    zero = jnp.zeros((TILE, LANES), jnp.bfloat16)
    return jnp.concatenate([jnp.where(m, value, zero) for m in masks], axis=0)


def mm(a, b, dims=(((1,), (0,)), ((), ())), precision=None):
    return lax.dot_general(a, b, dims, precision=precision, preferred_element_type=jnp.float32)


def ranks(owner, peers):
    rows = owner.shape[0]
    ra, ca = row_iota(LANES, 2 * LANES), lane_iota(LANES, 2 * LANES)
    earlier_lane = jnp.where((ra < ca) | (ca >= LANES), 1.0, 0.0).astype(jnp.bfloat16)
    earlier_row = jnp.where(row_iota(rows, rows) > lane_iota(rows, rows), 1.0, 0.0).astype(
        jnp.bfloat16
    )
    hits = [owner == peer for peer in range(peers)]
    ones = jnp.concatenate([jnp.where(h, 1.0, 0.0).astype(jnp.bfloat16) for h in hits], axis=0)
    counts = mm(ones, earlier_lane)
    part = [counts[p * rows : (p + 1) * rows] for p in range(peers)]
    before = mm(
        earlier_row, jnp.concatenate([c[:, LANES:] for c in part], axis=1).astype(jnp.bfloat16)
    )
    rank = jnp.zeros((rows, LANES), jnp.float32)
    for p in range(peers):
        rank = jnp.where(
            hits[p], part[p][:, :LANES] + before[:, p * LANES : (p + 1) * LANES], rank
        )
    return rank.astype(jnp.int32)


def route_body(
    peers, capacity, owner_hbm, cell_hbm, value_hbm, weight_hbm, out_ref,
    owner_ref, cell_ref, value_ref, weight_ref, sems,
):
    copies = [
        pltpu.make_async_copy(source, target, sems.at[i])
        for i, (source, target) in enumerate(
            (
                (owner_hbm, owner_ref),
                (cell_hbm, cell_ref),
                (value_hbm, value_ref),
                (weight_hbm, weight_ref),
            )
        )
    ]
    for copy in copies:
        copy.start()
    copies[0].wait()
    rows = owner_ref.shape[0]
    owner = owner_ref[...]
    position = owner * capacity + ranks(owner, peers)
    for copy in copies[1:]:
        copy.wait()
    slot_row = lax.shift_right_logical(position, LANE_BITS).astype(jnp.float32)
    slot_lane = (position & (LANES - 1)).astype(jnp.float32)
    cell = cell_ref[...]
    columns = [
        lax.shift_right_logical(cell, LANE_BITS).astype(jnp.float32),
        (cell & (LANES - 1)).astype(jnp.float32),
        *pieces_of(value_ref[...]),
        *halves_of(weight_ref[...]),
    ]
    slot_rows = peers * capacity // LANES
    one = jnp.ones((TILE, LANES), jnp.bfloat16)
    total = None
    for start in range(0, rows, TILE):
        at_row, at_lane = [], [[] for _ in columns]
        for r in range(start, start + TILE):
            at_row.append(filled16(hits16(slot_rows, spread16(slot_row, r)), one))
            masks = hits16(LANES, spread16(slot_lane, r))
            for q, column in enumerate(columns):
                at_lane[q].append(filled16(masks, spread16(column, r)))
        at_lane = jnp.concatenate([jnp.concatenate(q, axis=1) for q in at_lane], axis=0)
        part = mm(at_lane, jnp.concatenate(at_row, axis=1), NT)
        total = part if total is None else total + part
    part = [total[q * LANES : (q + 1) * LANES] for q in range(len(columns))]
    fields = [
        part[0] * LANES + part[1],
        part[2] + part[3] + part[4],
        part[5] + part[6],
    ]
    fields = [jnp.transpose(f) for f in fields]
    each = capacity // LANES
    for peer in range(peers):
        for q, field in enumerate(fields):
            out_ref[peer, q * each : (q + 1) * each, :] = field[peer * each : (peer + 1) * each]


def pilot_body(pilot_ref, spot_ref, slots_ref):
    peers = slots_ref.shape[0]
    blocks_x = pilot_ref.shape[0] // 4
    pilots = pilot_ref.shape[0] * pilot_ref.shape[1] // 8
    pilot = jnp.concatenate([pilot_ref[4 * r : 4 * r + 1, :] for r in range(blocks_x)], axis=0)
    owner = lax.div(pilot, jnp.int32(pilots))
    slot = pilot - owner * pilots
    first = (lane_iota(blocks_x) & 1) == 0
    owner = jnp.where(first, owner, -1)
    rank = ranks(owner, peers)
    spot_ref[...] = jnp.where(first, owner * LANES + rank, -1)
    left, high, low = [], [], []
    peer_at, lanes_at = row_iota(peers), row_iota(LANES)
    for r in range(blocks_x):
        left.append(jnp.where(peer_at == owner[r : r + 1], 1.0, 0.0).astype(jnp.bfloat16))
        hit = lanes_at == rank[r : r + 1]
        number = slot[r : r + 1]
        high.append(picked(hit, lax.shift_right_logical(number, LANE_BITS).astype(jnp.float32)))
        low.append(picked(hit, (number & (LANES - 1)).astype(jnp.float32)))
    left = jnp.concatenate(left, axis=1)
    slots_ref[...] = mm(left, jnp.concatenate(high, axis=1), NT) * LANES + mm(
        left, jnp.concatenate(low, axis=1), NT
    )


def source_body(
    each, got_ref, conductivity_ref, storage_ref, state_ref, out_ref, near_ref, far_ref
):
    peers = got_ref.shape[0]
    nz, nx = state_ref.shape[0], state_ref.shape[1]
    cells = nz * nx
    one = jnp.ones((TILE, LANES), jnp.bfloat16)

    def sixteen(group, q):
        peer, row = divmod(group * TILE, each)
        if each >= TILE:
            return got_ref[peer, q * each + row : q * each + row + TILE, :]
        return jnp.concatenate(
            [got_ref[peer + i, q * each : (q + 1) * each, :] for i in range(TILE // each)], axis=0
        )

    total = None
    for group in range(peers * each // TILE):
        cell = sixteen(group, 0).astype(jnp.int32)
        high = lax.shift_right_logical(cell, LANE_BITS)
        low = cell & (LANES - 1)
        at_row = jnp.concatenate(
            [
                filled16(hits16(cells, spread16(high.astype(jnp.float32), r)), one)
                for r in range(TILE)
            ],
            axis=1,
        )
        heads = []
        if group == 0:
            state = jnp.transpose(state_ref[...].reshape(cells, LANES))
            lines = mm(
                jnp.concatenate([p.astype(jnp.bfloat16) for p in pieces_of(state)], axis=0), at_row
            )
            for r in range(TILE):
                line = lines[:, r * LANES : (r + 1) * LANES]
                line = line[:LANES] + line[LANES : 2 * LANES] + line[2 * LANES :]
                hit = row_iota(LANES) == low[r : r + 1]
                heads.append(jnp.sum(jnp.where(hit, line, 0.0), axis=0, keepdims=True))
        for r in range(0, 0 if heads else TILE, 8):
            head = jnp.zeros((8, LANES), jnp.float32)
            for z in range(nz):
                for x in range(nx):
                    line = jnp.broadcast_to(state_ref[z, x : x + 1, :], (8, LANES))
                    line = jnp.take_along_axis(line, low[r : r + 8], axis=1)
                    head = jnp.where(high[r : r + 8] == z * nx + x, line, head)
            heads.append(head)
        misfit = sixteen(group, 2) * (jnp.concatenate(heads, axis=0) - sixteen(group, 1))
        pieces = halves_of(misfit)
        low = low.astype(jnp.float32)
        at_lane = [[] for _ in pieces]
        for r in range(TILE):
            masks = hits16(LANES, spread16(low, r))
            for q, piece in enumerate(pieces):
                at_lane[q].append(filled16(masks, spread16(piece, r)))
        at_lane = jnp.concatenate([jnp.concatenate(q, axis=1) for q in at_lane], axis=0)
        part = mm(at_lane, at_row, NT)
        total = part if total is None else total + part
    total = jnp.transpose(total[:LANES] + total[LANES:])
    out_ref[...] = total.reshape(nz, nx, LANES)
    even = (lax.axis_index("cols") & 1) == 0
    total = total.reshape(nz, nx, LANES)
    at = lax.broadcasted_iota(jnp.int32, (nz, HALO, LANES), 1)
    for f, field in enumerate((conductivity_ref, storage_ref, total)):
        low, high = field[:, :HALO, :], field[:, nx - HALO :, :]
        if f == 1:
            low = jnp.where(at == HALO - 1, state_ref[:, :1, :], low)
            high = jnp.where(at == 0, state_ref[:, nx - 1 :, :], high)
        near_ref[f] = jnp.where(even, high, low)
        far_ref[f] = jnp.where(even, low, high)


def all_sum(x):
    while x.ndim > 2:
        x = jnp.sum(x, axis=0)
    return jnp.sum(jnp.sum(x, axis=0, keepdims=True), axis=1, keepdims=True)


def safe_ratio(a, b):
    return jnp.where(b > 0.0, a / jnp.where(b > 0.0, b, 1.0), 0.0)


def pack_body(low_side, *refs):
    *fields, near_ref, far_ref, out_ref = refs
    even = (lax.axis_index("cols") & 1) == 0
    nz, nx = fields[0].shape[0], fields[0].shape[1]
    lanes = lane_iota(2 * (nx + 2 * HALO))
    tall = jnp.zeros(lanes.shape, jnp.float32)
    for pair in range(2):
        for z in range(nz):
            at = (pair * nz + z) * HALO
            x = jnp.concatenate(
                [
                    part
                    for f in (2 * pair, 2 * pair + 1)
                    for part in (
                        jnp.where(even, far_ref[EDGE[f], z], near_ref[EDGE[f], z]),
                        fields[f][z],
                        jnp.where(even, near_ref[EDGE[f], z], far_ref[EDGE[f], z]),
                    )
                ],
                axis=0,
            )
            if low_side is None:
                shift = (at + jnp.where(lax.axis_index("rows") == 0, HALO, 0)) & (LANES - 1)
            else:
                shift = at if low_side else (at + HALO) & (LANES - 1)
            x = pltpu.roll(x, shift, 1)
            tall = jnp.where((lanes >= at) & (lanes < at + HALO), x, tall)
    rest = LANES - tall.shape[0]
    tall = jnp.concatenate([tall, jnp.zeros((rest, LANES), jnp.float32)], axis=0)
    out_ref[...] = jnp.transpose(tall).reshape(out_ref.shape)


def joined(a, b):
    return jnp.where((a > 0.0) & (b > 0.0), 0.5 * (a + b), 0.0)


def right(x):
    return pltpu.roll(x, x.shape[1] - 1, 1)


def left(x):
    return pltpu.roll(x, 1, 1)


def fore(x):
    return pltpu.roll(x, x.shape[0] - 1, 0)


def back(x):
    return pltpu.roll(x, 1, 0)


def unpack(f, own, other, edges, padded, top=0):
    nz, nx = own.shape[0], own.shape[1]
    layer, even = lax.axis_index("layers"), (lax.axis_index("cols") & 1) == 0
    after = pl.multiple_of(jnp.where(even, top + HALO + nx, top), HALO)
    before = pl.multiple_of(jnp.where(even, top, top + HALO + nx), HALO)
    for half, block in ((0, own), (1, other)):
        near, far = edges[2 * half], edges[2 * half + 1]
        for i in range(nz):
            j = jnp.where(layer == 0, i, nz - 1 - i)
            to = half * nz + i
            padded[to, top + HALO : top + HALO + nx, :] = block[j]
            padded[to, pl.ds(after, HALO), :] = near[EDGE[f], j]
            padded[to, pl.ds(before, HALO), :] = far[EDGE[f], j]


def prepare_body(*refs):
    own, other, edges = refs[:3], refs[3:6], refs[6:10]
    c_pad, diag, wx, wx_back, wy, wz, grads, outer, s_pad, h_pad = refs[10:]
    nz, nx = own[0].shape[0], own[0].shape[1]
    planes, width = c_pad.shape[0], c_pad.shape[1]
    for f, target in enumerate((c_pad, s_pad, h_pad)):
        unpack(f, own[f], other[f], edges, target)
    none = jnp.zeros((1, LANES), jnp.float32)
    for z in range(planes):
        h_pad[z, HALO - 1 : HALO, :] = s_pad[z, :1, :]
        h_pad[z, width - HALO : width - HALO + 1, :] = s_pad[z, width - 1 :, :]
        s_pad[z, :1, :] = none
        s_pad[z, width - 1 :, :] = none
    lanes = lane_iota(width)
    last = lanes == LANES - 1
    for z in range(planes):
        c = c_pad[z]
        cf, cr = fore(c), jnp.where(last, 0.0, right(c))
        total = cf + back(c) + cr + jnp.where(lanes == 0, 0.0, left(c))
        wx[z] = joined(c, cf)
        wx_back[z] = joined(c, back(c))
        wy[z] = joined(c, cr)
        if z + 1 < planes:
            wz[z] = joined(c, c_pad[z + 1])
            total = total + c_pad[z + 1]
        if z:
            total = total + c_pad[z - 1]
        diag[z] = s_pad[z] + 3.0 * c + 0.5 * total

    span = HALO + nx
    rows, lanes = row_iota(width), lane_iota(width)
    mine = (rows >= HALO) & (rows < span)
    before = (rows >= HALO - 1) & (rows < span - 1)
    odd = (lanes & 1) == 1
    inside = mine & (lanes < LANES - 1)

    def kept(mask, x):
        return jnp.where(mask, x, 0.0)[:span]

    for z in range(nz):
        c, h = -0.5 * c_pad[z], h_pad[z]
        fall = h - fore(h)
        grads[0, z] = kept(mine, c * fall)
        grads[1, z] = kept(before, fore(c) * fall)
        fall = h - right(h)
        following = right(c) * fall
        grads[2, z] = kept(inside, c * fall + jnp.where(odd, 0.0, following))
        grads[3, z] = kept(inside & odd, following)
        weight = c + -0.5 * c_pad[z + 1] if z + 1 < nz else c
        grads[4, z] = kept(mine, weight * (h - h_pad[z + 1]))
        grads[5, z] = kept(mine & ((lanes == 0) | (lanes == LANES - 1)), c * h)
    outer[...] = kept(mine, -0.5 * c_pad[0] * h_pad[0])


def basis_body(peers, side_count, *refs):
    c_pad, diag_in, wx, wx_back, wy, wz, grads, outer = refs[:8]
    b_own, b_other, edges, refs = refs[8], refs[9], refs[10:14], refs[14:]
    sides = list(zip(refs[:side_count], refs[side_count : 2 * side_count]))
    spot_ref, slots_ref, own_ref, send_ref = refs[2 * side_count : 2 * side_count + 4]
    diag, ws, edge_grads, image, basis = refs[2 * side_count + 4 :]
    layer, row = lax.axis_index("layers"), lax.axis_index("rows")
    nz, nx = b_own.shape[0], b_own.shape[1]
    planes, width = c_pad.shape[0], c_pad.shape[1]
    span = HALO + nx
    inner = slice(HALO, span)
    top = HALO
    body = slice(top, top + width)
    for k in range(ITERS):
        for z in range(planes):
            basis[k, z, :top, :] = jnp.zeros((top, LANES), jnp.float32)
            basis[k, z, top + width :, :] = jnp.zeros((top, LANES), jnp.float32)
    unpack(3, b_own, b_other, edges, basis.at[0], top)

    lanes, rows = lane_iota(width), row_iota(width)
    y_at = lanes & (HALO - 1)
    if side_count == 1:
        meetings = [(jnp.where(row == 0, LANES - 1, 0), jnp.where(row == 0, 0, HALO - 1))]
    else:
        meetings = [(0, HALO - 1), (LANES - 1, 0)]
    strips = []
    for (here, there), (edge, meet) in zip(sides, meetings):
        halves = [jnp.transpose(x[...].reshape(LANES, LANES)) for x in (here, there)]
        first = jnp.where(layer == 0, halves[0], halves[1])
        second = jnp.where(layer == 0, halves[1], halves[0])
        fields = []
        for f in range(4):
            part = slice((f % 2) * width, (f % 2 + 1) * width)
            half = LANES // 2
            fields.append(
                jnp.where(
                    lanes < half,
                    pltpu.roll(first[part], half, 1) if f // 2 else first[part],
                    second[part] if f // 2 else pltpu.roll(second[part], half, 1),
                )
            )
        fields[1] = jnp.where((rows == 0) | (rows == width - 1), 0.0, fields[1])
        shifts = []
        for z in range(planes):
            spot = jnp.where(layer == 0, z, planes - 1 - z) * HALO + meet
            shifts.append(
                ((edge - spot) & (LANES - 1), (spot - edge) & (LANES - 1))
            )
        strips.append((fields, lanes == edge, shifts))

    def from_strips(values, z):
        total = jnp.zeros((width, LANES), jnp.float32)
        for (_, at_edge, shifts), value in zip(strips, values):
            total = jnp.where(at_edge, pltpu.roll(value, shifts[z][0], 1), total)
        return total

    def to_strip(strip, value, z):
        _, at_edge, shifts = strip
        if side_count > 1:
            value = jnp.where(at_edge, value, 0.0)
        return pltpu.roll(value, shifts[z][1], 1)

    edge_c = [jnp.zeros((width, LANES), jnp.float32) for _ in strips]
    mine = (rows >= HALO) & (rows < span)
    for z in range(planes):
        c = c_pad[z]
        c_side = from_strips([s[0][0] for s in strips], z)
        ws[z] = joined(c, c_side)
        diag[z] = diag_in[z] + 0.5 * c_side
        for i, strip in enumerate(strips):
            edge_c[i] = edge_c[i] + to_strip(strip, jnp.where(strip[1], c, 0.0), z)
        if z < nz:
            h_side = from_strips([s[0][2] for s in strips], z)
            edge_grads[z] = grads[5, z] + jnp.where(mine, 0.5 * c * h_side, 0.0)[:span]
    strip_terms = []
    for (fields, _, _), beside in zip(strips, edge_c):
        c = fields[0]
        cf = fore(c)
        cr = jnp.where(y_at < HALO - 1, right(c), 0.0)
        cu = jnp.where(lanes < LANES - HALO, pltpu.roll(c, LANES - HALO, 1), 0.0)
        total = cf + back(c) + cr + cu + beside
        total = total + jnp.where(y_at > 0, left(c), 0.0)
        total = total + jnp.where(lanes >= HALO, pltpu.roll(c, HALO, 1), 0.0)
        strip_terms.append(
            (fields[1] + 3.0 * c + 0.5 * total, joined(c, cf), joined(c, cr), joined(c, cu))
        )

    alphas, gammas, norms, sums = [], [], [], []

    def following(k, image_now, now, before):
        u = image_now - alphas[k - 1] * now
        return u - gammas[k - 1] * before if k > 1 else u

    def member(k, z):
        before = basis[k - 2, z, body, :] if k > 1 else None
        u = following(k, image[z], basis[k - 1, z, body, :], before)
        basis[k, z, body, :] = u
        return u

    def folded(x):
        return sum(x[r : r + 8] for r in range(8, width, 8)) + x[:8]

    side_now = [s[0][3] for s in strips]
    side_last, side_image = None, None
    for k in range(ITERS):
        above = member(k, 0) if k else basis[0, 0, body, :]
        v = None
        if k:
            side_next = [
                following(k, side_image[i], side_now[i], side_last[i] if k > 1 else None)
                for i in range(side_count)
            ]
            side_now, side_last = side_next, side_now
        norm = jnp.zeros((8, LANES), jnp.float32)
        energy = jnp.zeros((8, LANES), jnp.float32)
        side_image = []
        for x, (d, sx, sy, sz) in zip(side_now, strip_terms):
            ax = d * x - sx * fore(x) - back(sx * x) - sy * right(x) - left(sy * x)
            ax = ax - sz * pltpu.roll(x, LANES - HALO, 1) - pltpu.roll(sz * x, HALO, 1)
            side_image.append(ax)
        acc = basis[k, 0, top : top + span, :] * outer[...]
        acc_x = jnp.zeros((span, LANES), jnp.float32)
        acc_y = jnp.zeros((span, LANES), jnp.float32)
        for z in range(nz + ITERS - 1 - k):
            below, v = v, above
            above = member(k, z + 1) if k else basis[0, z + 1, body, :]
            side = from_strips(side_now, z)
            vf, vr = basis[k, z, top + 1 : top + 1 + width, :], right(v)
            vb = basis[k, z, top - 1 : top - 1 + width, :]
            wyz, wsz = wy[z], ws[z]
            av = diag[z] * v - wz[z] * above
            if z:
                av = av - wz[z - 1] * below
            av = av - wx[z] * vf - wx_back[z] * vb - wyz * vr - left(wyz * v) - wsz * side
            image[z] = av
            edge = wsz * v
            for i, strip in enumerate(strips):
                side_image[i] = side_image[i] - to_strip(strip, edge, z)
            norm = norm + folded(v * v)
            energy = energy + folded(v * av)
            if z < nz:
                fall = (v - vf)[:span]
                acc = acc + fall * grads[0, z]
                acc_x = acc_x + fall * grads[1, z]
                fall = (v - vr)[:span]
                acc = acc + fall * grads[2, z]
                acc_y = acc_y + fall * grads[3, z]
                acc = acc + (v - above)[:span] * grads[4, z]
                acc = acc + (v - side)[:span] * edge_grads[z]
                own_ref[k, jnp.where(layer == 0, z, nz - 1 - z)] = v[inner]
        for x, ax in zip(side_now, side_image):
            norm = norm + folded(x * x)
            energy = energy + folded(x * ax)
        sums.append((acc + back(acc_x) + left(acc_y))[inner])
        norm = all_sum(norm)
        alphas.append(safe_ratio(all_sum(energy), norm))
        gammas.append(safe_ratio(norm, norms[-1]) if k else jnp.zeros_like(norm))
        norms.append(norm)
    for z in range(nz):
        member(ITERS, z)
    own_rows = slice(top + HALO, top + span)

    dots = {}
    for i in range(ITERS + 1):
        for j in range(i + 1):
            acc = basis[i, 0, own_rows, :] * basis[j, 0, own_rows, :]
            for z in range(1, nz):
                acc = acc + basis[i, z, own_rows, :] * basis[j, z, own_rows, :]
            dots[i, j] = dots[j, i] = all_sum(acc)

    def operator(i, j):
        entry = dots[i, j + 1] + alphas[j] * dots[i, j]
        return entry + gammas[j] * dots[i, j - 1] if j else entry

    lanes = lane_iota(1)
    facts = []
    for j in range(ITERS):
        row_facts = [0.5 * (operator(j, m) + operator(m, j)) for m in range(ITERS)]
        row_facts += [alphas[j], gammas[j], norms[j], dots[j, 0]]
        entries = jnp.zeros((1, LANES), jnp.float32)
        for place, entry in enumerate(row_facts):
            entries = jnp.where(lanes == FACTS + place, entry, entries)
        facts.append(entries)

    blocks_x = nx // 4
    four = jnp.where(
        lax.shift_right_logical(lane_iota(blocks_x, nx), 2) == row_iota(blocks_x, nx), 1.0, 0.0
    )
    sums = mm(four, jnp.concatenate(sums, axis=1), precision=EXACT)
    spot = [spot_ref[r : r + 1, :] for r in range(blocks_x)]
    lane_hits = jnp.concatenate(
        [
            jnp.where(row_iota(LANES) == (p & (LANES - 1)), 1.0, 0.0).astype(jnp.bfloat16)
            for p in spot
        ],
        axis=1,
    )
    peer_at = row_iota(peers)
    row_hit = [(p >= 0) & (peer_at == lax.shift_right_arithmetic(p, LANE_BITS)) for p in spot]
    values = []
    for k in range(ITERS):
        pair = sums[:, k * LANES : (k + 1) * LANES]
        pair = pair + pltpu.roll(pair, LANES - 1, 1)
        for p in pieces_of(pair):
            values.append(
                jnp.concatenate(
                    [picked(row_hit[r], p[r : r + 1]) for r in range(blocks_x)], axis=1
                )
            )
    dense = mm(jnp.concatenate(values, axis=0), lane_hits, NT)
    copies = send_ref.shape[0] // peers
    for k in range(ITERS):
        at = 3 * k * peers
        rows = dense[at : at + peers] + dense[at + peers : at + 2 * peers]
        rows = rows + dense[at + 2 * peers : at + 3 * peers]
        rows = jnp.where(lane_iota(peers) < FACTS, rows, facts[k])
        if k < 2:
            slots = pltpu.roll(slots_ref[...], (1 - k) * (LANES - SLOTS) + FACTS, 1)
            rows = jnp.where(lane_iota(peers) < SLOTS, rows, slots)
        for peer in range(peers):
            for copy in range(copies):
                send_ref[peer * copies + copy, k : k + 1, :] = rows[peer : peer + 1]


def solve_body(copies, got_ref, own_ref, adjoint_ref, pilot_ref):
    senders = got_ref.shape[0]
    peers = senders // copies
    groups = senders * ITERS // LANES
    got = got_ref[...].reshape(groups, LANES, LANES)
    turned = [jnp.transpose(got[g])[FACTS:SLOTS] for g in range(groups)]

    def fact(place):
        return jnp.concatenate([t[place : place + 1] for t in turned], axis=0)

    alpha, gamma, weight, rhs = (fact(ITERS + place) for place in range(4))
    at = lane_iota(groups) & (ITERS - 1)
    gamma_next = jnp.where(at < ITERS - 1, pltpu.roll(gamma, LANES - 1, 1), 0.0)

    def over_senders(x):
        for shift in (8, 16, 32, 64):
            x = x + pltpu.roll(x, shift, 1)
        return jnp.sum(x, axis=0, keepdims=True)

    norm = over_senders(weight)
    means = safe_ratio(over_senders(weight * alpha), norm)
    growth = safe_ratio(norm, pltpu.roll(norm, 1, 1))
    now = jnp.where(at == 0, 1.0, 0.0)
    last = None
    common = [now]
    for k in range(ITERS - 1):
        image = jnp.where(at > 0, pltpu.roll(now, 1, 1), 0.0) + alpha * now
        image = image + gamma_next * pltpu.roll(now, LANES - 1, 1)
        following = image - means[:, k : k + 1] * now
        if k:
            following = following - growth[:, k : k + 1] * last
        now, last = following, now
        common.append(now)

    lanes = lane_iota(ITERS)
    system = jnp.zeros((ITERS, LANES), jnp.float32)
    stacked = []
    per = LANES // ITERS
    for g in range(groups):
        t = jnp.concatenate([c[g : g + 1] for c in common], axis=0)
        stacked.append(t)
        blocks = []
        for i in range(per):
            block = pltpu.roll(got_ref[g * per + i], (ITERS * i - FACTS) % LANES, 1)
            blocks.append(
                jnp.where((lanes >= ITERS * i) & (lanes < ITERS * (i + 1)), block, 0.0)
            )
        image = mm(t, jnp.concatenate(blocks, axis=0), precision=EXACT)
        beside = jnp.concatenate(
            [image, rhs[g : g + 1], jnp.zeros((LANES - ITERS - 1, LANES), jnp.float32)], axis=0
        )
        system = system + mm(t, beside, NT, precision=EXACT)
    rows = row_iota(ITERS)
    for p in range(ITERS):
        pivot = system[p : p + 1, p : p + 1]
        inverse = jnp.where(pivot > 0.0, 1.0 / jnp.where(pivot > 0.0, pivot, 1.0), 0.0)
        pivot_row = system[p : p + 1] * inverse
        system = jnp.where(rows == p, pivot_row, system - system[:, p : p + 1] * pivot_row)
    answer = system[:, ITERS : ITERS + 1]

    weights = [jnp.sum(answer * t, axis=0, keepdims=True) for t in stacked]
    me = lax.axis_index(GRID_AXES)
    mine = []
    for k in range(ITERS):
        w = jnp.zeros((1, 1), jnp.float32)
        for g in range(groups):
            hit = lane_iota(1) == me * ITERS + k - g * LANES
            w = w + jnp.sum(jnp.where(hit, weights[g], 0.0), axis=1, keepdims=True)
        mine.append(w)
    for z in range(own_ref.shape[1]):
        acc = mine[0] * own_ref[0, z]
        for k in range(1, ITERS):
            acc = acc + mine[k] * own_ref[k, z]
        adjoint_ref[z] = acc

    per_group = LANES // ITERS // copies
    sender = lax.div(lane_iota(per_group), jnp.int32(ITERS * copies))
    values = jnp.concatenate(
        [
            mm(jnp.where(sender == row_iota(per_group), weights[g], 0.0), got[g], precision=EXACT)
            for g in range(groups)
        ],
        axis=0,
    )
    rows_at, lanes_at = row_iota(pilot_ref.shape[0]), row_iota(LANES)
    held = lane_iota(peers) < pilot_ref.shape[0] * LANES // peers
    pieces = pieces_of(jnp.where(held, values, 0.0))
    left, right = [[], [], []], []
    room = LANES - SLOTS
    for s in range(peers):
        slot = jnp.where(
            lane_iota(1) < room,
            pltpu.roll(got_ref[s * copies, 0:1, :], room, 1),
            pltpu.roll(got_ref[s * copies, 1:2, :], 2 * room, 1),
        ).astype(jnp.int32)
        hit = rows_at == lax.shift_right_logical(slot, LANE_BITS)
        for q, piece in enumerate(pieces):
            left[q].append(picked(hit, piece[s : s + 1]))
        right.append(
            jnp.where(lanes_at == (slot & (LANES - 1)), 1.0, 0.0).astype(jnp.bfloat16)
        )
    right = jnp.concatenate(right, axis=1)
    pilot_ref[...] = sum(mm(jnp.concatenate(q, axis=1), right, NT) for q in left)


def tied(*values):
    return lax.optimization_barrier(values)


def neighbour_pairs(axis):
    forward = [(i, i + 1) for i in range(lax.axis_size(axis) - 1)]
    return forward, [(b, a) for a, b in forward]


def swap_pairs(axis, first):
    pairs = [(i, i + 1) for i in range(first, lax.axis_size(axis) - 1, 2)]
    return pairs + [(b, a) for a, b in pairs]


def swapped(x):
    return lax.ppermute(x, "layers", [(0, 1), (1, 0)])


def on_device(
    state_field,
    conductivity,
    storage,
    gauge_owner,
    gauge_cell,
    gauge_value,
    gauge_weight,
    pilot_index,
):
    nz, nx, ny = state_field.shape
    peers = lax.axis_size("cols") * lax.axis_size("rows")
    devices = peers * lax.axis_size("layers")
    gauges = gauge_owner.shape[0]
    capacity = 4 * gauges // peers
    f32 = jnp.float32
    row_count = lax.axis_size("rows")

    def shape(*dims, dtype=f32):
        return jax.ShapeDtypeStruct(dims, dtype)

    def flat(x):
        return x.reshape(gauges // LANES, LANES)

    obs = pltpu.VMEM((gauges // LANES, LANES), f32)
    obs_int = pltpu.VMEM((gauges // LANES, LANES), jnp.int32)
    payload = kernel_call(
        functools.partial(route_body, peers, capacity),
        shape(peers, 3 * capacity // LANES, LANES),
        [obs_int, obs_int, obs, obs, pltpu.SemaphoreType.DMA((4,))],
        weight=5,
        vmem=64 * 1024 * 1024,
    )(in_specs=[HBM] * 4, out_specs=VMEM)(
        flat(gauge_owner), flat(gauge_cell), flat(gauge_value), flat(gauge_weight)
    )
    payload, pilot_index = tied(payload, pilot_index)
    got = lax.all_to_all(payload, PEER_AXES, 0, 0, tiled=True)
    spot, slots = kernel_call(
        pilot_body, (shape(nx // 4, LANES, dtype=jnp.int32), shape(peers, LANES))
    )(in_specs=[VMEM], out_specs=(VMEM, VMEM))(pilot_index)

    fixed = (conductivity, storage, state_field)
    got, spot, *fixed_other = tied(got, spot, *(swapped(x) for x in fixed))
    edge = shape(3, nz, HALO, LANES)
    source, near, far = kernel_call(
        functools.partial(source_body, capacity // LANES),
        (shape(nz, nx, LANES), edge, edge),
        weight=6,
    )(in_specs=[VMEM] * 4, out_specs=(VMEM,) * 3)(got, *fixed)
    near = lax.ppermute(near, "cols", swap_pairs("cols", 0))
    far = lax.ppermute(far, "cols", swap_pairs("cols", 1))
    other = swapped(source)

    def packed(low_side):
        return kernel_call(
            functools.partial(pack_body, low_side), shape(2 * nz, HALO, LANES)
        )(in_specs=[VMEM] * 6, out_specs=VMEM)(*fixed, source, near, far)

    if row_count == 2:
        send = [(packed(None), [(0, 1), (1, 0)])]
    else:
        forward, backward = neighbour_pairs("rows")
        send = [(packed(False), forward), (packed(True), backward)]
    edges = tied(near, far, swapped(near), swapped(far), *(x for x, _ in send))[:4]
    sides = [lax.ppermute(x, "rows", pairs) for x, pairs in send]
    planes, width, span = 2 * nz, nx + 2 * HALO, nx + HALO
    padded = (planes, width, LANES)
    prepared = kernel_call(
        prepare_body,
        (*(shape(*padded) for _ in range(6)), shape(6, nz, span, LANES), shape(span, LANES)),
        [pltpu.VMEM(padded, f32)] * 2,
        weight=3,
    )(in_specs=[VMEM] * 10, out_specs=(VMEM,) * 8)(*fixed, *fixed_other, *edges)
    *sides, prepared = tied(*sides, prepared)
    sides = sides + [swapped(x) for x in sides]

    each = nx * ny // 8 // LANES
    own, send = kernel_call(
        functools.partial(basis_body, peers, len(sides) // 2),
        (shape(ITERS, nz, nx, LANES), shape(devices, ITERS, LANES)),
        [
            pltpu.VMEM(padded, f32),
            pltpu.VMEM(padded, f32),
            pltpu.VMEM((nz, span, LANES), f32),
            pltpu.VMEM(padded, f32),
            pltpu.VMEM((ITERS + 1, planes, width + 2 * HALO, LANES), f32),
        ],
        weight=10,
    )(in_specs=[VMEM] * (16 + len(sides)), out_specs=(VMEM, VMEM))(
        *prepared, source, other, *edges, *sides, spot, slots
    )
    parts = lax.all_to_all(send, GRID_AXES, 0, 0, tiled=True)
    adjoint, pilot = kernel_call(
        functools.partial(solve_body, devices // peers), (shape(nz, nx, ny), shape(each, LANES))
    )(in_specs=[VMEM] * 2, out_specs=(VMEM, VMEM))(parts, own)
    return adjoint, pilot.reshape(-1)


def solution(mesh):
    return jax.shard_map(
        on_device,
        mesh=mesh,
        in_specs=(
            P(("groups", "layers"), "cols", "rows"),
            P(("groups", "layers"), "cols", "rows"),
            P(("groups", "layers"), "cols", "rows"),
            P(("groups", "cols", "rows", "layers")),
            P(("groups", "cols", "rows", "layers")),
            P(("groups", "cols", "rows", "layers")),
            P(("groups", "cols", "rows", "layers")),
            P("cols", "rows"),
        ),
        out_specs=(P(("groups", "layers"), "cols", "rows"), P(("groups", "cols", "rows"))),
        check_vma=False,
    )
```

```python
import functools

import jax
import jax.numpy as jnp
from jax import lax
from jax.experimental import pallas as pl
from jax.experimental.pallas import tpu as pltpu
from jax.sharding import PartitionSpec as P

ITERS = 8
HALO = 8
EDGE = (0, 1, 1, 2)
FACTS = 64
SLOTS = 96
LANES = 128
LANE_BITS = 7
GRID_AXES = ("cols", "rows", "layers")
PEER_AXES = ("cols", "rows")
NT = (((1,), (1,)), ((), ()))
EXACT = lax.Precision.HIGHEST
VMEM_BYTES = 24 * 1024 * 1024


def kernel_call(body, out_shape, scratch=(), weight=1, vmem=VMEM_BYTES):
    return functools.partial(
        pl.pallas_call,
        body,
        out_shape=out_shape,
        scratch_shapes=list(scratch),
        compiler_params=pltpu.CompilerParams(vmem_limit_bytes=vmem),
        cost_estimate=pl.CostEstimate(
            flops=0, bytes_accessed=weight * 3_000_000, transcendentals=0
        ),
    )


VMEM = pl.BlockSpec(memory_space=pltpu.VMEM)
HBM = pl.BlockSpec(memory_space=pltpu.HBM)


def pieces_of(x):
    first = x.astype(jnp.bfloat16).astype(jnp.float32)
    rest = x - first
    second = rest.astype(jnp.bfloat16).astype(jnp.float32)
    return first, second, rest - second


def halves_of(x):
    first = x.astype(jnp.bfloat16).astype(jnp.float32)
    return first, x - first


def row_iota(rows, lanes=LANES):
    return lax.broadcasted_iota(jnp.int32, (rows, lanes), 0)


def lane_iota(rows, lanes=LANES):
    return lax.broadcasted_iota(jnp.int32, (rows, lanes), 1)


def picked(mask, row):
    return jnp.where(mask, row, jnp.zeros_like(row)).astype(jnp.bfloat16)


TILE = 16


def spread16(x, r):
    return jnp.broadcast_to(x[r : r + 1], (TILE, LANES)).astype(jnp.bfloat16)


def hits16(count, row):
    at = row_iota(TILE).astype(jnp.float32).astype(jnp.bfloat16)
    return [at + jnp.bfloat16(TILE * i) == row for i in range(count // TILE)]


def filled16(masks, value):
    zero = jnp.zeros((TILE, LANES), jnp.bfloat16)
    return jnp.concatenate([jnp.where(m, value, zero) for m in masks], axis=0)


def mm(a, b, dims=(((1,), (0,)), ((), ())), precision=None):
    return lax.dot_general(a, b, dims, precision=precision, preferred_element_type=jnp.float32)


def ranks(owner, peers):
    rows = owner.shape[0]
    ra, ca = row_iota(LANES, 2 * LANES), lane_iota(LANES, 2 * LANES)
    earlier_lane = jnp.where((ra < ca) | (ca >= LANES), 1.0, 0.0).astype(jnp.bfloat16)
    earlier_row = jnp.where(row_iota(rows, rows) > lane_iota(rows, rows), 1.0, 0.0).astype(
        jnp.bfloat16
    )
    hits = [owner == peer for peer in range(peers)]
    ones = jnp.concatenate([jnp.where(h, 1.0, 0.0).astype(jnp.bfloat16) for h in hits], axis=0)
    counts = mm(ones, earlier_lane)
    part = [counts[p * rows : (p + 1) * rows] for p in range(peers)]
    before = mm(
        earlier_row, jnp.concatenate([c[:, LANES:] for c in part], axis=1).astype(jnp.bfloat16)
    )
    rank = jnp.zeros((rows, LANES), jnp.float32)
    for p in range(peers):
        rank = jnp.where(
            hits[p], part[p][:, :LANES] + before[:, p * LANES : (p + 1) * LANES], rank
        )
    return rank.astype(jnp.int32)


def route_body(
    peers, capacity, owner_hbm, cell_hbm, value_hbm, weight_hbm, out_ref,
    owner_ref, cell_ref, value_ref, weight_ref, sems,
):
    copies = [
        pltpu.make_async_copy(source, target, sems.at[i])
        for i, (source, target) in enumerate(
            (
                (owner_hbm, owner_ref),
                (cell_hbm, cell_ref),
                (value_hbm, value_ref),
                (weight_hbm, weight_ref),
            )
        )
    ]
    for copy in copies:
        copy.start()
    copies[0].wait()
    rows = owner_ref.shape[0]
    owner = owner_ref[...]
    position = owner * capacity + ranks(owner, peers)
    for copy in copies[1:]:
        copy.wait()
    slot_row = lax.shift_right_logical(position, LANE_BITS).astype(jnp.float32)
    slot_lane = (position & (LANES - 1)).astype(jnp.float32)
    cell = cell_ref[...]
    columns = [
        lax.shift_right_logical(cell, LANE_BITS).astype(jnp.float32),
        (cell & (LANES - 1)).astype(jnp.float32),
        *pieces_of(value_ref[...]),
        *halves_of(weight_ref[...]),
    ]
    slot_rows = peers * capacity // LANES
    one = jnp.ones((TILE, LANES), jnp.bfloat16)
    total = None
    for start in range(0, rows, TILE):
        at_row, at_lane = [], [[] for _ in columns]
        for r in range(start, start + TILE):
            at_row.append(filled16(hits16(slot_rows, spread16(slot_row, r)), one))
            masks = hits16(LANES, spread16(slot_lane, r))
            for q, column in enumerate(columns):
                at_lane[q].append(filled16(masks, spread16(column, r)))
        at_lane = jnp.concatenate([jnp.concatenate(q, axis=1) for q in at_lane], axis=0)
        part = mm(at_lane, jnp.concatenate(at_row, axis=1), NT)
        total = part if total is None else total + part
    part = [total[q * LANES : (q + 1) * LANES] for q in range(len(columns))]
    fields = [
        part[0] * LANES + part[1],
        part[2] + part[3] + part[4],
        part[5] + part[6],
    ]
    fields = [jnp.transpose(f) for f in fields]
    each = capacity // LANES
    for peer in range(peers):
        for q, field in enumerate(fields):
            out_ref[peer, q * each : (q + 1) * each, :] = field[peer * each : (peer + 1) * each]


def pilot_body(pilot_ref, spot_ref, slots_ref):
    peers = slots_ref.shape[0]
    blocks_x = pilot_ref.shape[0] // 4
    pilots = pilot_ref.shape[0] * pilot_ref.shape[1] // 8
    pilot = jnp.concatenate([pilot_ref[4 * r : 4 * r + 1, :] for r in range(blocks_x)], axis=0)
    owner = lax.div(pilot, jnp.int32(pilots))
    slot = pilot - owner * pilots
    first = (lane_iota(blocks_x) & 1) == 0
    owner = jnp.where(first, owner, -1)
    rank = ranks(owner, peers)
    spot_ref[...] = jnp.where(first, owner * LANES + rank, -1)
    left, high, low = [], [], []
    peer_at, lanes_at = row_iota(peers), row_iota(LANES)
    for r in range(blocks_x):
        left.append(jnp.where(peer_at == owner[r : r + 1], 1.0, 0.0).astype(jnp.bfloat16))
        hit = lanes_at == rank[r : r + 1]
        number = slot[r : r + 1]
        high.append(picked(hit, lax.shift_right_logical(number, LANE_BITS).astype(jnp.float32)))
        low.append(picked(hit, (number & (LANES - 1)).astype(jnp.float32)))
    left = jnp.concatenate(left, axis=1)
    slots_ref[...] = mm(left, jnp.concatenate(high, axis=1), NT) * LANES + mm(
        left, jnp.concatenate(low, axis=1), NT
    )


def source_body(
    each, got_ref, conductivity_ref, storage_ref, state_ref, out_ref, near_ref, far_ref
):
    peers = got_ref.shape[0]
    nz, nx = state_ref.shape[0], state_ref.shape[1]
    cells = nz * nx
    one = jnp.ones((TILE, LANES), jnp.bfloat16)

    def sixteen(group, q):
        peer, row = divmod(group * TILE, each)
        if each >= TILE:
            return got_ref[peer, q * each + row : q * each + row + TILE, :]
        return jnp.concatenate(
            [got_ref[peer + i, q * each : (q + 1) * each, :] for i in range(TILE // each)], axis=0
        )

    total = None
    for group in range(peers * each // TILE):
        cell = sixteen(group, 0).astype(jnp.int32)
        high = lax.shift_right_logical(cell, LANE_BITS)
        low = cell & (LANES - 1)
        at_row = jnp.concatenate(
            [
                filled16(hits16(cells, spread16(high.astype(jnp.float32), r)), one)
                for r in range(TILE)
            ],
            axis=1,
        )
        heads = []
        if group == 0:
            state = jnp.transpose(state_ref[...].reshape(cells, LANES))
            lines = mm(
                jnp.concatenate([p.astype(jnp.bfloat16) for p in pieces_of(state)], axis=0), at_row
            )
            for r in range(TILE):
                line = lines[:, r * LANES : (r + 1) * LANES]
                line = line[:LANES] + line[LANES : 2 * LANES] + line[2 * LANES :]
                hit = row_iota(LANES) == low[r : r + 1]
                heads.append(jnp.sum(jnp.where(hit, line, 0.0), axis=0, keepdims=True))
        for r in range(0, 0 if heads else TILE, 8):
            head = jnp.zeros((8, LANES), jnp.float32)
            for z in range(nz):
                for x in range(nx):
                    line = jnp.broadcast_to(state_ref[z, x : x + 1, :], (8, LANES))
                    line = jnp.take_along_axis(line, low[r : r + 8], axis=1)
                    head = jnp.where(high[r : r + 8] == z * nx + x, line, head)
            heads.append(head)
        misfit = sixteen(group, 2) * (jnp.concatenate(heads, axis=0) - sixteen(group, 1))
        pieces = halves_of(misfit)
        low = low.astype(jnp.float32)
        at_lane = [[] for _ in pieces]
        for r in range(TILE):
            masks = hits16(LANES, spread16(low, r))
            for q, piece in enumerate(pieces):
                at_lane[q].append(filled16(masks, spread16(piece, r)))
        at_lane = jnp.concatenate([jnp.concatenate(q, axis=1) for q in at_lane], axis=0)
        part = mm(at_lane, at_row, NT)
        total = part if total is None else total + part
    total = jnp.transpose(total[:LANES] + total[LANES:])
    out_ref[...] = total.reshape(nz, nx, LANES)
    even = (lax.axis_index("cols") & 1) == 0
    total = total.reshape(nz, nx, LANES)
    at = lax.broadcasted_iota(jnp.int32, (nz, HALO, LANES), 1)
    for f, field in enumerate((conductivity_ref, storage_ref, total)):
        low, high = field[:, :HALO, :], field[:, nx - HALO :, :]
        if f == 1:
            low = jnp.where(at == HALO - 1, state_ref[:, :1, :], low)
            high = jnp.where(at == 0, state_ref[:, nx - 1 :, :], high)
        near_ref[f] = jnp.where(even, high, low)
        far_ref[f] = jnp.where(even, low, high)


def all_sum(x):
    while x.ndim > 2:
        x = jnp.sum(x, axis=0)
    return jnp.sum(jnp.sum(x, axis=0, keepdims=True), axis=1, keepdims=True)


def safe_ratio(a, b):
    return jnp.where(b > 0.0, a / jnp.where(b > 0.0, b, 1.0), 0.0)


def pack_body(low_side, *refs):
    *fields, near_ref, far_ref, out_ref = refs
    even = (lax.axis_index("cols") & 1) == 0
    nz, nx = fields[0].shape[0], fields[0].shape[1]
    lanes = lane_iota(2 * (nx + 2 * HALO))
    tall = jnp.zeros(lanes.shape, jnp.float32)
    for pair in range(2):
        for z in range(nz):
            at = (pair * nz + z) * HALO
            x = jnp.concatenate(
                [
                    part
                    for f in (2 * pair, 2 * pair + 1)
                    for part in (
                        jnp.where(even, far_ref[EDGE[f], z], near_ref[EDGE[f], z]),
                        fields[f][z],
                        jnp.where(even, near_ref[EDGE[f], z], far_ref[EDGE[f], z]),
                    )
                ],
                axis=0,
            )
            if low_side is None:
                shift = (at + jnp.where(lax.axis_index("rows") == 0, HALO, 0)) & (LANES - 1)
            else:
                shift = at if low_side else (at + HALO) & (LANES - 1)
            x = pltpu.roll(x, shift, 1)
            tall = jnp.where((lanes >= at) & (lanes < at + HALO), x, tall)
    rest = LANES - tall.shape[0]
    tall = jnp.concatenate([tall, jnp.zeros((rest, LANES), jnp.float32)], axis=0)
    out_ref[...] = jnp.transpose(tall).reshape(out_ref.shape)


def joined(a, b):
    return jnp.where((a > 0.0) & (b > 0.0), 0.5 * (a + b), 0.0)


def right(x):
    return pltpu.roll(x, x.shape[1] - 1, 1)


def left(x):
    return pltpu.roll(x, 1, 1)


def fore(x):
    return pltpu.roll(x, x.shape[0] - 1, 0)


def back(x):
    return pltpu.roll(x, 1, 0)


def unpack(f, own, other, edges, padded, top=0):
    nz, nx = own.shape[0], own.shape[1]
    layer, even = lax.axis_index("layers"), (lax.axis_index("cols") & 1) == 0
    after = pl.multiple_of(jnp.where(even, top + HALO + nx, top), HALO)
    before = pl.multiple_of(jnp.where(even, top, top + HALO + nx), HALO)
    for half, block in ((0, own), (1, other)):
        near, far = edges[2 * half], edges[2 * half + 1]
        for i in range(nz):
            j = jnp.where(layer == 0, i, nz - 1 - i)
            to = half * nz + i
            padded[to, top + HALO : top + HALO + nx, :] = block[j]
            padded[to, pl.ds(after, HALO), :] = near[EDGE[f], j]
            padded[to, pl.ds(before, HALO), :] = far[EDGE[f], j]


def prepare_body(*refs):
    own, other, edges = refs[:3], refs[3:6], refs[6:10]
    c_pad, diag, wx, wx_back, wy, wz, grads, outer, s_pad, h_pad = refs[10:]
    nz, nx = own[0].shape[0], own[0].shape[1]
    planes, width = c_pad.shape[0], c_pad.shape[1]
    for f, target in enumerate((c_pad, s_pad, h_pad)):
        unpack(f, own[f], other[f], edges, target)
    none = jnp.zeros((1, LANES), jnp.float32)
    for z in range(planes):
        h_pad[z, HALO - 1 : HALO, :] = s_pad[z, :1, :]
        h_pad[z, width - HALO : width - HALO + 1, :] = s_pad[z, width - 1 :, :]
        s_pad[z, :1, :] = none
        s_pad[z, width - 1 :, :] = none
    lanes = lane_iota(width)
    last = lanes == LANES - 1
    for z in range(planes):
        c = c_pad[z]
        cf, cr = fore(c), jnp.where(last, 0.0, right(c))
        total = cf + back(c) + cr + jnp.where(lanes == 0, 0.0, left(c))
        wx[z] = joined(c, cf)
        wx_back[z] = joined(c, back(c))
        wy[z] = joined(c, cr)
        if z + 1 < planes:
            wz[z] = joined(c, c_pad[z + 1])
            total = total + c_pad[z + 1]
        if z:
            total = total + c_pad[z - 1]
        diag[z] = s_pad[z] + 3.0 * c + 0.5 * total

    span = HALO + nx
    rows, lanes = row_iota(width), lane_iota(width)
    mine = (rows >= HALO) & (rows < span)
    before = (rows >= HALO - 1) & (rows < span - 1)
    odd = (lanes & 1) == 1
    inside = mine & (lanes < LANES - 1)

    def kept(mask, x):
        return jnp.where(mask, x, 0.0)[:span]

    for z in range(nz):
        c, h = -0.5 * c_pad[z], h_pad[z]
        fall = h - fore(h)
        grads[0, z] = kept(mine, c * fall)
        grads[1, z] = kept(before, fore(c) * fall)
        fall = h - right(h)
        following = right(c) * fall
        grads[2, z] = kept(inside, c * fall + jnp.where(odd, 0.0, following))
        grads[3, z] = kept(inside & odd, following)
        weight = c + -0.5 * c_pad[z + 1] if z + 1 < nz else c
        grads[4, z] = kept(mine, weight * (h - h_pad[z + 1]))
        grads[5, z] = kept(mine & ((lanes == 0) | (lanes == LANES - 1)), c * h)
    outer[...] = kept(mine, -0.5 * c_pad[0] * h_pad[0])


def basis_body(peers, side_count, *refs):
    c_pad, diag_in, wx, wx_back, wy, wz, grads, outer = refs[:8]
    b_own, b_other, edges, refs = refs[8], refs[9], refs[10:14], refs[14:]
    sides = list(zip(refs[:side_count], refs[side_count : 2 * side_count]))
    spot_ref, slots_ref, own_ref, send_ref = refs[2 * side_count : 2 * side_count + 4]
    diag, ws, edge_grads, image, basis = refs[2 * side_count + 4 :]
    layer, row = lax.axis_index("layers"), lax.axis_index("rows")
    nz, nx = b_own.shape[0], b_own.shape[1]
    planes, width = c_pad.shape[0], c_pad.shape[1]
    span = HALO + nx
    inner = slice(HALO, span)
    top = HALO
    body = slice(top, top + width)
    for k in range(ITERS):
        for z in range(planes):
            basis[k, z, :top, :] = jnp.zeros((top, LANES), jnp.float32)
            basis[k, z, top + width :, :] = jnp.zeros((top, LANES), jnp.float32)
    unpack(3, b_own, b_other, edges, basis.at[0], top)

    lanes, rows = lane_iota(width), row_iota(width)
    y_at = lanes & (HALO - 1)
    if side_count == 1:
        meetings = [(jnp.where(row == 0, LANES - 1, 0), jnp.where(row == 0, 0, HALO - 1))]
    else:
        meetings = [(0, HALO - 1), (LANES - 1, 0)]
    strips = []
    for (here, there), (edge, meet) in zip(sides, meetings):
        halves = [jnp.transpose(x[...].reshape(LANES, LANES)) for x in (here, there)]
        first = jnp.where(layer == 0, halves[0], halves[1])
        second = jnp.where(layer == 0, halves[1], halves[0])
        fields = []
        for f in range(4):
            part = slice((f % 2) * width, (f % 2 + 1) * width)
            half = LANES // 2
            fields.append(
                jnp.where(
                    lanes < half,
                    pltpu.roll(first[part], half, 1) if f // 2 else first[part],
                    second[part] if f // 2 else pltpu.roll(second[part], half, 1),
                )
            )
        fields[1] = jnp.where((rows == 0) | (rows == width - 1), 0.0, fields[1])
        shifts = []
        for z in range(planes):
            spot = jnp.where(layer == 0, z, planes - 1 - z) * HALO + meet
            shifts.append(
                ((edge - spot) & (LANES - 1), (spot - edge) & (LANES - 1))
            )
        strips.append((fields, lanes == edge, shifts))

    def from_strips(values, z):
        total = jnp.zeros((width, LANES), jnp.float32)
        for (_, at_edge, shifts), value in zip(strips, values):
            total = jnp.where(at_edge, pltpu.roll(value, shifts[z][0], 1), total)
        return total

    def to_strip(strip, value, z):
        _, at_edge, shifts = strip
        if side_count > 1:
            value = jnp.where(at_edge, value, 0.0)
        return pltpu.roll(value, shifts[z][1], 1)

    edge_c = [jnp.zeros((width, LANES), jnp.float32) for _ in strips]
    mine = (rows >= HALO) & (rows < span)
    for z in range(planes):
        c = c_pad[z]
        c_side = from_strips([s[0][0] for s in strips], z)
        ws[z] = joined(c, c_side)
        diag[z] = diag_in[z] + 0.5 * c_side
        for i, strip in enumerate(strips):
            edge_c[i] = edge_c[i] + to_strip(strip, jnp.where(strip[1], c, 0.0), z)
        if z < nz:
            h_side = from_strips([s[0][2] for s in strips], z)
            edge_grads[z] = grads[5, z] + jnp.where(mine, 0.5 * c * h_side, 0.0)[:span]
    strip_terms = []
    for (fields, _, _), beside in zip(strips, edge_c):
        c = fields[0]
        cf = fore(c)
        cr = jnp.where(y_at < HALO - 1, right(c), 0.0)
        cu = jnp.where(lanes < LANES - HALO, pltpu.roll(c, LANES - HALO, 1), 0.0)
        total = cf + back(c) + cr + cu + beside
        total = total + jnp.where(y_at > 0, left(c), 0.0)
        total = total + jnp.where(lanes >= HALO, pltpu.roll(c, HALO, 1), 0.0)
        strip_terms.append(
            (fields[1] + 3.0 * c + 0.5 * total, joined(c, cf), joined(c, cr), joined(c, cu))
        )

    alphas, gammas, norms, sums = [], [], [], []

    def following(k, image_now, now, before):
        u = image_now - alphas[k - 1] * now
        return u - gammas[k - 1] * before if k > 1 else u

    def member(k, z):
        before = basis[k - 2, z, body, :] if k > 1 else None
        u = following(k, image[z], basis[k - 1, z, body, :], before)
        basis[k, z, body, :] = u
        return u

    def folded(x):
        return sum(x[r : r + 8] for r in range(8, width, 8)) + x[:8]

    side_now = [s[0][3] for s in strips]
    side_last, side_image = None, None
    for k in range(ITERS):
        above = member(k, 0) if k else basis[0, 0, body, :]
        v = None
        if k:
            side_next = [
                following(k, side_image[i], side_now[i], side_last[i] if k > 1 else None)
                for i in range(side_count)
            ]
            side_now, side_last = side_next, side_now
        norm = jnp.zeros((8, LANES), jnp.float32)
        energy = jnp.zeros((8, LANES), jnp.float32)
        side_image = []
        final = k == ITERS - 1
        for x, (d, sx, sy, sz) in zip(side_now, strip_terms):
            if final:
                break
            ax = d * x - sx * fore(x) - back(sx * x) - sy * right(x) - left(sy * x)
            ax = ax - sz * pltpu.roll(x, LANES - HALO, 1) - pltpu.roll(sz * x, HALO, 1)
            side_image.append(ax)
        acc = basis[k, 0, top : top + span, :] * outer[...]
        acc_x = jnp.zeros((span, LANES), jnp.float32)
        acc_y = jnp.zeros((span, LANES), jnp.float32)
        for z in range(nz + ITERS - 1 - k):
            below, v = v, above
            above = member(k, z + 1) if k else basis[0, z + 1, body, :]
            side = from_strips(side_now, z)
            vf, vr = basis[k, z, top + 1 : top + 1 + width, :], right(v)
            vb = basis[k, z, top - 1 : top - 1 + width, :]
            wyz, wsz = wy[z], ws[z]
            av = diag[z] * v - wz[z] * above
            if z:
                av = av - wz[z - 1] * below
            av = av - wx[z] * vf - wx_back[z] * vb - wyz * vr - left(wyz * v) - wsz * side
            if final:
                basis[ITERS, z, body, :] = av
            else:
                image[z] = av
                edge = wsz * v
                for i, strip in enumerate(strips):
                    side_image[i] = side_image[i] - to_strip(strip, edge, z)
                norm = norm + folded(v * v)
                energy = energy + folded(v * av)
            if z < nz:
                fall = (v - vf)[:span]
                acc = acc + fall * grads[0, z]
                acc_x = acc_x + fall * grads[1, z]
                fall = (v - vr)[:span]
                acc = acc + fall * grads[2, z]
                acc_y = acc_y + fall * grads[3, z]
                acc = acc + (v - above)[:span] * grads[4, z]
                acc = acc + (v - side)[:span] * edge_grads[z]
                own_ref[k, jnp.where(layer == 0, z, nz - 1 - z)] = v[inner]
        for x, ax in zip(side_now, side_image):
            norm = norm + folded(x * x)
            energy = energy + folded(x * ax)
        sums.append((acc + back(acc_x) + left(acc_y))[inner])
        norm = all_sum(norm) if not final else jnp.zeros((1, 1), jnp.float32)
        alphas.append(safe_ratio(all_sum(energy), norm) if not final else norm)
        gammas.append(safe_ratio(norm, norms[-1]) if k else jnp.zeros_like(norm))
        norms.append(norm)
    own_rows = slice(top + HALO, top + span)

    dots = {}
    for i in range(ITERS + 1):
        for j in range(i + 1):
            acc = basis[i, 0, own_rows, :] * basis[j, 0, own_rows, :]
            for z in range(1, nz):
                acc = acc + basis[i, z, own_rows, :] * basis[j, z, own_rows, :]
            dots[i, j] = dots[j, i] = all_sum(acc)

    def operator(i, j):
        entry = dots[i, j + 1] + alphas[j] * dots[i, j]
        return entry + gammas[j] * dots[i, j - 1] if j else entry

    lanes = lane_iota(1)
    facts = []
    for j in range(ITERS):
        row_facts = [0.5 * (operator(j, m) + operator(m, j)) for m in range(ITERS)]
        row_facts += [alphas[j], gammas[j], norms[j], dots[j, 0]]
        entries = jnp.zeros((1, LANES), jnp.float32)
        for place, entry in enumerate(row_facts):
            entries = jnp.where(lanes == FACTS + place, entry, entries)
        facts.append(entries)

    blocks_x = nx // 4
    four = jnp.where(
        lax.shift_right_logical(lane_iota(blocks_x, nx), 2) == row_iota(blocks_x, nx), 1.0, 0.0
    )
    sums = mm(four, jnp.concatenate(sums, axis=1), precision=EXACT)
    spot = [spot_ref[r : r + 1, :] for r in range(blocks_x)]
    lane_hits = jnp.concatenate(
        [
            jnp.where(row_iota(LANES) == (p & (LANES - 1)), 1.0, 0.0).astype(jnp.bfloat16)
            for p in spot
        ],
        axis=1,
    )
    peer_at = row_iota(peers)
    row_hit = [(p >= 0) & (peer_at == lax.shift_right_arithmetic(p, LANE_BITS)) for p in spot]
    values = []
    for k in range(ITERS):
        pair = sums[:, k * LANES : (k + 1) * LANES]
        pair = pair + pltpu.roll(pair, LANES - 1, 1)
        for p in pieces_of(pair):
            values.append(
                jnp.concatenate(
                    [picked(row_hit[r], p[r : r + 1]) for r in range(blocks_x)], axis=1
                )
            )
    dense = mm(jnp.concatenate(values, axis=0), lane_hits, NT)
    copies = send_ref.shape[0] // peers
    for k in range(ITERS):
        at = 3 * k * peers
        rows = dense[at : at + peers] + dense[at + peers : at + 2 * peers]
        rows = rows + dense[at + 2 * peers : at + 3 * peers]
        rows = jnp.where(lane_iota(peers) < FACTS, rows, facts[k])
        if k < 2:
            slots = pltpu.roll(slots_ref[...], (1 - k) * (LANES - SLOTS) + FACTS, 1)
            rows = jnp.where(lane_iota(peers) < SLOTS, rows, slots)
        for peer in range(peers):
            for copy in range(copies):
                send_ref[peer * copies + copy, k : k + 1, :] = rows[peer : peer + 1]


def solve_body(copies, got_ref, own_ref, adjoint_ref, pilot_ref):
    senders = got_ref.shape[0]
    peers = senders // copies
    groups = senders * ITERS // LANES
    got = got_ref[...].reshape(groups, LANES, LANES)
    turned = [jnp.transpose(got[g])[FACTS:SLOTS] for g in range(groups)]

    def fact(place):
        return jnp.concatenate([t[place : place + 1] for t in turned], axis=0)

    alpha, gamma, weight, rhs = (fact(ITERS + place) for place in range(4))
    at = lane_iota(groups) & (ITERS - 1)
    gamma_next = jnp.where(at < ITERS - 1, pltpu.roll(gamma, LANES - 1, 1), 0.0)

    def over_senders(x):
        for shift in (8, 16, 32, 64):
            x = x + pltpu.roll(x, shift, 1)
        return jnp.sum(x, axis=0, keepdims=True)

    norm = over_senders(weight)
    means = safe_ratio(over_senders(weight * alpha), norm)
    growth = safe_ratio(norm, pltpu.roll(norm, 1, 1))
    now = jnp.where(at == 0, 1.0, 0.0)
    last = None
    common = [now]
    for k in range(ITERS - 1):
        image = jnp.where(at > 0, pltpu.roll(now, 1, 1), 0.0) + alpha * now
        image = image + gamma_next * pltpu.roll(now, LANES - 1, 1)
        following = image - means[:, k : k + 1] * now
        if k:
            following = following - growth[:, k : k + 1] * last
        now, last = following, now
        common.append(now)

    lanes = lane_iota(ITERS)
    system = jnp.zeros((ITERS, LANES), jnp.float32)
    stacked = []
    per = LANES // ITERS
    for g in range(groups):
        t = jnp.concatenate([c[g : g + 1] for c in common], axis=0)
        stacked.append(t)
        blocks = []
        for i in range(per):
            block = pltpu.roll(got_ref[g * per + i], (ITERS * i - FACTS) % LANES, 1)
            blocks.append(
                jnp.where((lanes >= ITERS * i) & (lanes < ITERS * (i + 1)), block, 0.0)
            )
        image = mm(t, jnp.concatenate(blocks, axis=0), precision=EXACT)
        beside = jnp.concatenate(
            [image, rhs[g : g + 1], jnp.zeros((LANES - ITERS - 1, LANES), jnp.float32)], axis=0
        )
        system = system + mm(t, beside, NT, precision=EXACT)
    rows = row_iota(ITERS)
    for p in range(ITERS):
        pivot = system[p : p + 1, p : p + 1]
        inverse = jnp.where(pivot > 0.0, 1.0 / jnp.where(pivot > 0.0, pivot, 1.0), 0.0)
        pivot_row = system[p : p + 1] * inverse
        system = jnp.where(rows == p, pivot_row, system - system[:, p : p + 1] * pivot_row)
    answer = system[:, ITERS : ITERS + 1]

    weights = [jnp.sum(answer * t, axis=0, keepdims=True) for t in stacked]
    me = lax.axis_index(GRID_AXES)
    mine = []
    for k in range(ITERS):
        w = jnp.zeros((1, 1), jnp.float32)
        for g in range(groups):
            hit = lane_iota(1) == me * ITERS + k - g * LANES
            w = w + jnp.sum(jnp.where(hit, weights[g], 0.0), axis=1, keepdims=True)
        mine.append(w)
    for z in range(own_ref.shape[1]):
        acc = mine[0] * own_ref[0, z]
        for k in range(1, ITERS):
            acc = acc + mine[k] * own_ref[k, z]
        adjoint_ref[z] = acc

    per_group = LANES // ITERS // copies
    sender = lax.div(lane_iota(per_group), jnp.int32(ITERS * copies))
    values = jnp.concatenate(
        [
            mm(jnp.where(sender == row_iota(per_group), weights[g], 0.0), got[g], precision=EXACT)
            for g in range(groups)
        ],
        axis=0,
    )
    rows_at, lanes_at = row_iota(pilot_ref.shape[0]), row_iota(LANES)
    held = lane_iota(peers) < pilot_ref.shape[0] * LANES // peers
    pieces = pieces_of(jnp.where(held, values, 0.0))
    left, right = [[], [], []], []
    room = LANES - SLOTS
    for s in range(peers):
        slot = jnp.where(
            lane_iota(1) < room,
            pltpu.roll(got_ref[s * copies, 0:1, :], room, 1),
            pltpu.roll(got_ref[s * copies, 1:2, :], 2 * room, 1),
        ).astype(jnp.int32)
        hit = rows_at == lax.shift_right_logical(slot, LANE_BITS)
        for q, piece in enumerate(pieces):
            left[q].append(picked(hit, piece[s : s + 1]))
        right.append(
            jnp.where(lanes_at == (slot & (LANES - 1)), 1.0, 0.0).astype(jnp.bfloat16)
        )
    right = jnp.concatenate(right, axis=1)
    pilot_ref[...] = sum(mm(jnp.concatenate(q, axis=1), right, NT) for q in left)


def tied(*values):
    return lax.optimization_barrier(values)


def neighbour_pairs(axis):
    forward = [(i, i + 1) for i in range(lax.axis_size(axis) - 1)]
    return forward, [(b, a) for a, b in forward]


def swap_pairs(axis, first):
    pairs = [(i, i + 1) for i in range(first, lax.axis_size(axis) - 1, 2)]
    return pairs + [(b, a) for a, b in pairs]


def swapped(x):
    return lax.ppermute(x, "layers", [(0, 1), (1, 0)])


def on_device(
    state_field,
    conductivity,
    storage,
    gauge_owner,
    gauge_cell,
    gauge_value,
    gauge_weight,
    pilot_index,
):
    nz, nx, ny = state_field.shape
    peers = lax.axis_size("cols") * lax.axis_size("rows")
    devices = peers * lax.axis_size("layers")
    gauges = gauge_owner.shape[0]
    capacity = 4 * gauges // peers
    f32 = jnp.float32
    row_count = lax.axis_size("rows")

    def shape(*dims, dtype=f32):
        return jax.ShapeDtypeStruct(dims, dtype)

    def flat(x):
        return x.reshape(gauges // LANES, LANES)

    obs = pltpu.VMEM((gauges // LANES, LANES), f32)
    obs_int = pltpu.VMEM((gauges // LANES, LANES), jnp.int32)
    payload = kernel_call(
        functools.partial(route_body, peers, capacity),
        shape(peers, 3 * capacity // LANES, LANES),
        [obs_int, obs_int, obs, obs, pltpu.SemaphoreType.DMA((4,))],
        weight=5,
        vmem=64 * 1024 * 1024,
    )(in_specs=[HBM] * 4, out_specs=VMEM)(
        flat(gauge_owner), flat(gauge_cell), flat(gauge_value), flat(gauge_weight)
    )
    payload, pilot_index = tied(payload, pilot_index)
    got = lax.all_to_all(payload, PEER_AXES, 0, 0, tiled=True)
    spot, slots = kernel_call(
        pilot_body, (shape(nx // 4, LANES, dtype=jnp.int32), shape(peers, LANES))
    )(in_specs=[VMEM], out_specs=(VMEM, VMEM))(pilot_index)

    fixed = (conductivity, storage, state_field)
    got, spot, *fixed_other = tied(got, spot, *(swapped(x) for x in fixed))
    edge = shape(3, nz, HALO, LANES)
    source, near, far = kernel_call(
        functools.partial(source_body, capacity // LANES),
        (shape(nz, nx, LANES), edge, edge),
        weight=6,
    )(in_specs=[VMEM] * 4, out_specs=(VMEM,) * 3)(got, *fixed)
    near = lax.ppermute(near, "cols", swap_pairs("cols", 0))
    far = lax.ppermute(far, "cols", swap_pairs("cols", 1))
    other = swapped(source)

    def packed(low_side):
        return kernel_call(
            functools.partial(pack_body, low_side), shape(2 * nz, HALO, LANES)
        )(in_specs=[VMEM] * 6, out_specs=VMEM)(*fixed, source, near, far)

    if row_count == 2:
        send = [(packed(None), [(0, 1), (1, 0)])]
    else:
        forward, backward = neighbour_pairs("rows")
        send = [(packed(False), forward), (packed(True), backward)]
    edges = tied(near, far, swapped(near), swapped(far), *(x for x, _ in send))[:4]
    sides = [lax.ppermute(x, "rows", pairs) for x, pairs in send]
    planes, width, span = 2 * nz, nx + 2 * HALO, nx + HALO
    padded = (planes, width, LANES)
    prepared = kernel_call(
        prepare_body,
        (*(shape(*padded) for _ in range(6)), shape(6, nz, span, LANES), shape(span, LANES)),
        [pltpu.VMEM(padded, f32)] * 2,
        weight=3,
    )(in_specs=[VMEM] * 10, out_specs=(VMEM,) * 8)(*fixed, *fixed_other, *edges)
    *sides, prepared = tied(*sides, prepared)
    sides = sides + [swapped(x) for x in sides]

    each = nx * ny // 8 // LANES
    own, send = kernel_call(
        functools.partial(basis_body, peers, len(sides) // 2),
        (shape(ITERS, nz, nx, LANES), shape(devices, ITERS, LANES)),
        [
            pltpu.VMEM(padded, f32),
            pltpu.VMEM(padded, f32),
            pltpu.VMEM((nz, span, LANES), f32),
            pltpu.VMEM(padded, f32),
            pltpu.VMEM((ITERS + 1, planes, width + 2 * HALO, LANES), f32),
        ],
        weight=10,
    )(in_specs=[VMEM] * (16 + len(sides)), out_specs=(VMEM, VMEM))(
        *prepared, source, other, *edges, *sides, spot, slots
    )
    parts = lax.all_to_all(send, GRID_AXES, 0, 0, tiled=True)
    adjoint, pilot = kernel_call(
        functools.partial(solve_body, devices // peers), (shape(nz, nx, ny), shape(each, LANES))
    )(in_specs=[VMEM] * 2, out_specs=(VMEM, VMEM))(parts, own)
    return adjoint, pilot.reshape(-1)


def solution(mesh):
    return jax.shard_map(
        on_device,
        mesh=mesh,
        in_specs=(
            P(("groups", "layers"), "cols", "rows"),
            P(("groups", "layers"), "cols", "rows"),
            P(("groups", "layers"), "cols", "rows"),
            P(("groups", "cols", "rows", "layers")),
            P(("groups", "cols", "rows", "layers")),
            P(("groups", "cols", "rows", "layers")),
            P(("groups", "cols", "rows", "layers")),
            P("cols", "rows"),
        ),
        out_specs=(P(("groups", "layers"), "cols", "rows"), P(("groups", "cols", "rows"))),
        check_vma=False,
    )
```

```python
import functools

import jax
import jax.numpy as jnp
from jax import lax
from jax.experimental import pallas as pl
from jax.experimental.pallas import tpu as pltpu
from jax.sharding import PartitionSpec as P

ITERS = 8
HALO = 8
EDGE = (0, 1, 1, 2)
FACTS = 64
SLOTS = 96
LANES = 128
LANE_BITS = 7
GRID_AXES = ("cols", "rows", "layers")
PEER_AXES = ("cols", "rows")
NT = (((1,), (1,)), ((), ()))
EXACT = lax.Precision.HIGHEST
VMEM_BYTES = 24 * 1024 * 1024


def kernel_call(body, out_shape, scratch=(), weight=1, vmem=VMEM_BYTES):
    return functools.partial(
        pl.pallas_call,
        body,
        out_shape=out_shape,
        scratch_shapes=list(scratch),
        compiler_params=pltpu.CompilerParams(vmem_limit_bytes=vmem),
        cost_estimate=pl.CostEstimate(
            flops=0, bytes_accessed=weight * 3_000_000, transcendentals=0
        ),
    )


VMEM = pl.BlockSpec(memory_space=pltpu.VMEM)
HBM = pl.BlockSpec(memory_space=pltpu.HBM)


def pieces_of(x):
    first = x.astype(jnp.bfloat16).astype(jnp.float32)
    rest = x - first
    second = rest.astype(jnp.bfloat16).astype(jnp.float32)
    return first, second, rest - second


def halves_of(x):
    first = x.astype(jnp.bfloat16).astype(jnp.float32)
    return first, x - first


def row_iota(rows, lanes=LANES):
    return lax.broadcasted_iota(jnp.int32, (rows, lanes), 0)


def lane_iota(rows, lanes=LANES):
    return lax.broadcasted_iota(jnp.int32, (rows, lanes), 1)


def picked(mask, row):
    return jnp.where(mask, row, jnp.zeros_like(row)).astype(jnp.bfloat16)


TILE = 16


def spread16(x, r):
    return jnp.broadcast_to(x[r : r + 1], (TILE, LANES)).astype(jnp.bfloat16)


def hits16(count, row):
    at = row_iota(TILE).astype(jnp.float32).astype(jnp.bfloat16)
    return [at + jnp.bfloat16(TILE * i) == row for i in range(count // TILE)]


def filled16(masks, value):
    zero = jnp.zeros((TILE, LANES), jnp.bfloat16)
    return jnp.concatenate([jnp.where(m, value, zero) for m in masks], axis=0)


def mm(a, b, dims=(((1,), (0,)), ((), ())), precision=None):
    return lax.dot_general(a, b, dims, precision=precision, preferred_element_type=jnp.float32)


def ranks(owner, peers):
    rows = owner.shape[0]
    ra, ca = row_iota(LANES, 2 * LANES), lane_iota(LANES, 2 * LANES)
    earlier_lane = jnp.where((ra < ca) | (ca >= LANES), 1.0, 0.0).astype(jnp.bfloat16)
    earlier_row = jnp.where(row_iota(rows, rows) > lane_iota(rows, rows), 1.0, 0.0).astype(
        jnp.bfloat16
    )
    hits = [owner == peer for peer in range(peers)]
    ones = jnp.concatenate([jnp.where(h, 1.0, 0.0).astype(jnp.bfloat16) for h in hits], axis=0)
    counts = mm(ones, earlier_lane)
    part = [counts[p * rows : (p + 1) * rows] for p in range(peers)]
    before = mm(
        earlier_row, jnp.concatenate([c[:, LANES:] for c in part], axis=1).astype(jnp.bfloat16)
    )
    rank = jnp.zeros((rows, LANES), jnp.float32)
    for p in range(peers):
        rank = jnp.where(
            hits[p], part[p][:, :LANES] + before[:, p * LANES : (p + 1) * LANES], rank
        )
    return rank.astype(jnp.int32)


def route_body(
    peers, capacity, owner_hbm, cell_hbm, value_hbm, weight_hbm, out_ref,
    owner_ref, cell_ref, value_ref, weight_ref, sems,
):
    copies = [
        pltpu.make_async_copy(source, target, sems.at[i])
        for i, (source, target) in enumerate(
            (
                (owner_hbm, owner_ref),
                (cell_hbm, cell_ref),
                (value_hbm, value_ref),
                (weight_hbm, weight_ref),
            )
        )
    ]
    for copy in copies:
        copy.start()
    copies[0].wait()
    rows = owner_ref.shape[0]
    owner = owner_ref[...]
    position = owner * capacity + ranks(owner, peers)
    for copy in copies[1:]:
        copy.wait()
    slot_row = lax.shift_right_logical(position, LANE_BITS).astype(jnp.float32)
    slot_lane = (position & (LANES - 1)).astype(jnp.float32)
    cell = cell_ref[...]
    columns = [
        lax.shift_right_logical(cell, LANE_BITS).astype(jnp.float32),
        (cell & (LANES - 1)).astype(jnp.float32),
        *pieces_of(value_ref[...]),
        *halves_of(weight_ref[...]),
    ]
    slot_rows = peers * capacity // LANES
    one = jnp.ones((TILE, LANES), jnp.bfloat16)
    total = None
    for start in range(0, rows, TILE):
        at_row, at_lane = [], [[] for _ in columns]
        for r in range(start, start + TILE):
            at_row.append(filled16(hits16(slot_rows, spread16(slot_row, r)), one))
            masks = hits16(LANES, spread16(slot_lane, r))
            for q, column in enumerate(columns):
                at_lane[q].append(filled16(masks, spread16(column, r)))
        at_lane = jnp.concatenate([jnp.concatenate(q, axis=1) for q in at_lane], axis=0)
        part = mm(at_lane, jnp.concatenate(at_row, axis=1), NT)
        total = part if total is None else total + part
    part = [total[q * LANES : (q + 1) * LANES] for q in range(len(columns))]
    fields = [
        part[0] * LANES + part[1],
        part[2] + part[3] + part[4],
        part[5] + part[6],
    ]
    fields = [jnp.transpose(f) for f in fields]
    each = capacity // LANES
    for peer in range(peers):
        for q, field in enumerate(fields):
            out_ref[peer, q * each : (q + 1) * each, :] = field[peer * each : (peer + 1) * each]


def pilot_body(pilot_ref, spot_ref, slots_ref):
    peers = slots_ref.shape[0]
    blocks_x = pilot_ref.shape[0] // 4
    pilots = pilot_ref.shape[0] * pilot_ref.shape[1] // 8
    pilot = jnp.concatenate([pilot_ref[4 * r : 4 * r + 1, :] for r in range(blocks_x)], axis=0)
    owner = lax.div(pilot, jnp.int32(pilots))
    slot = pilot - owner * pilots
    first = (lane_iota(blocks_x) & 1) == 0
    owner = jnp.where(first, owner, -1)
    rank = ranks(owner, peers)
    spot_ref[...] = jnp.where(first, owner * LANES + rank, -1)
    left, high, low = [], [], []
    peer_at, lanes_at = row_iota(peers), row_iota(LANES)
    for r in range(blocks_x):
        left.append(jnp.where(peer_at == owner[r : r + 1], 1.0, 0.0).astype(jnp.bfloat16))
        hit = lanes_at == rank[r : r + 1]
        number = slot[r : r + 1]
        high.append(picked(hit, lax.shift_right_logical(number, LANE_BITS).astype(jnp.float32)))
        low.append(picked(hit, (number & (LANES - 1)).astype(jnp.float32)))
    left = jnp.concatenate(left, axis=1)
    slots_ref[...] = mm(left, jnp.concatenate(high, axis=1), NT) * LANES + mm(
        left, jnp.concatenate(low, axis=1), NT
    )


def source_body(
    each, got_ref, conductivity_ref, storage_ref, state_ref, out_ref, near_ref, far_ref
):
    peers = got_ref.shape[0]
    nz, nx = state_ref.shape[0], state_ref.shape[1]
    cells = nz * nx
    one = jnp.ones((TILE, LANES), jnp.bfloat16)

    def sixteen(group, q):
        peer, row = divmod(group * TILE, each)
        if each >= TILE:
            return got_ref[peer, q * each + row : q * each + row + TILE, :]
        return jnp.concatenate(
            [got_ref[peer + i, q * each : (q + 1) * each, :] for i in range(TILE // each)], axis=0
        )

    total = None
    for group in range(peers * each // TILE):
        cell = sixteen(group, 0).astype(jnp.int32)
        high = lax.shift_right_logical(cell, LANE_BITS)
        low = cell & (LANES - 1)
        at_row = jnp.concatenate(
            [
                filled16(hits16(cells, spread16(high.astype(jnp.float32), r)), one)
                for r in range(TILE)
            ],
            axis=1,
        )
        heads = []
        if group == 0:
            state = jnp.transpose(state_ref[...].reshape(cells, LANES))
            lines = mm(
                jnp.concatenate([p.astype(jnp.bfloat16) for p in pieces_of(state)], axis=0), at_row
            )
            for r in range(TILE):
                line = lines[:, r * LANES : (r + 1) * LANES]
                line = line[:LANES] + line[LANES : 2 * LANES] + line[2 * LANES :]
                hit = row_iota(LANES) == low[r : r + 1]
                heads.append(jnp.sum(jnp.where(hit, line, 0.0), axis=0, keepdims=True))
        for r in range(0, 0 if heads else TILE, 8):
            head = jnp.zeros((8, LANES), jnp.float32)
            for z in range(nz):
                for x in range(nx):
                    line = jnp.broadcast_to(state_ref[z, x : x + 1, :], (8, LANES))
                    line = jnp.take_along_axis(line, low[r : r + 8], axis=1)
                    head = jnp.where(high[r : r + 8] == z * nx + x, line, head)
            heads.append(head)
        misfit = sixteen(group, 2) * (jnp.concatenate(heads, axis=0) - sixteen(group, 1))
        pieces = halves_of(misfit)
        low = low.astype(jnp.float32)
        at_lane = [[] for _ in pieces]
        for r in range(TILE):
            masks = hits16(LANES, spread16(low, r))
            for q, piece in enumerate(pieces):
                at_lane[q].append(filled16(masks, spread16(piece, r)))
        at_lane = jnp.concatenate([jnp.concatenate(q, axis=1) for q in at_lane], axis=0)
        part = mm(at_lane, at_row, NT)
        total = part if total is None else total + part
    total = jnp.transpose(total[:LANES] + total[LANES:])
    out_ref[...] = total.reshape(nz, nx, LANES)
    even = (lax.axis_index("cols") & 1) == 0
    total = total.reshape(nz, nx, LANES)
    at = lax.broadcasted_iota(jnp.int32, (nz, HALO, LANES), 1)
    for f, field in enumerate((conductivity_ref, storage_ref, total)):
        low, high = field[:, :HALO, :], field[:, nx - HALO :, :]
        if f == 1:
            low = jnp.where(at == HALO - 1, state_ref[:, :1, :], low)
            high = jnp.where(at == 0, state_ref[:, nx - 1 :, :], high)
        near_ref[f] = jnp.where(even, high, low)
        far_ref[f] = jnp.where(even, low, high)


def all_sum(x):
    while x.ndim > 2:
        x = jnp.sum(x, axis=0)
    return jnp.sum(jnp.sum(x, axis=0, keepdims=True), axis=1, keepdims=True)


def safe_ratio(a, b):
    return jnp.where(b > 0.0, a / jnp.where(b > 0.0, b, 1.0), 0.0)


def pack_body(low_side, *refs):
    *fields, near_ref, far_ref, out_ref = refs
    even = (lax.axis_index("cols") & 1) == 0
    nz, nx = fields[0].shape[0], fields[0].shape[1]
    lanes = lane_iota(2 * (nx + 2 * HALO))
    tall = jnp.zeros(lanes.shape, jnp.float32)
    for pair in range(2):
        for z in range(nz):
            at = (pair * nz + z) * HALO
            x = jnp.concatenate(
                [
                    part
                    for f in (2 * pair, 2 * pair + 1)
                    for part in (
                        jnp.where(even, far_ref[EDGE[f], z], near_ref[EDGE[f], z]),
                        fields[f][z],
                        jnp.where(even, near_ref[EDGE[f], z], far_ref[EDGE[f], z]),
                    )
                ],
                axis=0,
            )
            if low_side is None:
                shift = (at + jnp.where(lax.axis_index("rows") == 0, HALO, 0)) & (LANES - 1)
            else:
                shift = at if low_side else (at + HALO) & (LANES - 1)
            x = pltpu.roll(x, shift, 1)
            tall = jnp.where((lanes >= at) & (lanes < at + HALO), x, tall)
    rest = LANES - tall.shape[0]
    tall = jnp.concatenate([tall, jnp.zeros((rest, LANES), jnp.float32)], axis=0)
    out_ref[...] = jnp.transpose(tall).reshape(out_ref.shape)


def joined(a, b):
    return jnp.where((a > 0.0) & (b > 0.0), 0.5 * (a + b), 0.0)


def right(x):
    return pltpu.roll(x, x.shape[1] - 1, 1)


def left(x):
    return pltpu.roll(x, 1, 1)


def fore(x):
    return pltpu.roll(x, x.shape[0] - 1, 0)


def back(x):
    return pltpu.roll(x, 1, 0)


def unpack(f, own, other, edges, padded, top=0):
    nz, nx = own.shape[0], own.shape[1]
    layer, even = lax.axis_index("layers"), (lax.axis_index("cols") & 1) == 0
    after = pl.multiple_of(jnp.where(even, top + HALO + nx, top), HALO)
    before = pl.multiple_of(jnp.where(even, top, top + HALO + nx), HALO)
    for half, block in ((0, own), (1, other)):
        near, far = edges[2 * half], edges[2 * half + 1]
        for i in range(nz):
            j = jnp.where(layer == 0, i, nz - 1 - i)
            to = half * nz + i
            padded[to, top + HALO : top + HALO + nx, :] = block[j]
            padded[to, pl.ds(after, HALO), :] = near[EDGE[f], j]
            padded[to, pl.ds(before, HALO), :] = far[EDGE[f], j]


def prepare_body(*refs):
    own, other, edges = refs[:3], refs[3:6], refs[6:10]
    c_pad, diag, wx, wx_back, wy, wz, grads, outer, s_pad, h_pad = refs[10:]
    nz, nx = own[0].shape[0], own[0].shape[1]
    planes, width = c_pad.shape[0], c_pad.shape[1]
    for f, target in enumerate((c_pad, s_pad, h_pad)):
        unpack(f, own[f], other[f], edges, target)
    none = jnp.zeros((1, LANES), jnp.float32)
    for z in range(planes):
        h_pad[z, HALO - 1 : HALO, :] = s_pad[z, :1, :]
        h_pad[z, width - HALO : width - HALO + 1, :] = s_pad[z, width - 1 :, :]
        s_pad[z, :1, :] = none
        s_pad[z, width - 1 :, :] = none
    lanes = lane_iota(width)
    last = lanes == LANES - 1
    for z in range(planes):
        c = c_pad[z]
        cf, cr = fore(c), jnp.where(last, 0.0, right(c))
        total = cf + back(c) + cr + jnp.where(lanes == 0, 0.0, left(c))
        wx[z] = joined(c, cf)
        wx_back[z] = joined(c, back(c))
        wy[z] = joined(c, cr)
        if z + 1 < planes:
            wz[z] = joined(c, c_pad[z + 1])
            total = total + c_pad[z + 1]
        if z:
            total = total + c_pad[z - 1]
        diag[z] = s_pad[z] + 3.0 * c + 0.5 * total

    span = HALO + nx
    rows, lanes = row_iota(width), lane_iota(width)
    mine = (rows >= HALO) & (rows < span)
    before = (rows >= HALO - 1) & (rows < span - 1)
    odd = (lanes & 1) == 1
    inside = mine & (lanes < LANES - 1)

    def kept(mask, x):
        return jnp.where(mask, x, 0.0)[:span]

    for z in range(nz):
        c, h = -0.5 * c_pad[z], h_pad[z]
        fall = h - fore(h)
        grads[0, z] = kept(mine, c * fall)
        grads[1, z] = kept(before, fore(c) * fall)
        fall = h - right(h)
        following = right(c) * fall
        grads[2, z] = kept(inside, c * fall + jnp.where(odd, 0.0, following))
        grads[3, z] = kept(inside & odd, following)
        weight = c + -0.5 * c_pad[z + 1] if z + 1 < nz else c
        grads[4, z] = kept(mine, weight * (h - h_pad[z + 1]))
        grads[5, z] = kept(mine & ((lanes == 0) | (lanes == LANES - 1)), c * h)
    outer[...] = kept(mine, -0.5 * c_pad[0] * h_pad[0])


def basis_body(peers, side_count, *refs):
    c_pad, diag_in, wx, wx_back, wy, wz, grads, outer = refs[:8]
    b_own, b_other, edges, refs = refs[8], refs[9], refs[10:14], refs[14:]
    sides = list(zip(refs[:side_count], refs[side_count : 2 * side_count]))
    spot_ref, slots_ref, own_ref, send_ref = refs[2 * side_count : 2 * side_count + 4]
    diag, ws, edge_grads, image, basis = refs[2 * side_count + 4 :]
    layer, row = lax.axis_index("layers"), lax.axis_index("rows")
    nz, nx = b_own.shape[0], b_own.shape[1]
    planes, width = c_pad.shape[0], c_pad.shape[1]
    span = HALO + nx
    inner = slice(HALO, span)
    top = HALO
    body = slice(top, top + width)
    for k in range(ITERS):
        for z in range(planes):
            basis[k, z, :top, :] = jnp.zeros((top, LANES), jnp.float32)
            basis[k, z, top + width :, :] = jnp.zeros((top, LANES), jnp.float32)
    unpack(3, b_own, b_other, edges, basis.at[0], top)

    lanes, rows = lane_iota(width), row_iota(width)
    y_at = lanes & (HALO - 1)
    if side_count == 1:
        meetings = [(jnp.where(row == 0, LANES - 1, 0), jnp.where(row == 0, 0, HALO - 1))]
    else:
        meetings = [(0, HALO - 1), (LANES - 1, 0)]
    strips = []
    for (here, there), (edge, meet) in zip(sides, meetings):
        halves = [jnp.transpose(x[...].reshape(LANES, LANES)) for x in (here, there)]
        first = jnp.where(layer == 0, halves[0], halves[1])
        second = jnp.where(layer == 0, halves[1], halves[0])
        fields = []
        for f in range(4):
            part = slice((f % 2) * width, (f % 2 + 1) * width)
            half = LANES // 2
            fields.append(
                jnp.where(
                    lanes < half,
                    pltpu.roll(first[part], half, 1) if f // 2 else first[part],
                    second[part] if f // 2 else pltpu.roll(second[part], half, 1),
                )
            )
        fields[1] = jnp.where((rows == 0) | (rows == width - 1), 0.0, fields[1])
        shifts = []
        for z in range(planes):
            spot = jnp.where(layer == 0, z, planes - 1 - z) * HALO + meet
            shifts.append(
                ((edge - spot) & (LANES - 1), (spot - edge) & (LANES - 1))
            )
        strips.append((fields, lanes == edge, shifts))

    def from_strips(values, z):
        total = jnp.zeros((width, LANES), jnp.float32)
        for (_, at_edge, shifts), value in zip(strips, values):
            total = jnp.where(at_edge, pltpu.roll(value, shifts[z][0], 1), total)
        return total

    def to_strip(strip, value, z):
        _, at_edge, shifts = strip
        if side_count > 1:
            value = jnp.where(at_edge, value, 0.0)
        return pltpu.roll(value, shifts[z][1], 1)

    edge_c = [jnp.zeros((width, LANES), jnp.float32) for _ in strips]
    mine = (rows >= HALO) & (rows < span)
    for z in range(planes):
        c = c_pad[z]
        c_side = from_strips([s[0][0] for s in strips], z)
        ws[z] = joined(c, c_side)
        diag[z] = diag_in[z] + 0.5 * c_side
        for i, strip in enumerate(strips):
            edge_c[i] = edge_c[i] + to_strip(strip, jnp.where(strip[1], c, 0.0), z)
        if z < nz:
            h_side = from_strips([s[0][2] for s in strips], z)
            edge_grads[z] = grads[5, z] + jnp.where(mine, 0.5 * c * h_side, 0.0)[:span]
    strip_terms = []
    for (fields, _, _), beside in zip(strips, edge_c):
        c = fields[0]
        cf = fore(c)
        cr = jnp.where(y_at < HALO - 1, right(c), 0.0)
        cu = jnp.where(lanes < LANES - HALO, pltpu.roll(c, LANES - HALO, 1), 0.0)
        total = cf + back(c) + cr + cu + beside
        total = total + jnp.where(y_at > 0, left(c), 0.0)
        total = total + jnp.where(lanes >= HALO, pltpu.roll(c, HALO, 1), 0.0)
        strip_terms.append(
            (fields[1] + 3.0 * c + 0.5 * total, joined(c, cf), joined(c, cr), joined(c, cu))
        )

    alphas, gammas, norms, sums = [], [], [], []

    def following(k, image_now, now, before):
        u = image_now - alphas[k - 1] * now
        return u - gammas[k - 1] * before if k > 1 else u

    def member(k, z):
        before = basis[k - 2, z, body, :] if k > 1 else None
        u = following(k, image[z], basis[k - 1, z, body, :], before)
        basis[k, z, body, :] = u
        return u

    def folded(x):
        return sum(x[r : r + 8] for r in range(8, width, 8)) + x[:8]

    side_now = [s[0][3] for s in strips]
    side_last, side_image = None, None
    for k in range(ITERS):
        above = member(k, 0) if k else basis[0, 0, body, :]
        v = None
        if k:
            side_next = [
                following(k, side_image[i], side_now[i], side_last[i] if k > 1 else None)
                for i in range(side_count)
            ]
            side_now, side_last = side_next, side_now
        norm = jnp.zeros((8, LANES), jnp.float32)
        energy = jnp.zeros((8, LANES), jnp.float32)
        side_image = []
        final = k == ITERS - 1
        for x, (d, sx, sy, sz) in zip(side_now, strip_terms):
            if final:
                break
            ax = d * x - sx * fore(x) - back(sx * x) - sy * right(x) - left(sy * x)
            ax = ax - sz * pltpu.roll(x, LANES - HALO, 1) - pltpu.roll(sz * x, HALO, 1)
            side_image.append(ax)
        acc = basis[k, 0, top : top + span, :] * outer[...]
        acc_x = jnp.zeros((span, LANES), jnp.float32)
        acc_y = jnp.zeros((span, LANES), jnp.float32)
        for z in range(nz + ITERS - 1 - k):
            below, v = v, above
            above = member(k, z + 1) if k else basis[0, z + 1, body, :]
            side = from_strips(side_now, z)
            vf, vr = basis[k, z, top + 1 : top + 1 + width, :], right(v)
            vb = basis[k, z, top - 1 : top - 1 + width, :]
            wyz, wsz = wy[z], ws[z]
            av = diag[z] * v - wz[z] * above
            if z:
                av = av - wz[z - 1] * below
            av = av - wx[z] * vf - wx_back[z] * vb - wyz * vr - left(wyz * v) - wsz * side
            if final:
                basis[ITERS, z, body, :] = av
            else:
                image[z] = av
                edge = wsz * v
                for i, strip in enumerate(strips):
                    side_image[i] = side_image[i] - to_strip(strip, edge, z)
                norm = norm + folded(v * v)
                energy = energy + folded(v * av)
            if z < nz:
                fall = (v - vf)[:span]
                acc = acc + fall * grads[0, z]
                acc_x = acc_x + fall * grads[1, z]
                fall = (v - vr)[:span]
                acc = acc + fall * grads[2, z]
                acc_y = acc_y + fall * grads[3, z]
                acc = acc + (v - above)[:span] * grads[4, z]
                acc = acc + (v - side)[:span] * edge_grads[z]
                own_ref[k, jnp.where(layer == 0, z, nz - 1 - z)] = v[inner]
        for x, ax in zip(side_now, side_image):
            norm = norm + folded(x * x)
            energy = energy + folded(x * ax)
        sums.append((acc + back(acc_x) + left(acc_y))[inner])
        norm = all_sum(norm) if not final else jnp.zeros((1, 1), jnp.float32)
        alphas.append(safe_ratio(all_sum(energy), norm) if not final else norm)
        gammas.append(safe_ratio(norm, norms[-1]) if k else jnp.zeros_like(norm))
        norms.append(norm)
    own_rows = slice(top + HALO, top + span)

    dots = {}
    for i in range(ITERS + 1):
        for j in range(i + 1):
            acc = basis[i, 0, own_rows, :] * basis[j, 0, own_rows, :]
            for z in range(1, nz):
                acc = acc + basis[i, z, own_rows, :] * basis[j, z, own_rows, :]
            dots[i, j] = dots[j, i] = all_sum(acc)

    def operator(i, j):
        entry = dots[i, j + 1] + alphas[j] * dots[i, j]
        return entry + gammas[j] * dots[i, j - 1] if j else entry

    lanes = lane_iota(1)
    facts = []
    for j in range(ITERS):
        row_facts = [0.5 * (operator(j, m) + operator(m, j)) for m in range(ITERS)]
        row_facts += [alphas[j], gammas[j], norms[j], dots[j, 0]]
        entries = jnp.zeros((1, LANES), jnp.float32)
        for place, entry in enumerate(row_facts):
            entries = jnp.where(lanes == FACTS + place, entry, entries)
        facts.append(entries)

    blocks_x = nx // 4
    sums = jnp.concatenate(sums, axis=1)
    sums = sums + fore(sums)
    sums = sums + pltpu.roll(sums, nx - 2, 0)
    spot = [spot_ref[r : r + 1, :] for r in range(blocks_x)]
    lane_hits = jnp.concatenate(
        [
            jnp.where(row_iota(LANES) == (p & (LANES - 1)), 1.0, 0.0).astype(jnp.bfloat16)
            for p in spot
        ],
        axis=1,
    )
    peer_at = row_iota(peers)
    row_hit = [(p >= 0) & (peer_at == lax.shift_right_arithmetic(p, LANE_BITS)) for p in spot]
    values = []
    for k in range(ITERS):
        pair = sums[:, k * LANES : (k + 1) * LANES]
        pair = pair + pltpu.roll(pair, LANES - 1, 1)
        for p in halves_of(pair):
            values.append(
                jnp.concatenate(
                    [picked(row_hit[r], p[4 * r : 4 * r + 1]) for r in range(blocks_x)], axis=1
                )
            )
    dense = mm(jnp.concatenate(values, axis=0), lane_hits, NT)
    copies = send_ref.shape[0] // peers
    for k in range(ITERS):
        at = 2 * k * peers
        rows = dense[at : at + peers] + dense[at + peers : at + 2 * peers]
        rows = jnp.where(lane_iota(peers) < FACTS, rows, facts[k])
        if k < 2:
            slots = pltpu.roll(slots_ref[...], (1 - k) * (LANES - SLOTS) + FACTS, 1)
            rows = jnp.where(lane_iota(peers) < SLOTS, rows, slots)
        for peer in range(peers):
            for copy in range(copies):
                send_ref[peer * copies + copy, k : k + 1, :] = rows[peer : peer + 1]


def solve_body(copies, got_ref, own_ref, adjoint_ref, pilot_ref):
    senders = got_ref.shape[0]
    peers = senders // copies
    groups = senders * ITERS // LANES
    got = got_ref[...].reshape(groups, LANES, LANES)
    turned = [jnp.transpose(got[g])[FACTS:SLOTS] for g in range(groups)]

    def fact(place):
        return jnp.concatenate([t[place : place + 1] for t in turned], axis=0)

    alpha, gamma, weight, rhs = (fact(ITERS + place) for place in range(4))
    at = lane_iota(groups) & (ITERS - 1)
    gamma_next = jnp.where(at < ITERS - 1, pltpu.roll(gamma, LANES - 1, 1), 0.0)

    def over_senders(x):
        for shift in (8, 16, 32, 64):
            x = x + pltpu.roll(x, shift, 1)
        return jnp.sum(x, axis=0, keepdims=True)

    norm = over_senders(weight)
    means = safe_ratio(over_senders(weight * alpha), norm)
    growth = safe_ratio(norm, pltpu.roll(norm, 1, 1))
    now = jnp.where(at == 0, 1.0, 0.0)
    last = None
    common = [now]
    for k in range(ITERS - 1):
        image = jnp.where(at > 0, pltpu.roll(now, 1, 1), 0.0) + alpha * now
        image = image + gamma_next * pltpu.roll(now, LANES - 1, 1)
        following = image - means[:, k : k + 1] * now
        if k:
            following = following - growth[:, k : k + 1] * last
        now, last = following, now
        common.append(now)

    lanes = lane_iota(ITERS)
    system = jnp.zeros((ITERS, LANES), jnp.float32)
    stacked = []
    per = LANES // ITERS
    for g in range(groups):
        t = jnp.concatenate([c[g : g + 1] for c in common], axis=0)
        stacked.append(t)
        blocks = []
        for i in range(per):
            block = pltpu.roll(got_ref[g * per + i], (ITERS * i - FACTS) % LANES, 1)
            blocks.append(
                jnp.where((lanes >= ITERS * i) & (lanes < ITERS * (i + 1)), block, 0.0)
            )
        image = mm(t, jnp.concatenate(blocks, axis=0), precision=EXACT)
        beside = jnp.concatenate(
            [image, rhs[g : g + 1], jnp.zeros((LANES - ITERS - 1, LANES), jnp.float32)], axis=0
        )
        system = system + mm(t, beside, NT, precision=EXACT)
    rows = row_iota(ITERS)
    for p in range(ITERS):
        pivot = system[p : p + 1, p : p + 1]
        inverse = jnp.where(pivot > 0.0, 1.0 / jnp.where(pivot > 0.0, pivot, 1.0), 0.0)
        pivot_row = system[p : p + 1] * inverse
        system = jnp.where(rows == p, pivot_row, system - system[:, p : p + 1] * pivot_row)
    answer = system[:, ITERS : ITERS + 1]

    weights = [jnp.sum(answer * t, axis=0, keepdims=True) for t in stacked]
    me = lax.axis_index(GRID_AXES)
    mine = []
    for k in range(ITERS):
        w = jnp.zeros((1, 1), jnp.float32)
        for g in range(groups):
            hit = lane_iota(1) == me * ITERS + k - g * LANES
            w = w + jnp.sum(jnp.where(hit, weights[g], 0.0), axis=1, keepdims=True)
        mine.append(w)
    for z in range(own_ref.shape[1]):
        acc = mine[0] * own_ref[0, z]
        for k in range(1, ITERS):
            acc = acc + mine[k] * own_ref[k, z]
        adjoint_ref[z] = acc

    per_group = LANES // ITERS // copies
    sender = lax.div(lane_iota(per_group), jnp.int32(ITERS * copies))
    values = jnp.concatenate(
        [
            mm(jnp.where(sender == row_iota(per_group), weights[g], 0.0), got[g], precision=EXACT)
            for g in range(groups)
        ],
        axis=0,
    )
    rows_at, lanes_at = row_iota(pilot_ref.shape[0]), row_iota(LANES)
    held = lane_iota(peers) < pilot_ref.shape[0] * LANES // peers
    pieces = pieces_of(jnp.where(held, values, 0.0))
    left, right = [[], [], []], []
    room = LANES - SLOTS
    for s in range(peers):
        slot = jnp.where(
            lane_iota(1) < room,
            pltpu.roll(got_ref[s * copies, 0:1, :], room, 1),
            pltpu.roll(got_ref[s * copies, 1:2, :], 2 * room, 1),
        ).astype(jnp.int32)
        hit = rows_at == lax.shift_right_logical(slot, LANE_BITS)
        for q, piece in enumerate(pieces):
            left[q].append(picked(hit, piece[s : s + 1]))
        right.append(
            jnp.where(lanes_at == (slot & (LANES - 1)), 1.0, 0.0).astype(jnp.bfloat16)
        )
    right = jnp.concatenate(right, axis=1)
    pilot_ref[...] = sum(mm(jnp.concatenate(q, axis=1), right, NT) for q in left)


def tied(*values):
    return lax.optimization_barrier(values)


def neighbour_pairs(axis):
    forward = [(i, i + 1) for i in range(lax.axis_size(axis) - 1)]
    return forward, [(b, a) for a, b in forward]


def swap_pairs(axis, first):
    pairs = [(i, i + 1) for i in range(first, lax.axis_size(axis) - 1, 2)]
    return pairs + [(b, a) for a, b in pairs]


def swapped(x):
    return lax.ppermute(x, "layers", [(0, 1), (1, 0)])


def on_device(
    state_field,
    conductivity,
    storage,
    gauge_owner,
    gauge_cell,
    gauge_value,
    gauge_weight,
    pilot_index,
):
    nz, nx, ny = state_field.shape
    peers = lax.axis_size("cols") * lax.axis_size("rows")
    devices = peers * lax.axis_size("layers")
    gauges = gauge_owner.shape[0]
    capacity = 4 * gauges // peers
    f32 = jnp.float32
    row_count = lax.axis_size("rows")

    def shape(*dims, dtype=f32):
        return jax.ShapeDtypeStruct(dims, dtype)

    def flat(x):
        return x.reshape(gauges // LANES, LANES)

    obs = pltpu.VMEM((gauges // LANES, LANES), f32)
    obs_int = pltpu.VMEM((gauges // LANES, LANES), jnp.int32)
    payload = kernel_call(
        functools.partial(route_body, peers, capacity),
        shape(peers, 3 * capacity // LANES, LANES),
        [obs_int, obs_int, obs, obs, pltpu.SemaphoreType.DMA((4,))],
        weight=5,
        vmem=64 * 1024 * 1024,
    )(in_specs=[HBM] * 4, out_specs=VMEM)(
        flat(gauge_owner), flat(gauge_cell), flat(gauge_value), flat(gauge_weight)
    )
    payload, pilot_index = tied(payload, pilot_index)
    got = lax.all_to_all(payload, PEER_AXES, 0, 0, tiled=True)
    spot, slots = kernel_call(
        pilot_body, (shape(nx // 4, LANES, dtype=jnp.int32), shape(peers, LANES))
    )(in_specs=[VMEM], out_specs=(VMEM, VMEM))(pilot_index)

    fixed = (conductivity, storage, state_field)
    got, spot, *fixed_other = tied(got, spot, *(swapped(x) for x in fixed))
    edge = shape(3, nz, HALO, LANES)
    source, near, far = kernel_call(
        functools.partial(source_body, capacity // LANES),
        (shape(nz, nx, LANES), edge, edge),
        weight=6,
    )(in_specs=[VMEM] * 4, out_specs=(VMEM,) * 3)(got, *fixed)
    near = lax.ppermute(near, "cols", swap_pairs("cols", 0))
    far = lax.ppermute(far, "cols", swap_pairs("cols", 1))
    other = swapped(source)

    def packed(low_side):
        return kernel_call(
            functools.partial(pack_body, low_side), shape(2 * nz, HALO, LANES)
        )(in_specs=[VMEM] * 6, out_specs=VMEM)(*fixed, source, near, far)

    if row_count == 2:
        send = [(packed(None), [(0, 1), (1, 0)])]
    else:
        forward, backward = neighbour_pairs("rows")
        send = [(packed(False), forward), (packed(True), backward)]
    edges = tied(near, far, swapped(near), swapped(far), *(x for x, _ in send))[:4]
    sides = [lax.ppermute(x, "rows", pairs) for x, pairs in send]
    planes, width, span = 2 * nz, nx + 2 * HALO, nx + HALO
    padded = (planes, width, LANES)
    prepared = kernel_call(
        prepare_body,
        (*(shape(*padded) for _ in range(6)), shape(6, nz, span, LANES), shape(span, LANES)),
        [pltpu.VMEM(padded, f32)] * 2,
        weight=3,
    )(in_specs=[VMEM] * 10, out_specs=(VMEM,) * 8)(*fixed, *fixed_other, *edges)
    *sides, prepared = tied(*sides, prepared)
    sides = sides + [swapped(x) for x in sides]

    each = nx * ny // 8 // LANES
    own, send = kernel_call(
        functools.partial(basis_body, peers, len(sides) // 2),
        (shape(ITERS, nz, nx, LANES), shape(devices, ITERS, LANES)),
        [
            pltpu.VMEM(padded, f32),
            pltpu.VMEM(padded, f32),
            pltpu.VMEM((nz, span, LANES), f32),
            pltpu.VMEM(padded, f32),
            pltpu.VMEM((ITERS + 1, planes, width + 2 * HALO, LANES), f32),
        ],
        weight=10,
    )(in_specs=[VMEM] * (16 + len(sides)), out_specs=(VMEM, VMEM))(
        *prepared, source, other, *edges, *sides, spot, slots
    )
    parts = lax.all_to_all(send, GRID_AXES, 0, 0, tiled=True)
    adjoint, pilot = kernel_call(
        functools.partial(solve_body, devices // peers), (shape(nz, nx, ny), shape(each, LANES))
    )(in_specs=[VMEM] * 2, out_specs=(VMEM, VMEM))(parts, own)
    return adjoint, pilot.reshape(-1)


def solution(mesh):
    return jax.shard_map(
        on_device,
        mesh=mesh,
        in_specs=(
            P(("groups", "layers"), "cols", "rows"),
            P(("groups", "layers"), "cols", "rows"),
            P(("groups", "layers"), "cols", "rows"),
            P(("groups", "cols", "rows", "layers")),
            P(("groups", "cols", "rows", "layers")),
            P(("groups", "cols", "rows", "layers")),
            P(("groups", "cols", "rows", "layers")),
            P("cols", "rows"),
        ),
        out_specs=(P(("groups", "layers"), "cols", "rows"), P(("groups", "cols", "rows"))),
        check_vma=False,
    )
```

```python
import functools

import jax
import jax.numpy as jnp
from jax import lax
from jax.experimental import pallas as pl
from jax.experimental.pallas import tpu as pltpu
from jax.sharding import PartitionSpec as P

ITERS = 8
HALO = 8
EDGE = (0, 1, 1, 2)
FACTS = 64
SLOTS = 96
LANES = 128
LANE_BITS = 7
GRID_AXES = ("cols", "rows", "layers")
PEER_AXES = ("cols", "rows")
NT = (((1,), (1,)), ((), ()))
EXACT = lax.Precision.HIGHEST
VMEM_BYTES = 24 * 1024 * 1024


def kernel_call(body, out_shape, scratch=(), weight=1, vmem=VMEM_BYTES):
    return functools.partial(
        pl.pallas_call,
        body,
        out_shape=out_shape,
        scratch_shapes=list(scratch),
        compiler_params=pltpu.CompilerParams(vmem_limit_bytes=vmem),
        cost_estimate=pl.CostEstimate(
            flops=0, bytes_accessed=weight * 3_000_000, transcendentals=0
        ),
    )


VMEM = pl.BlockSpec(memory_space=pltpu.VMEM)
HBM = pl.BlockSpec(memory_space=pltpu.HBM)


def pieces_of(x):
    first = x.astype(jnp.bfloat16).astype(jnp.float32)
    rest = x - first
    second = rest.astype(jnp.bfloat16).astype(jnp.float32)
    return first, second, rest - second


def halves_of(x):
    first = x.astype(jnp.bfloat16).astype(jnp.float32)
    return first, x - first


def row_iota(rows, lanes=LANES):
    return lax.broadcasted_iota(jnp.int32, (rows, lanes), 0)


def lane_iota(rows, lanes=LANES):
    return lax.broadcasted_iota(jnp.int32, (rows, lanes), 1)


def picked(mask, row):
    return jnp.where(mask, row, jnp.zeros_like(row)).astype(jnp.bfloat16)


TILE = 16


def spread16(x, r):
    return jnp.broadcast_to(x[r : r + 1], (TILE, LANES)).astype(jnp.bfloat16)


def hits16(count, row):
    at = row_iota(TILE).astype(jnp.float32).astype(jnp.bfloat16)
    return [at + jnp.bfloat16(TILE * i) == row for i in range(count // TILE)]


def filled16(masks, value):
    zero = jnp.zeros((TILE, LANES), jnp.bfloat16)
    return jnp.concatenate([jnp.where(m, value, zero) for m in masks], axis=0)


def mm(a, b, dims=(((1,), (0,)), ((), ())), precision=None):
    return lax.dot_general(a, b, dims, precision=precision, preferred_element_type=jnp.float32)


def ranks(owner, peers):
    rows = owner.shape[0]
    ra, ca = row_iota(LANES, 2 * LANES), lane_iota(LANES, 2 * LANES)
    earlier_lane = jnp.where((ra < ca) | (ca >= LANES), 1.0, 0.0).astype(jnp.bfloat16)
    earlier_row = jnp.where(row_iota(rows, rows) > lane_iota(rows, rows), 1.0, 0.0).astype(
        jnp.bfloat16
    )
    hits = [owner == peer for peer in range(peers)]
    ones = jnp.concatenate([jnp.where(h, 1.0, 0.0).astype(jnp.bfloat16) for h in hits], axis=0)
    counts = mm(ones, earlier_lane)
    part = [counts[p * rows : (p + 1) * rows] for p in range(peers)]
    before = mm(
        earlier_row, jnp.concatenate([c[:, LANES:] for c in part], axis=1).astype(jnp.bfloat16)
    )
    rank = jnp.zeros((rows, LANES), jnp.float32)
    for p in range(peers):
        rank = jnp.where(
            hits[p], part[p][:, :LANES] + before[:, p * LANES : (p + 1) * LANES], rank
        )
    return rank.astype(jnp.int32)


def route_body(
    peers, capacity, owner_hbm, cell_hbm, value_hbm, weight_hbm, out_ref,
    owner_ref, cell_ref, value_ref, weight_ref, sems,
):
    copies = [
        pltpu.make_async_copy(source, target, sems.at[i])
        for i, (source, target) in enumerate(
            (
                (owner_hbm, owner_ref),
                (cell_hbm, cell_ref),
                (value_hbm, value_ref),
                (weight_hbm, weight_ref),
            )
        )
    ]
    for copy in copies:
        copy.start()
    copies[0].wait()
    rows = owner_ref.shape[0]
    owner = owner_ref[...]
    position = owner * capacity + ranks(owner, peers)
    for copy in copies[1:]:
        copy.wait()
    slot_row = lax.shift_right_logical(position, LANE_BITS).astype(jnp.float32)
    slot_lane = (position & (LANES - 1)).astype(jnp.float32)
    cell = cell_ref[...]
    columns = [
        lax.shift_right_logical(cell, LANE_BITS).astype(jnp.float32),
        (cell & (LANES - 1)).astype(jnp.float32),
        *pieces_of(value_ref[...]),
        *halves_of(weight_ref[...]),
    ]
    slot_rows = peers * capacity // LANES
    one = jnp.ones((TILE, LANES), jnp.bfloat16)
    total = None
    for start in range(0, rows, TILE):
        at_row, at_lane = [], [[] for _ in columns]
        for r in range(start, start + TILE):
            at_row.append(filled16(hits16(slot_rows, spread16(slot_row, r)), one))
            masks = hits16(LANES, spread16(slot_lane, r))
            for q, column in enumerate(columns):
                at_lane[q].append(filled16(masks, spread16(column, r)))
        at_lane = jnp.concatenate([jnp.concatenate(q, axis=1) for q in at_lane], axis=0)
        part = mm(at_lane, jnp.concatenate(at_row, axis=1), NT)
        total = part if total is None else total + part
    part = [total[q * LANES : (q + 1) * LANES] for q in range(len(columns))]
    fields = [
        part[0] * LANES + part[1],
        part[2] + part[3] + part[4],
        part[5] + part[6],
    ]
    fields = [jnp.transpose(f) for f in fields]
    each = capacity // LANES
    for peer in range(peers):
        for q, field in enumerate(fields):
            out_ref[peer, q * each : (q + 1) * each, :] = field[peer * each : (peer + 1) * each]


def pilot_body(pilot_ref, spot_ref, slots_ref):
    peers = slots_ref.shape[0]
    blocks_x = pilot_ref.shape[0] // 4
    pilots = pilot_ref.shape[0] * pilot_ref.shape[1] // 8
    pilot = jnp.concatenate([pilot_ref[4 * r : 4 * r + 1, :] for r in range(blocks_x)], axis=0)
    owner = lax.div(pilot, jnp.int32(pilots))
    slot = pilot - owner * pilots
    first = (lane_iota(blocks_x) & 1) == 0
    owner = jnp.where(first, owner, -1)
    rank = ranks(owner, peers)
    spot_ref[...] = jnp.where(first, owner * LANES + rank, -1)
    left, high, low = [], [], []
    peer_at, lanes_at = row_iota(peers), row_iota(LANES)
    for r in range(blocks_x):
        left.append(jnp.where(peer_at == owner[r : r + 1], 1.0, 0.0).astype(jnp.bfloat16))
        hit = lanes_at == rank[r : r + 1]
        number = slot[r : r + 1]
        high.append(picked(hit, lax.shift_right_logical(number, LANE_BITS).astype(jnp.float32)))
        low.append(picked(hit, (number & (LANES - 1)).astype(jnp.float32)))
    left = jnp.concatenate(left, axis=1)
    slots_ref[...] = mm(left, jnp.concatenate(high, axis=1), NT) * LANES + mm(
        left, jnp.concatenate(low, axis=1), NT
    )


def source_body(
    each, got_ref, conductivity_ref, storage_ref, state_ref, out_ref, near_ref, far_ref
):
    peers = got_ref.shape[0]
    nz, nx = state_ref.shape[0], state_ref.shape[1]
    cells = nz * nx
    one = jnp.ones((TILE, LANES), jnp.bfloat16)

    def sixteen(group, q):
        peer, row = divmod(group * TILE, each)
        if each >= TILE:
            return got_ref[peer, q * each + row : q * each + row + TILE, :]
        return jnp.concatenate(
            [got_ref[peer + i, q * each : (q + 1) * each, :] for i in range(TILE // each)], axis=0
        )

    total = None
    for group in range(peers * each // TILE):
        cell = sixteen(group, 0).astype(jnp.int32)
        high = lax.shift_right_logical(cell, LANE_BITS)
        low = cell & (LANES - 1)
        at_row = jnp.concatenate(
            [
                filled16(hits16(cells, spread16(high.astype(jnp.float32), r)), one)
                for r in range(TILE)
            ],
            axis=1,
        )
        heads = []
        if group == 0:
            state = jnp.transpose(state_ref[...].reshape(cells, LANES))
            lines = mm(
                jnp.concatenate([p.astype(jnp.bfloat16) for p in pieces_of(state)], axis=0), at_row
            )
            for r in range(TILE):
                line = lines[:, r * LANES : (r + 1) * LANES]
                line = line[:LANES] + line[LANES : 2 * LANES] + line[2 * LANES :]
                hit = row_iota(LANES) == low[r : r + 1]
                heads.append(jnp.sum(jnp.where(hit, line, 0.0), axis=0, keepdims=True))
        for r in range(0, 0 if heads else TILE, 8):
            head = jnp.zeros((8, LANES), jnp.float32)
            for z in range(nz):
                for x in range(nx):
                    line = jnp.broadcast_to(state_ref[z, x : x + 1, :], (8, LANES))
                    line = jnp.take_along_axis(line, low[r : r + 8], axis=1)
                    head = jnp.where(high[r : r + 8] == z * nx + x, line, head)
            heads.append(head)
        misfit = sixteen(group, 2) * (jnp.concatenate(heads, axis=0) - sixteen(group, 1))
        pieces = halves_of(misfit)
        low = low.astype(jnp.float32)
        at_lane = [[] for _ in pieces]
        for r in range(TILE):
            masks = hits16(LANES, spread16(low, r))
            for q, piece in enumerate(pieces):
                at_lane[q].append(filled16(masks, spread16(piece, r)))
        at_lane = jnp.concatenate([jnp.concatenate(q, axis=1) for q in at_lane], axis=0)
        part = mm(at_lane, at_row, NT)
        total = part if total is None else total + part
    total = jnp.transpose(total[:LANES] + total[LANES:])
    out_ref[...] = total.reshape(nz, nx, LANES)
    even = (lax.axis_index("cols") & 1) == 0
    total = total.reshape(nz, nx, LANES)
    at = lax.broadcasted_iota(jnp.int32, (nz, HALO, LANES), 1)
    for f, field in enumerate((conductivity_ref, storage_ref, total)):
        low, high = field[:, :HALO, :], field[:, nx - HALO :, :]
        if f == 1:
            low = jnp.where(at == HALO - 1, state_ref[:, :1, :], low)
            high = jnp.where(at == 0, state_ref[:, nx - 1 :, :], high)
        near_ref[f] = jnp.where(even, high, low)
        far_ref[f] = jnp.where(even, low, high)


def all_sum(x):
    while x.ndim > 2:
        x = jnp.sum(x, axis=0)
    return jnp.sum(jnp.sum(x, axis=0, keepdims=True), axis=1, keepdims=True)


def safe_ratio(a, b):
    return jnp.where(b > 0.0, a / jnp.where(b > 0.0, b, 1.0), 0.0)


def pack_body(low_side, *refs):
    *fields, near_ref, far_ref, out_ref = refs
    even = (lax.axis_index("cols") & 1) == 0
    nz, nx = fields[0].shape[0], fields[0].shape[1]
    lanes = lane_iota(2 * (nx + 2 * HALO))
    tall = jnp.zeros(lanes.shape, jnp.float32)
    for pair in range(2):
        for z in range(nz):
            at = (pair * nz + z) * HALO
            x = jnp.concatenate(
                [
                    part
                    for f in (2 * pair, 2 * pair + 1)
                    for part in (
                        jnp.where(even, far_ref[EDGE[f], z], near_ref[EDGE[f], z]),
                        fields[f][z],
                        jnp.where(even, near_ref[EDGE[f], z], far_ref[EDGE[f], z]),
                    )
                ],
                axis=0,
            )
            if low_side is None:
                shift = (at + jnp.where(lax.axis_index("rows") == 0, HALO, 0)) & (LANES - 1)
            else:
                shift = at if low_side else (at + HALO) & (LANES - 1)
            x = pltpu.roll(x, shift, 1)
            tall = jnp.where((lanes >= at) & (lanes < at + HALO), x, tall)
    rest = LANES - tall.shape[0]
    tall = jnp.concatenate([tall, jnp.zeros((rest, LANES), jnp.float32)], axis=0)
    out_ref[...] = jnp.transpose(tall).reshape(out_ref.shape)


def joined(a, b):
    return jnp.where((a > 0.0) & (b > 0.0), 0.5 * (a + b), 0.0)


def right(x):
    return pltpu.roll(x, x.shape[1] - 1, 1)


def left(x):
    return pltpu.roll(x, 1, 1)


def fore(x):
    return pltpu.roll(x, x.shape[0] - 1, 0)


def back(x):
    return pltpu.roll(x, 1, 0)


def unpack(f, own, other, edges, padded, top=0):
    nz, nx = own.shape[0], own.shape[1]
    layer, even = lax.axis_index("layers"), (lax.axis_index("cols") & 1) == 0
    after = pl.multiple_of(jnp.where(even, top + HALO + nx, top), HALO)
    before = pl.multiple_of(jnp.where(even, top, top + HALO + nx), HALO)
    for half, block in ((0, own), (1, other)):
        near, far = edges[2 * half], edges[2 * half + 1]
        for i in range(nz):
            j = jnp.where(layer == 0, i, nz - 1 - i)
            to = half * nz + i
            padded[to, top + HALO : top + HALO + nx, :] = block[j]
            padded[to, pl.ds(after, HALO), :] = near[EDGE[f], j]
            padded[to, pl.ds(before, HALO), :] = far[EDGE[f], j]


def prepare_body(*refs):
    own, other, edges = refs[:3], refs[3:6], refs[6:10]
    c_pad, diag, wx, wx_back, wy, wz, grads, outer, s_pad, h_pad = refs[10:]
    nz, nx = own[0].shape[0], own[0].shape[1]
    planes, width = c_pad.shape[0], c_pad.shape[1]
    for f, target in enumerate((c_pad, s_pad, h_pad)):
        unpack(f, own[f], other[f], edges, target)
    none = jnp.zeros((1, LANES), jnp.float32)
    for z in range(planes):
        h_pad[z, HALO - 1 : HALO, :] = s_pad[z, :1, :]
        h_pad[z, width - HALO : width - HALO + 1, :] = s_pad[z, width - 1 :, :]
        s_pad[z, :1, :] = none
        s_pad[z, width - 1 :, :] = none
    lanes = lane_iota(width)
    last = lanes == LANES - 1
    for z in range(planes):
        c = c_pad[z]
        cf, cr = fore(c), jnp.where(last, 0.0, right(c))
        total = cf + back(c) + cr + jnp.where(lanes == 0, 0.0, left(c))
        wx[z] = joined(c, cf)
        wx_back[z] = joined(c, back(c))
        wy[z] = joined(c, cr)
        if z + 1 < planes:
            wz[z] = joined(c, c_pad[z + 1])
            total = total + c_pad[z + 1]
        if z:
            total = total + c_pad[z - 1]
        diag[z] = s_pad[z] + 3.0 * c + 0.5 * total

    span = HALO + nx
    rows, lanes = row_iota(width), lane_iota(width)
    mine = (rows >= HALO) & (rows < span)
    before = (rows >= HALO - 1) & (rows < span - 1)
    odd = (lanes & 1) == 1
    inside = mine & (lanes < LANES - 1)

    def kept(mask, x):
        return jnp.where(mask, x, 0.0)[:span]

    for z in range(nz):
        c, h = -0.5 * c_pad[z], h_pad[z]
        fall = h - fore(h)
        grads[0, z] = kept(mine, c * fall)
        grads[1, z] = kept(before, fore(c) * fall)
        fall = h - right(h)
        following = right(c) * fall
        grads[2, z] = kept(inside, c * fall + jnp.where(odd, 0.0, following))
        grads[3, z] = kept(inside & odd, following)
        weight = c + -0.5 * c_pad[z + 1] if z + 1 < nz else c
        grads[4, z] = kept(mine, weight * (h - h_pad[z + 1]))
        grads[5, z] = kept(mine & ((lanes == 0) | (lanes == LANES - 1)), c * h)
    outer[...] = kept(mine, -0.5 * c_pad[0] * h_pad[0])


def basis_body(peers, side_count, *refs):
    c_pad, diag_in, wx, wx_back, wy, wz, grads, outer = refs[:8]
    b_own, b_other, edges, refs = refs[8], refs[9], refs[10:14], refs[14:]
    sides = list(zip(refs[:side_count], refs[side_count : 2 * side_count]))
    spot_ref, slots_ref, own_ref, send_ref = refs[2 * side_count : 2 * side_count + 4]
    diag, ws, edge_grads, image, basis = refs[2 * side_count + 4 :]
    layer, row = lax.axis_index("layers"), lax.axis_index("rows")
    nz, nx = b_own.shape[0], b_own.shape[1]
    planes, width = c_pad.shape[0], c_pad.shape[1]
    span = HALO + nx
    inner = slice(HALO, span)
    top = HALO
    body = slice(top, top + width)
    own_rows = slice(top + HALO, top + span)
    for k in range(ITERS):
        for z in range(planes):
            basis[k, z, :top, :] = jnp.zeros((top, LANES), jnp.float32)
            basis[k, z, top + width :, :] = jnp.zeros((top, LANES), jnp.float32)
    unpack(3, b_own, b_other, edges, basis.at[0], top)

    lanes, rows = lane_iota(width), row_iota(width)
    y_at = lanes & (HALO - 1)
    if side_count == 1:
        meetings = [(jnp.where(row == 0, LANES - 1, 0), jnp.where(row == 0, 0, HALO - 1))]
    else:
        meetings = [(0, HALO - 1), (LANES - 1, 0)]
    strips = []
    for (here, there), (edge, meet) in zip(sides, meetings):
        halves = [jnp.transpose(x[...].reshape(LANES, LANES)) for x in (here, there)]
        first = jnp.where(layer == 0, halves[0], halves[1])
        second = jnp.where(layer == 0, halves[1], halves[0])
        fields = []
        for f in range(4):
            part = slice((f % 2) * width, (f % 2 + 1) * width)
            half = LANES // 2
            fields.append(
                jnp.where(
                    lanes < half,
                    pltpu.roll(first[part], half, 1) if f // 2 else first[part],
                    second[part] if f // 2 else pltpu.roll(second[part], half, 1),
                )
            )
        fields[1] = jnp.where((rows == 0) | (rows == width - 1), 0.0, fields[1])
        shifts = []
        for z in range(planes):
            spot = jnp.where(layer == 0, z, planes - 1 - z) * HALO + meet
            shifts.append(
                ((edge - spot) & (LANES - 1), (spot - edge) & (LANES - 1))
            )
        strips.append((fields, lanes == edge, shifts))

    def from_strips(values, z):
        total = jnp.zeros((width, LANES), jnp.float32)
        for (_, at_edge, shifts), value in zip(strips, values):
            total = jnp.where(at_edge, pltpu.roll(value, shifts[z][0], 1), total)
        return total

    def to_strip(strip, value, z):
        _, at_edge, shifts = strip
        if side_count > 1:
            value = jnp.where(at_edge, value, 0.0)
        return pltpu.roll(value, shifts[z][1], 1)

    edge_c = [jnp.zeros((width, LANES), jnp.float32) for _ in strips]
    mine = (rows >= HALO) & (rows < span)
    for z in range(planes):
        c = c_pad[z]
        c_side = from_strips([s[0][0] for s in strips], z)
        ws[z] = joined(c, c_side)
        diag[z] = diag_in[z] + 0.5 * c_side
        for i, strip in enumerate(strips):
            edge_c[i] = edge_c[i] + to_strip(strip, jnp.where(strip[1], c, 0.0), z)
        if z < nz:
            h_side = from_strips([s[0][2] for s in strips], z)
            edge_grads[z] = grads[5, z] + jnp.where(mine, 0.5 * c * h_side, 0.0)[:span]
    strip_terms = []
    for (fields, _, _), beside in zip(strips, edge_c):
        c = fields[0]
        cf = fore(c)
        cr = jnp.where(y_at < HALO - 1, right(c), 0.0)
        cu = jnp.where(lanes < LANES - HALO, pltpu.roll(c, LANES - HALO, 1), 0.0)
        total = cf + back(c) + cr + cu + beside
        total = total + jnp.where(y_at > 0, left(c), 0.0)
        total = total + jnp.where(lanes >= HALO, pltpu.roll(c, HALO, 1), 0.0)
        strip_terms.append(
            (fields[1] + 3.0 * c + 0.5 * total, joined(c, cf), joined(c, cr), joined(c, cu))
        )

    alphas, gammas, norms, sums = [], [], [], []

    def following(k, image_now, now, before):
        u = image_now - alphas[k - 1] * now
        return u - gammas[k - 1] * before if k > 1 else u

    def member(k, z):
        before = basis[k - 2, z, body, :] if k > 1 else None
        u = following(k, image[z], basis[k - 1, z, body, :], before)
        basis[k, z, body, :] = u
        return u

    def folded(x):
        return sum(x[r : r + 8] for r in range(8, width, 8)) + x[:8]

    side_now = [s[0][3] for s in strips]
    side_last, side_image = None, None
    for k in range(ITERS):
        above = member(k, 0) if k else basis[0, 0, body, :]
        v = None
        if k:
            side_next = [
                following(k, side_image[i], side_now[i], side_last[i] if k > 1 else None)
                for i in range(side_count)
            ]
            side_now, side_last = side_next, side_now
        norm = jnp.zeros((8, LANES), jnp.float32)
        energy = jnp.zeros((8, LANES), jnp.float32)
        side_image = []
        final = k == ITERS - 1
        for x, (d, sx, sy, sz) in zip(side_now, strip_terms):
            if final:
                break
            ax = d * x - sx * fore(x) - back(sx * x) - sy * right(x) - left(sy * x)
            ax = ax - sz * pltpu.roll(x, LANES - HALO, 1) - pltpu.roll(sz * x, HALO, 1)
            side_image.append(ax)
        acc = basis[k, 0, top : top + span, :] * outer[...]
        acc_x = jnp.zeros((span, LANES), jnp.float32)
        acc_y = jnp.zeros((span, LANES), jnp.float32)
        for z in range(nz + ITERS - 1 - k):
            below, v = v, above
            above = member(k, z + 1) if k else basis[0, z + 1, body, :]
            side = from_strips(side_now, z)
            vf, vr = basis[k, z, top + 1 : top + 1 + width, :], right(v)
            vb = basis[k, z, top - 1 : top - 1 + width, :]
            wyz, wsz = wy[z], ws[z]
            part = inner if final else slice(0, width)
            av = diag[z, part, :] * v[part] - wz[z, part, :] * above[part]
            if z:
                av = av - wz[z - 1, part, :] * below[part]
            av = av - wx[z, part, :] * vf[part] - wx_back[z, part, :] * vb[part]
            av = av - wyz[part] * vr[part] - left(wyz[part] * v[part]) - wsz[part] * side[part]
            if final:
                basis[ITERS, z, own_rows, :] = av
            else:
                image[z] = av
                edge = wsz * v
                for i, strip in enumerate(strips):
                    side_image[i] = side_image[i] - to_strip(strip, edge, z)
                norm = norm + folded(v * v)
                energy = energy + folded(v * av)
            if z < nz:
                fall = (v - vf)[:span]
                acc = acc + fall * grads[0, z]
                acc_x = acc_x + fall * grads[1, z]
                fall = (v - vr)[:span]
                acc = acc + fall * grads[2, z]
                acc_y = acc_y + fall * grads[3, z]
                acc = acc + (v - above)[:span] * grads[4, z]
                acc = acc + (v - side)[:span] * edge_grads[z]
                own_ref[k, jnp.where(layer == 0, z, nz - 1 - z)] = v[inner]
        for x, ax in zip(side_now, side_image):
            norm = norm + folded(x * x)
            energy = energy + folded(x * ax)
        sums.append((acc + back(acc_x) + left(acc_y))[inner])
        norm = all_sum(norm) if not final else jnp.zeros((1, 1), jnp.float32)
        alphas.append(safe_ratio(all_sum(energy), norm) if not final else norm)
        gammas.append(safe_ratio(norm, norms[-1]) if k else jnp.zeros_like(norm))
        norms.append(norm)

    dots = {}
    for i in range(ITERS + 1):
        for j in range(min(i + 1, ITERS)):
            acc = basis[i, 0, own_rows, :] * basis[j, 0, own_rows, :]
            for z in range(1, nz):
                acc = acc + basis[i, z, own_rows, :] * basis[j, z, own_rows, :]
            dots[i, j] = dots[j, i] = all_sum(acc)

    def operator(i, j):
        entry = dots[i, j + 1] + alphas[j] * dots[i, j]
        return entry + gammas[j] * dots[i, j - 1] if j else entry

    lanes = lane_iota(1)
    facts = []
    for j in range(ITERS):
        row_facts = [0.5 * (operator(j, m) + operator(m, j)) for m in range(ITERS)]
        row_facts += [alphas[j], gammas[j], norms[j], dots[j, 0]]
        entries = jnp.zeros((1, LANES), jnp.float32)
        for place, entry in enumerate(row_facts):
            entries = jnp.where(lanes == FACTS + place, entry, entries)
        facts.append(entries)

    blocks_x = nx // 4
    four = jnp.where(
        lax.shift_right_logical(lane_iota(blocks_x, nx), 2) == row_iota(blocks_x, nx), 1.0, 0.0
    )
    sums = mm(four, jnp.concatenate(sums, axis=1), precision=EXACT)
    spot = [spot_ref[r : r + 1, :] for r in range(blocks_x)]
    lane_hits = jnp.concatenate(
        [
            jnp.where(row_iota(LANES) == (p & (LANES - 1)), 1.0, 0.0).astype(jnp.bfloat16)
            for p in spot
        ],
        axis=1,
    )
    peer_at = row_iota(peers)
    row_hit = [(p >= 0) & (peer_at == lax.shift_right_arithmetic(p, LANE_BITS)) for p in spot]
    values = []
    for k in range(ITERS):
        pair = sums[:, k * LANES : (k + 1) * LANES]
        pair = pair + pltpu.roll(pair, LANES - 1, 1)
        for p in pieces_of(pair):
            values.append(
                jnp.concatenate(
                    [picked(row_hit[r], p[r : r + 1]) for r in range(blocks_x)], axis=1
                )
            )
    dense = mm(jnp.concatenate(values, axis=0), lane_hits, NT)
    copies = send_ref.shape[0] // peers
    for k in range(ITERS):
        at = 3 * k * peers
        rows = dense[at : at + peers] + dense[at + peers : at + 2 * peers]
        rows = rows + dense[at + 2 * peers : at + 3 * peers]
        rows = jnp.where(lane_iota(peers) < FACTS, rows, facts[k])
        if k < 2:
            slots = pltpu.roll(slots_ref[...], (1 - k) * (LANES - SLOTS) + FACTS, 1)
            rows = jnp.where(lane_iota(peers) < SLOTS, rows, slots)
        for peer in range(peers):
            for copy in range(copies):
                send_ref[peer * copies + copy, k : k + 1, :] = rows[peer : peer + 1]


def solve_body(copies, got_ref, own_ref, adjoint_ref, pilot_ref):
    senders = got_ref.shape[0]
    peers = senders // copies
    groups = senders * ITERS // LANES
    got = got_ref[...].reshape(groups, LANES, LANES)
    turned = [jnp.transpose(got[g])[FACTS:SLOTS] for g in range(groups)]

    def fact(place):
        return jnp.concatenate([t[place : place + 1] for t in turned], axis=0)

    alpha, gamma, weight, rhs = (fact(ITERS + place) for place in range(4))
    at = lane_iota(groups) & (ITERS - 1)
    gamma_next = jnp.where(at < ITERS - 1, pltpu.roll(gamma, LANES - 1, 1), 0.0)

    def over_senders(x):
        for shift in (8, 16, 32, 64):
            x = x + pltpu.roll(x, shift, 1)
        return jnp.sum(x, axis=0, keepdims=True)

    norm = over_senders(weight)
    means = safe_ratio(over_senders(weight * alpha), norm)
    growth = safe_ratio(norm, pltpu.roll(norm, 1, 1))
    now = jnp.where(at == 0, 1.0, 0.0)
    last = None
    common = [now]
    for k in range(ITERS - 1):
        image = jnp.where(at > 0, pltpu.roll(now, 1, 1), 0.0) + alpha * now
        image = image + gamma_next * pltpu.roll(now, LANES - 1, 1)
        following = image - means[:, k : k + 1] * now
        if k:
            following = following - growth[:, k : k + 1] * last
        now, last = following, now
        common.append(now)

    lanes = lane_iota(ITERS)
    system = jnp.zeros((ITERS, LANES), jnp.float32)
    stacked = []
    per = LANES // ITERS
    for g in range(groups):
        t = jnp.concatenate([c[g : g + 1] for c in common], axis=0)
        stacked.append(t)
        blocks = []
        for i in range(per):
            block = pltpu.roll(got_ref[g * per + i], (ITERS * i - FACTS) % LANES, 1)
            blocks.append(
                jnp.where((lanes >= ITERS * i) & (lanes < ITERS * (i + 1)), block, 0.0)
            )
        image = mm(t, jnp.concatenate(blocks, axis=0), precision=EXACT)
        beside = jnp.concatenate(
            [image, rhs[g : g + 1], jnp.zeros((LANES - ITERS - 1, LANES), jnp.float32)], axis=0
        )
        system = system + mm(t, beside, NT, precision=EXACT)
    rows = row_iota(ITERS)
    for p in range(ITERS):
        pivot = system[p : p + 1, p : p + 1]
        inverse = jnp.where(pivot > 0.0, 1.0 / jnp.where(pivot > 0.0, pivot, 1.0), 0.0)
        pivot_row = system[p : p + 1] * inverse
        system = jnp.where(rows == p, pivot_row, system - system[:, p : p + 1] * pivot_row)
    answer = system[:, ITERS : ITERS + 1]

    weights = [jnp.sum(answer * t, axis=0, keepdims=True) for t in stacked]
    me = lax.axis_index(GRID_AXES)
    mine = []
    for k in range(ITERS):
        w = jnp.zeros((1, 1), jnp.float32)
        for g in range(groups):
            hit = lane_iota(1) == me * ITERS + k - g * LANES
            w = w + jnp.sum(jnp.where(hit, weights[g], 0.0), axis=1, keepdims=True)
        mine.append(w)
    for z in range(own_ref.shape[1]):
        acc = mine[0] * own_ref[0, z]
        for k in range(1, ITERS):
            acc = acc + mine[k] * own_ref[k, z]
        adjoint_ref[z] = acc

    per_group = LANES // ITERS // copies
    sender = lax.div(lane_iota(per_group), jnp.int32(ITERS * copies))
    values = jnp.concatenate(
        [
            mm(jnp.where(sender == row_iota(per_group), weights[g], 0.0), got[g], precision=EXACT)
            for g in range(groups)
        ],
        axis=0,
    )
    rows_at, lanes_at = row_iota(pilot_ref.shape[0]), row_iota(LANES)
    held = lane_iota(peers) < pilot_ref.shape[0] * LANES // peers
    pieces = pieces_of(jnp.where(held, values, 0.0))
    left, right = [[], [], []], []
    room = LANES - SLOTS
    for s in range(peers):
        slot = jnp.where(
            lane_iota(1) < room,
            pltpu.roll(got_ref[s * copies, 0:1, :], room, 1),
            pltpu.roll(got_ref[s * copies, 1:2, :], 2 * room, 1),
        ).astype(jnp.int32)
        hit = rows_at == lax.shift_right_logical(slot, LANE_BITS)
        for q, piece in enumerate(pieces):
            left[q].append(picked(hit, piece[s : s + 1]))
        right.append(
            jnp.where(lanes_at == (slot & (LANES - 1)), 1.0, 0.0).astype(jnp.bfloat16)
        )
    right = jnp.concatenate(right, axis=1)
    pilot_ref[...] = sum(mm(jnp.concatenate(q, axis=1), right, NT) for q in left)


def tied(*values):
    return lax.optimization_barrier(values)


def neighbour_pairs(axis):
    forward = [(i, i + 1) for i in range(lax.axis_size(axis) - 1)]
    return forward, [(b, a) for a, b in forward]


def swap_pairs(axis, first):
    pairs = [(i, i + 1) for i in range(first, lax.axis_size(axis) - 1, 2)]
    return pairs + [(b, a) for a, b in pairs]


def swapped(x):
    return lax.ppermute(x, "layers", [(0, 1), (1, 0)])


def on_device(
    state_field,
    conductivity,
    storage,
    gauge_owner,
    gauge_cell,
    gauge_value,
    gauge_weight,
    pilot_index,
):
    nz, nx, ny = state_field.shape
    peers = lax.axis_size("cols") * lax.axis_size("rows")
    devices = peers * lax.axis_size("layers")
    gauges = gauge_owner.shape[0]
    capacity = 4 * gauges // peers
    f32 = jnp.float32
    row_count = lax.axis_size("rows")

    def shape(*dims, dtype=f32):
        return jax.ShapeDtypeStruct(dims, dtype)

    def flat(x):
        return x.reshape(gauges // LANES, LANES)

    obs = pltpu.VMEM((gauges // LANES, LANES), f32)
    obs_int = pltpu.VMEM((gauges // LANES, LANES), jnp.int32)
    payload = kernel_call(
        functools.partial(route_body, peers, capacity),
        shape(peers, 3 * capacity // LANES, LANES),
        [obs_int, obs_int, obs, obs, pltpu.SemaphoreType.DMA((4,))],
        weight=5,
        vmem=64 * 1024 * 1024,
    )(in_specs=[HBM] * 4, out_specs=VMEM)(
        flat(gauge_owner), flat(gauge_cell), flat(gauge_value), flat(gauge_weight)
    )
    payload, pilot_index = tied(payload, pilot_index)
    got = lax.all_to_all(payload, PEER_AXES, 0, 0, tiled=True)
    spot, slots = kernel_call(
        pilot_body, (shape(nx // 4, LANES, dtype=jnp.int32), shape(peers, LANES))
    )(in_specs=[VMEM], out_specs=(VMEM, VMEM))(pilot_index)

    fixed = (conductivity, storage, state_field)
    got, spot, *fixed_other = tied(got, spot, *(swapped(x) for x in fixed))
    edge = shape(3, nz, HALO, LANES)
    source, near, far = kernel_call(
        functools.partial(source_body, capacity // LANES),
        (shape(nz, nx, LANES), edge, edge),
        weight=6,
    )(in_specs=[VMEM] * 4, out_specs=(VMEM,) * 3)(got, *fixed)
    near = lax.ppermute(near, "cols", swap_pairs("cols", 0))
    far = lax.ppermute(far, "cols", swap_pairs("cols", 1))
    other = swapped(source)

    def packed(low_side):
        return kernel_call(
            functools.partial(pack_body, low_side), shape(2 * nz, HALO, LANES)
        )(in_specs=[VMEM] * 6, out_specs=VMEM)(*fixed, source, near, far)

    if row_count == 2:
        send = [(packed(None), [(0, 1), (1, 0)])]
    else:
        forward, backward = neighbour_pairs("rows")
        send = [(packed(False), forward), (packed(True), backward)]
    edges = tied(near, far, swapped(near), swapped(far), *(x for x, _ in send))[:4]
    sides = [lax.ppermute(x, "rows", pairs) for x, pairs in send]
    planes, width, span = 2 * nz, nx + 2 * HALO, nx + HALO
    padded = (planes, width, LANES)
    prepared = kernel_call(
        prepare_body,
        (*(shape(*padded) for _ in range(6)), shape(6, nz, span, LANES), shape(span, LANES)),
        [pltpu.VMEM(padded, f32)] * 2,
        weight=3,
    )(in_specs=[VMEM] * 10, out_specs=(VMEM,) * 8)(*fixed, *fixed_other, *edges)
    *sides, prepared = tied(*sides, prepared)
    sides = sides + [swapped(x) for x in sides]

    each = nx * ny // 8 // LANES
    own, send = kernel_call(
        functools.partial(basis_body, peers, len(sides) // 2),
        (shape(ITERS, nz, nx, LANES), shape(devices, ITERS, LANES)),
        [
            pltpu.VMEM(padded, f32),
            pltpu.VMEM(padded, f32),
            pltpu.VMEM((nz, span, LANES), f32),
            pltpu.VMEM(padded, f32),
            pltpu.VMEM((ITERS + 1, planes, width + 2 * HALO, LANES), f32),
        ],
        weight=10,
    )(in_specs=[VMEM] * (16 + len(sides)), out_specs=(VMEM, VMEM))(
        *prepared, source, other, *edges, *sides, spot, slots
    )
    parts = lax.all_to_all(send, GRID_AXES, 0, 0, tiled=True)
    adjoint, pilot = kernel_call(
        functools.partial(solve_body, devices // peers), (shape(nz, nx, ny), shape(each, LANES))
    )(in_specs=[VMEM] * 2, out_specs=(VMEM, VMEM))(parts, own)
    return adjoint, pilot.reshape(-1)


def solution(mesh):
    return jax.shard_map(
        on_device,
        mesh=mesh,
        in_specs=(
            P(("groups", "layers"), "cols", "rows"),
            P(("groups", "layers"), "cols", "rows"),
            P(("groups", "layers"), "cols", "rows"),
            P(("groups", "cols", "rows", "layers")),
            P(("groups", "cols", "rows", "layers")),
            P(("groups", "cols", "rows", "layers")),
            P(("groups", "cols", "rows", "layers")),
            P("cols", "rows"),
        ),
        out_specs=(P(("groups", "layers"), "cols", "rows"), P(("groups", "cols", "rows"))),
        check_vma=False,
    )
```
